32 devices in a mesh: groups: 2 (over x), examples: 16 (over z, y, core).
Axes of the slice: x: 2, y: 2, z: 4, core: 2. Of those that a mesh axis runs over, the one named last changes fastest.
Arguments:
- layer_inputs: bfloat16 [4096, 4096], P(('groups', 'examples')), parts along dimension 0, may hold values from -6 to 6
- example_lengths: int32 [32], P(('groups', 'examples')), parts along dimension 0, may hold values from 32 to 128, as said below
- norm_gain: float32 [4096], replicated, may hold values from 0.25 to 1.75
- gate_weight: bfloat16 [4096, 14336], P(None, 'examples'), may hold values from -0.09375 to 0.09375
- up_weight: bfloat16 [4096, 14336], P(None, 'examples'), may hold values from -0.09375 to 0.09375
- in_factor: bfloat16 [14336, 64], P('examples'), may hold values from -0.046875 to 0.046875
- out_factor: bfloat16 [4096, 64], replicated, may hold values from -0.09375 to 0.09375
- out_grads: bfloat16 [4096, 4096], P(('groups', 'examples')), parts along dimension 0, may hold values from -6 to 6
- queries: bfloat16 [256, 4096], P('examples'), may hold values from -0.023925781 to 0.023925781
- query_ids: int32 [256], P('examples'), may hold values from 0 to 255
Outputs:
- influence: float32 [32, 256], P(('groups', 'examples')), parts along dimension 0
The draws below stay inside these ranges and needn't reach their ends.
There are 2 independent parts, one for each index of `groups`. The reference program is written for one: setup_inputs(seed, part) draws one part's arguments, and reference() takes and returns one part's arrays. A program takes and returns all parts, laid end to end along the dimension named above; an argument that names none is the same for every part. Nothing has to cross between parts.
Inputs may be any that keep to these rules, and one draw needn't show every extreme that they name: `example_lengths`: in every draw one example has exactly 128 live slots and another exactly 32.
All inputs are finite; a program needn't handle non-finite values.
Results may differ from the reference program's by a relative error of at most 0.0059.
Values may be sent and summed in bfloat16 or wider, within the bound.
No kernel may reach another device: no remote copies, remote signals or barrier semaphores. Data moves between devices by JAX's collectives and lax.ppermute only.
A program may use at most 128 MiB of HBM per device.

```python
import math
import jax
import jax.numpy as jnp
from jax import lax

D = 4096
FF = 14336
R = 64
NVAL = 256
SPAN = 128
TOKENS = 2048
E_ALL = 16
NQ = 256
RR = 4096


def draw_example_lengths(key, part):
    key = jax.random.fold_in(key, 7)
    keys = jax.random.split(key, 3)
    lengths = jax.random.randint(keys[0], (E_ALL,), SPAN // 4, SPAN + 1)
    first = jax.random.randint(keys[1], (), 0, E_ALL)
    second = (first + 1 + jax.random.randint(keys[2], (), 0, E_ALL - 1)) % E_ALL
    places = jnp.arange(E_ALL, dtype=jnp.int32)
    lengths = jnp.where(places == first, SPAN, lengths)
    lengths = jnp.where(places == second, SPAN // 4, lengths)
    return lengths.astype(jnp.int32)


def with_ends(array, stream_key, low, high):
    spot = [jax.random.randint(jax.random.fold_in(stream_key, axis), (), 0, length) for axis, length in enumerate(array.shape)]
    longest = array.shape.index(max(array.shape))
    next_to = spot[:longest] + [(spot[longest] + 1) % array.shape[longest]] + spot[longest + 1:]
    return array.at[tuple(spot)].set(low).at[tuple(next_to)].set(high)


def shard_levels(own_key, extent, cuts, smallest, top_value):
    gain, own = 1.0, jax.random.fold_in(own_key, 6)
    for position, blocks in cuts:
        draws = jnp.exp(jax.random.uniform(jax.random.fold_in(own, position), (blocks,), jnp.float32, smallest / len(cuts), top_value / len(cuts)))
        gain = gain * jnp.repeat(draws, extent[position] // blocks).reshape([-1 if axis == position else 1 for axis in range(len(extent))])
    return gain


def centred(own_key, dims, deviation, bound, shards=(), kind=jnp.bfloat16):
    entries = jax.random.normal(own_key, dims, jnp.float32) * deviation
    if len(shards) > 0:
        entries = shard_levels(own_key, dims, shards, -0.22, 0.18) * entries
    return jnp.clip(entries, min=-bound, max=bound).astype(kind)


def setup_inputs(seed: int = 0, part: int = 0) -> dict:
    arg_keys = jax.random.split(jax.random.key(seed), 11)
    part_splits = jax.random.split(jax.random.fold_in(arg_keys[10], part), 11)
    return {
        "layer_inputs": centred(part_splits[0], (TOKENS, D), 1.0, 6.0, ((0, 16),)),
        "example_lengths": draw_example_lengths(jax.random.fold_in(jax.random.fold_in(arg_keys[10], part), 71), part),
        "norm_gain": jnp.clip(1.0 + 0.15 * jax.random.normal(arg_keys[2], (D,), jnp.float32), 0.25, 1.75),
        "gate_weight": centred(arg_keys[3], (D, FF), D ** -0.5, 0.09375, ((1, 16),)),
        "up_weight": centred(arg_keys[4], (D, FF), D ** -0.5, 0.09375, ((1, 16),)),
        "in_factor": centred(arg_keys[5], (FF, R), FF ** -0.5, 0.046875, ((0, 16),)),
        "out_factor": centred(arg_keys[6], (D, R), D ** -0.5, 0.09375),
        "out_grads": centred(part_splits[7], (TOKENS, D), 1.0, 6.0, ((0, 16),)),
        "queries": centred(arg_keys[8], (NQ, RR), 0.004, 0.023925781, ((0, 16),)),
        "query_ids": with_ends(jax.random.randint(arg_keys[9], (NQ,), 0, NVAL), jax.random.fold_in(arg_keys[9], 1), 0, NVAL - 1).astype(jnp.int32),
    }


def normed(inputs, norm_gain):
    rows = inputs.astype(jnp.float32)
    scale = lax.rsqrt(lax.optimization_barrier(jnp.mean(rows * rows, axis=-1, keepdims=True)) + 1e-05)
    return (rows * scale * norm_gain).astype(jnp.bfloat16)

def projected(normed_rows, gate_weight, up_weight, in_factor):
    count = normed_rows.shape[0]
    block = math.gcd(count, 1024)

    def one_block(piece):
        gate = jnp.dot(piece, gate_weight, preferred_element_type=jnp.float32)
        up_part = jnp.dot(piece, up_weight, preferred_element_type=jnp.float32)
        hidden = (jax.nn.silu(gate) * up_part).astype(jnp.bfloat16)
        return jnp.dot(hidden, in_factor, preferred_element_type=jnp.float32)
    result = lax.map(one_block, normed_rows.reshape(count // block, block, normed_rows.shape[1]))
    return result.reshape(count, in_factor.shape[1])

def live_rows(right, lengths):
    count = lengths.shape[0]
    span = right.shape[0] // count
    places = jnp.arange(span, dtype=jnp.int32)
    live = (places[None, :] < lengths[:, None]).astype(jnp.float32).reshape(count * span, 1)
    return right * live

def sketches(left, masked, count):
    order = left.shape[1]
    span = left.shape[0] // count
    result = jnp.einsum('etk,etj->ekj', left.reshape(count, span, order), masked.reshape(count, span, order), precision=lax.Precision.HIGHEST)
    return result.reshape(count, order * order)

def reference(layer_inputs, example_lengths, norm_gain, gate_weight, up_weight, in_factor, out_factor, out_grads, queries, query_ids):
    normed_all = normed(layer_inputs, norm_gain)
    left = projected(normed_all, gate_weight, up_weight, in_factor)
    right = jnp.dot(out_grads, out_factor, preferred_element_type=jnp.float32)
    masked = live_rows(right, example_lengths)
    sketch = sketches(left, masked, E_ALL).astype(jnp.bfloat16)
    scores = jnp.dot(sketch, queries.T, preferred_element_type=jnp.float32)
    members = (query_ids[:, None] == jnp.arange(NVAL, dtype=jnp.int32)[None, :]).astype(jnp.float32)
    return jnp.dot(scores, members, precision=lax.Precision.HIGHEST)
```

```python
import functools

import jax
import jax.numpy as jnp
from jax import lax
from jax.experimental import pallas as pl
from jax.experimental.pallas import tpu as pltpu
from jax.sharding import PartitionSpec as P

NVAL = 256
LANES = 128
MIB = 1024 * 1024


def chip_ring(chips):
    if chips == 8:
        return [0, 2, 4, 6, 7, 5, 3, 1]
    return list(range(chips))


def pack_body(gate_ref, up_ref, out_ref):
    out_ref[0, :, :LANES] = gate_ref[...]
    out_ref[0, :, LANES:] = up_ref[...]


def pack_weights(gate_weight, up_weight):
    depth, units = gate_weight.shape
    tiles = units // LANES
    return pl.pallas_call(
        pack_body,
        grid=(tiles,),
        in_specs=[pl.BlockSpec((depth, LANES), lambda i: (0, i))] * 2,
        out_specs=pl.BlockSpec((1, depth, 2 * LANES), lambda i: (i, 0, 0)),
        out_shape=jax.ShapeDtypeStruct((tiles, depth, 2 * LANES), gate_weight.dtype),
        compiler_params=pltpu.CompilerParams(vmem_limit_bytes=24 * MIB),
        cost_estimate=pl.CostEstimate(flops=0, bytes_accessed=8 * depth * units, transcendentals=0),
        name="pack_weights",
    )(gate_weight, up_weight)


def chunk_body(pieces, *refs):
    x_refs = refs[:pieces]
    gain_ref, w_ref, f_ref, _, out_ref, xn = refs[pieces:]
    rows = x_refs[0].shape[0]
    step = pl.program_id(0)

    @pl.when(step == 0)
    def _():
        for k, ref in enumerate(x_refs):
            x = ref[...].astype(jnp.float32)
            scale = lax.rsqrt(jnp.mean(x * x, axis=-1, keepdims=True) + 1e-05)
            xn[k * rows : (k + 1) * rows, :] = (x * scale * gain_ref[...]).astype(jnp.bfloat16)

    both = jnp.dot(xn[...], w_ref[0], preferred_element_type=jnp.float32)
    gate, up = both[:, :LANES], both[:, LANES:]
    hidden = (jax.nn.silu(gate) * up).astype(jnp.bfloat16)
    part = jnp.dot(hidden, f_ref[...], preferred_element_type=jnp.float32)

    @pl.when(step == 0)
    def _():
        out_ref[...] = part

    @pl.when(step > 0)
    def _():
        out_ref[...] += part


def chunk(xs, gain, packed, in_factor, left, index):
    pieces = len(xs)
    rows, depth = xs[0].shape
    tiles = packed.shape[0]
    order = in_factor.shape[1]
    total = pieces * rows
    return pl.pallas_call(
        functools.partial(chunk_body, pieces),
        grid=(tiles,),
        in_specs=[pl.BlockSpec((rows, depth), lambda i: (0, 0))] * pieces
        + [
            pl.BlockSpec((1, depth), lambda i: (0, 0)),
            pl.BlockSpec((1, depth, 2 * LANES), lambda i: (i, 0, 0)),
            pl.BlockSpec((LANES, order), lambda i: (i, 0)),
            pl.BlockSpec(memory_space=pl.ANY),
        ],
        out_specs=pl.BlockSpec((total, order), lambda i: (index, 0)),
        out_shape=jax.ShapeDtypeStruct(left.shape, left.dtype),
        scratch_shapes=[pltpu.VMEM((total, depth), jnp.bfloat16)],
        input_output_aliases={pieces + 3: 0},
        compiler_params=pltpu.CompilerParams(vmem_limit_bytes=32 * MIB),
        cost_estimate=pl.CostEstimate(
            flops=2 * total * depth * tiles * 2 * LANES,
            bytes_accessed=2 * tiles * depth * 2 * LANES,
            transcendentals=0,
        ),
        name="chunk",
    )(*xs, gain, packed, in_factor, left)


def sketch_body(at_f, at_b, left_ref, masked_ref, out_ref):
    half = left_ref.shape[0] // (2 * at_f.shape[0])
    e = pl.program_id(0)
    first = left_ref[pl.ds(pl.multiple_of(at_f[e] * half, half), half), :]
    second = left_ref[pl.ds(pl.multiple_of(at_b[e] * half, half), half), :]
    left = jnp.concatenate([first, second], axis=0)
    sketch = lax.dot_general(
        left,
        masked_ref[...].astype(jnp.float32),
        (((0,), (0,)), ((), ())),
        precision=lax.Precision.HIGHEST,
        preferred_element_type=jnp.float32,
    )
    out_ref[0] = sketch


def sketch_all(left, masked, at_f, at_b):
    count = at_f.shape[0]
    tokens, order = left.shape
    span = tokens // count
    return pl.pallas_call(
        sketch_body,
        grid_spec=pltpu.PrefetchScalarGridSpec(
            num_scalar_prefetch=2,
            grid=(count,),
            in_specs=[
                pl.BlockSpec((tokens, order), lambda i, *_: (0, 0)),
                pl.BlockSpec((span, order), lambda i, *_: (i, 0)),
            ],
            out_specs=pl.BlockSpec((1, order, order), lambda i, *_: (i, 0, 0)),
        ),
        out_shape=jax.ShapeDtypeStruct((count, order, order), jnp.float32),
        compiler_params=pltpu.CompilerParams(vmem_limit_bytes=24 * MIB),
        name="sketch",
    )(at_f, at_b, left, masked)


def local(
    devices,
    layer_inputs,
    example_lengths,
    norm_gain,
    gate_weight,
    up_weight,
    in_factor,
    out_factor,
    out_grads,
    queries,
    query_ids,
):
    chips = devices // 2
    ring = chip_ring(chips)
    me = lax.axis_index("examples")
    core = me % 2
    place_of = [ring.index(c) for c in range(chips)]
    place = jnp.array(place_of, jnp.int32)[me // 2]

    forward = [(ring[r] * 2 + c, ring[(r + 1) % chips] * 2 + c) for r in range(chips) for c in range(2)]
    backward = [(b, a) for a, b in forward]
    other_core = [(d, d ^ 1) for d in range(devices)]

    span, depth = layer_inputs.shape
    half = span // 2
    order = in_factor.shape[1]

    right = jnp.dot(out_grads, out_factor, preferred_element_type=jnp.float32)
    live = jnp.arange(span, dtype=jnp.int32)[:, None] < example_lengths[0]
    masked = jnp.where(live, right, 0.0).astype(jnp.bfloat16)
    nq = queries.shape[0]
    mrows = span * order // depth
    ids_row = jnp.pad(query_ids.astype(jnp.bfloat16)[None, :], ((0, 0), (0, depth - nq)))
    side = jnp.concatenate([queries, masked.reshape(mrows, depth), ids_row], axis=0)
    side = jnp.pad(side, ((0, -side.shape[0] % 8), (0, 0)))
    side_all = lax.all_gather(side, "examples", axis=0)
    queries_all = side_all[:, :nq].reshape(devices * nq, depth)
    masked_all = side_all[:, nq : nq + mrows].reshape(devices * span, order)
    ids_all = side_all[:, nq + mrows, :nq].reshape(devices * nq)
    members = (ids_all[:, None] == jnp.arange(NVAL, dtype=jnp.float32)[None, :]).astype(jnp.float32)

    units = gate_weight.shape[1]
    short = -units % LANES
    if short:
        gate_weight = jnp.pad(gate_weight, ((0, 0), (0, short)))
        up_weight = jnp.pad(up_weight, ((0, 0), (0, short)))
        in_factor = jnp.pad(in_factor, ((0, short), (0, 0)))
    packed = pack_weights(gate_weight, up_weight)
    gain = norm_gain[None, :]

    going_f, going_b = layer_inputs[:half], layer_inputs[half:]
    left = jnp.zeros((devices * span, order), jnp.float32)
    for step in range(chips):
        own = (going_f, going_b)
        if step < chips - 1:
            going_f = lax.ppermute(own[0], "examples", forward)
            going_b = lax.ppermute(own[1], "examples", backward)
        swapped = tuple(lax.ppermute(x, "examples", other_core) for x in own)
        left = chunk(own + swapped, gain, packed, in_factor, left, step)

    example = jnp.arange(devices, dtype=jnp.int32)
    origin = jnp.array(place_of, jnp.int32)[example // 2]
    foreign = (example % 2 != core).astype(jnp.int32)
    at_f = ((place - origin) % chips) * 4 + foreign * 2
    at_b = ((origin - place) % chips) * 4 + foreign * 2 + 1

    sketch = sketch_all(left, masked_all, at_f, at_b)
    sketch = sketch.astype(jnp.bfloat16).reshape(devices, order * order)
    scores = jnp.dot(sketch, queries_all.T, preferred_element_type=jnp.float32)
    partial = jnp.dot(scores, members, precision=lax.Precision.HIGHEST)
    shares = lax.all_to_all(partial, "examples", split_axis=0, concat_axis=0, tiled=True)
    return jnp.sum(shares, axis=0, keepdims=True)


def solution(mesh):
    return jax.shard_map(
        functools.partial(local, mesh.shape["examples"]),
        mesh=mesh,
        in_specs=(
            P(("groups", "examples"), None),
            P(("groups", "examples")),
            P(),
            P(None, "examples"),
            P(None, "examples"),
            P("examples", None),
            P(),
            P(("groups", "examples"), None),
            P("examples", None),
            P("examples"),
        ),
        out_specs=P(("groups", "examples"), None),
        check_vma=False,
    )
```

```python
import functools

import jax
import jax.numpy as jnp
from jax import lax
from jax.experimental import pallas as pl
from jax.experimental.pallas import tpu as pltpu
from jax.sharding import PartitionSpec as P

NVAL = 256
LANES = 128
MIB = 1024 * 1024


def chip_ring(chips):
    if chips == 8:
        return [0, 2, 4, 6, 7, 5, 3, 1]
    return list(range(chips))


def norm_rows(x_refs, gain_ref, xn):
    rows = x_refs[0].shape[0]
    for k, ref in enumerate(x_refs):
        x = ref[...].astype(jnp.float32)
        scale = lax.rsqrt(jnp.mean(x * x, axis=-1, keepdims=True) + 1e-05)
        xn[k * rows : (k + 1) * rows, :] = (x * scale * gain_ref[...]).astype(jnp.bfloat16)


def project_tile(xn, w_ref, f_ref, out_ref):
    step = pl.program_id(0)
    both = jnp.dot(xn[...], w_ref[0], preferred_element_type=jnp.float32)
    gate, up = both[:, :LANES], both[:, LANES:]
    hidden = (jax.nn.silu(gate) * up).astype(jnp.bfloat16)
    part = jnp.dot(hidden, f_ref[...], preferred_element_type=jnp.float32)

    @pl.when(step == 0)
    def _():
        out_ref[...] = part

    @pl.when(step > 0)
    def _():
        out_ref[...] += part


def first_body(pieces, *refs):
    x_refs = refs[:pieces]
    gain_ref, gate_ref, up_ref, f_ref, out_ref, w_ref, xn = refs[pieces:]

    @pl.when(pl.program_id(0) == 0)
    def _():
        norm_rows(x_refs, gain_ref, xn)

    w_ref[0, :, :LANES] = gate_ref[...]
    w_ref[0, :, LANES:] = up_ref[...]
    project_tile(xn, w_ref, f_ref, out_ref)


def first_chunk(xs, gain, gate_weight, up_weight, in_factor, tokens):
    pieces = len(xs)
    rows, depth = xs[0].shape
    units, order = in_factor.shape
    tiles = units // LANES
    total = pieces * rows
    return pl.pallas_call(
        functools.partial(first_body, pieces),
        grid=(tiles,),
        in_specs=[pl.BlockSpec((rows, depth), lambda i: (0, 0))] * pieces
        + [
            pl.BlockSpec((1, depth), lambda i: (0, 0)),
            pl.BlockSpec((depth, LANES), lambda i: (0, i)),
            pl.BlockSpec((depth, LANES), lambda i: (0, i)),
            pl.BlockSpec((LANES, order), lambda i: (i, 0)),
        ],
        out_specs=[
            pl.BlockSpec((total, order), lambda i: (0, 0)),
            pl.BlockSpec((1, depth, 2 * LANES), lambda i: (i, 0, 0)),
        ],
        out_shape=[
            jax.ShapeDtypeStruct((tokens, order), jnp.float32),
            jax.ShapeDtypeStruct((tiles, depth, 2 * LANES), gate_weight.dtype),
        ],
        scratch_shapes=[pltpu.VMEM((total, depth), jnp.bfloat16)],
        compiler_params=pltpu.CompilerParams(vmem_limit_bytes=16 * MIB),
        cost_estimate=pl.CostEstimate(
            flops=2 * total * depth * tiles * 2 * LANES,
            bytes_accessed=8 * depth * units,
            transcendentals=0,
        ),
        name="first_chunk",
    )(*xs, gain, gate_weight, up_weight, in_factor)


def chunk_body(pieces, *refs):
    x_refs = refs[:pieces]
    gain_ref, w_ref, f_ref, _, out_ref, xn = refs[pieces:]

    @pl.when(pl.program_id(0) == 0)
    def _():
        norm_rows(x_refs, gain_ref, xn)

    project_tile(xn, w_ref, f_ref, out_ref)


def chunk(xs, gain, packed, in_factor, left, index):
    pieces = len(xs)
    rows, depth = xs[0].shape
    tiles = packed.shape[0]
    order = in_factor.shape[1]
    total = pieces * rows
    return pl.pallas_call(
        functools.partial(chunk_body, pieces),
        grid=(tiles,),
        in_specs=[pl.BlockSpec((rows, depth), lambda i: (0, 0))] * pieces
        + [
            pl.BlockSpec((1, depth), lambda i: (0, 0)),
            pl.BlockSpec((1, depth, 2 * LANES), lambda i: (i, 0, 0)),
            pl.BlockSpec((LANES, order), lambda i: (i, 0)),
            pl.BlockSpec(memory_space=pl.ANY),
        ],
        out_specs=pl.BlockSpec((total, order), lambda i: (index, 0)),
        out_shape=jax.ShapeDtypeStruct(left.shape, left.dtype),
        scratch_shapes=[pltpu.VMEM((total, depth), jnp.bfloat16)],
        input_output_aliases={pieces + 3: 0},
        compiler_params=pltpu.CompilerParams(vmem_limit_bytes=16 * MIB),
        cost_estimate=pl.CostEstimate(
            flops=2 * total * depth * tiles * 2 * LANES,
            bytes_accessed=2 * tiles * depth * 2 * LANES,
            transcendentals=0,
        ),
        name="chunk",
    )(*xs, gain, packed, in_factor, left)


def sketch_body(at_f, at_b, left_ref, masked_ref, out_ref):
    half = left_ref.shape[0] // (2 * at_f.shape[0])
    e = pl.program_id(0)
    first = left_ref[pl.ds(pl.multiple_of(at_f[e] * half, half), half), :]
    second = left_ref[pl.ds(pl.multiple_of(at_b[e] * half, half), half), :]
    left = jnp.concatenate([first, second], axis=0)
    high = left.astype(jnp.bfloat16)
    low = (left - high.astype(jnp.float32)).astype(jnp.bfloat16)
    masked = masked_ref[...]
    sketch = sum(
        lax.dot_general(part, masked, (((0,), (0,)), ((), ())), preferred_element_type=jnp.float32)
        for part in (low, high)
    )
    out_ref[0] = sketch


def sketch_all(left, masked, at_f, at_b):
    count = at_f.shape[0]
    tokens, order = left.shape
    span = tokens // count
    return pl.pallas_call(
        sketch_body,
        grid_spec=pltpu.PrefetchScalarGridSpec(
            num_scalar_prefetch=2,
            grid=(count,),
            in_specs=[
                pl.BlockSpec((tokens, order), lambda i, *_: (0, 0)),
                pl.BlockSpec((span, order), lambda i, *_: (i, 0)),
            ],
            out_specs=pl.BlockSpec((1, order, order), lambda i, *_: (i, 0, 0)),
        ),
        out_shape=jax.ShapeDtypeStruct((count, order, order), jnp.float32),
        compiler_params=pltpu.CompilerParams(vmem_limit_bytes=24 * MIB),
        name="sketch",
    )(at_f, at_b, left, masked)


def local(
    devices,
    layer_inputs,
    example_lengths,
    norm_gain,
    gate_weight,
    up_weight,
    in_factor,
    out_factor,
    out_grads,
    queries,
    query_ids,
):
    chips = devices // 2
    ring = chip_ring(chips)
    me = lax.axis_index("examples")
    core = me % 2
    place_of = [ring.index(c) for c in range(chips)]
    place = jnp.array(place_of, jnp.int32)[me // 2]

    forward = [(ring[r] * 2 + c, ring[(r + 1) % chips] * 2 + c) for r in range(chips) for c in range(2)]
    backward = [(b, a) for a, b in forward]
    other_core = [(d, d ^ 1) for d in range(devices)]

    span, depth = layer_inputs.shape
    half = span // 2
    order = in_factor.shape[1]

    right = jnp.dot(out_grads, out_factor, preferred_element_type=jnp.float32)
    live = jnp.arange(span, dtype=jnp.int32)[:, None] < example_lengths[0]
    masked = jnp.where(live, right, 0.0).astype(jnp.bfloat16)
    nq = queries.shape[0]
    mrows = span * order // depth
    ids_row = jnp.pad(query_ids.astype(jnp.bfloat16)[None, :], ((0, 0), (0, depth - nq)))
    side = jnp.concatenate([queries, masked.reshape(mrows, depth), ids_row], axis=0)
    side = jnp.pad(side, ((0, -side.shape[0] % 8), (0, 0)))
    side_all = lax.all_gather(side, "examples", axis=0)
    queries_all = side_all[:, :nq].reshape(devices * nq, depth)
    masked_all = side_all[:, nq : nq + mrows].reshape(devices * span, order)
    ids_all = side_all[:, nq + mrows, :nq].reshape(devices * nq)
    members = (ids_all[:, None] == jnp.arange(NVAL, dtype=jnp.float32)[None, :]).astype(jnp.float32)

    units = gate_weight.shape[1]
    short = -units % LANES
    if short:
        gate_weight = jnp.pad(gate_weight, ((0, 0), (0, short)))
        up_weight = jnp.pad(up_weight, ((0, 0), (0, short)))
        in_factor = jnp.pad(in_factor, ((0, short), (0, 0)))
    gain = norm_gain[None, :]

    def both_ways(pair):
        return lax.ppermute(pair[0], "examples", forward), lax.ppermute(pair[1], "examples", backward)

    def swap(pair):
        return tuple(lax.ppermute(x, "examples", other_core) for x in pair)

    own = (layer_inputs[:half], layer_inputs[half:])
    coming = both_ways(own)
    swapped = swap(own)
    left, packed = first_chunk(own, gain, gate_weight, up_weight, in_factor, devices * span)
    for step in range(1, chips):
        own_f, own_b, left = lax.optimization_barrier((*coming, left))
        own = (own_f, own_b)
        if step < chips - 1:
            coming = both_ways(own)
        before, swapped = swapped, swap(own)
        left = chunk(own + before, gain, packed, in_factor, left, step)
    left = chunk(swapped, gain, packed, in_factor, left, 1)

    example = jnp.arange(devices, dtype=jnp.int32)
    origin = jnp.array(place_of, jnp.int32)[example // 2]
    foreign = (example % 2 != core).astype(jnp.int32)
    hops_f = (place - origin) % chips
    hops_b = (origin - place) % chips
    here = example % 2 == core
    at_f = jnp.where(here, 4 * hops_f, 4 * ((hops_f + 1) % chips) + 2)
    at_b = jnp.where(here, 4 * hops_b, 4 * ((hops_b + 1) % chips) + 2) + 1

    sketch = sketch_all(left, masked_all, at_f, at_b)
    sketch = sketch.astype(jnp.bfloat16).reshape(devices, order * order)
    scores = jnp.dot(sketch, queries_all.T, preferred_element_type=jnp.float32)
    partial = jnp.dot(scores, members, precision=lax.Precision.HIGHEST)
    shares = lax.all_to_all(partial, "examples", split_axis=0, concat_axis=0, tiled=True)
    return jnp.sum(shares, axis=0, keepdims=True)


def solution(mesh):
    return jax.shard_map(
        functools.partial(local, mesh.shape["examples"]),
        mesh=mesh,
        in_specs=(
            P(("groups", "examples"), None),
            P(("groups", "examples")),
            P(),
            P(None, "examples"),
            P(None, "examples"),
            P("examples", None),
            P(),
            P(("groups", "examples"), None),
            P("examples", None),
            P("examples"),
        ),
        out_specs=P(("groups", "examples"), None),
        check_vma=False,
    )
```

```python
import functools

import jax
import jax.numpy as jnp
from jax import lax
from jax.experimental import pallas as pl
from jax.experimental.pallas import tpu as pltpu
from jax.sharding import PartitionSpec as P

NVAL = 256
LANES = 128
MIB = 1024 * 1024
NT = (((1,), (1,)), ((), ()))
TN = (((0,), (0,)), ((), ()))


def chip_ring(chips):
    if chips == 8:
        return [0, 2, 4, 6, 7, 5, 3, 1]
    return list(range(chips))


def chunk_body(pieces, *refs):
    x_refs = refs[:pieces]
    gain_ref, gate_ref, up_ref, f_ref, out_ref, xn = refs[pieces], *refs[pieces + 1 : pieces + 4], *refs[-2:]
    rows = x_refs[0].shape[0]
    step = pl.program_id(0)

    @pl.when(step == 0)
    def _():
        for k, ref in enumerate(x_refs):
            x = ref[...].astype(jnp.float32)
            scale = lax.rsqrt(jnp.mean(x * x, axis=-1, keepdims=True) + 1e-05)
            xn[k * rows : (k + 1) * rows, :] = (x * scale * gain_ref[...]).astype(jnp.bfloat16)

    weights = jnp.concatenate([gate_ref[...], up_ref[...]], axis=1)
    both = jnp.dot(xn[...], weights, preferred_element_type=jnp.float32)
    gate, up = both[:, :LANES], both[:, LANES:]
    hidden = (jax.nn.silu(gate) * up).astype(jnp.bfloat16)
    part = jnp.dot(hidden, f_ref[...], preferred_element_type=jnp.float32)

    @pl.when(step == 0)
    def _():
        out_ref[...] = part

    @pl.when(step > 0)
    def _():
        out_ref[...] += part


def chunk(xs, gain, gate_weight, up_weight, in_factor, left, index, tokens):
    pieces = len(xs)
    rows, depth = xs[0].shape
    units, order = in_factor.shape
    tiles = units // LANES
    total = pieces * rows
    operands = [*xs, gain, gate_weight, up_weight, in_factor]
    in_specs = [pl.BlockSpec((rows, depth), lambda i: (0, 0))] * pieces + [
        pl.BlockSpec((1, depth), lambda i: (0, 0)),
        pl.BlockSpec((depth, LANES), lambda i: (0, i)),
        pl.BlockSpec((depth, LANES), lambda i: (0, i)),
        pl.BlockSpec((LANES, order), lambda i: (i, 0)),
    ]
    aliases = {}
    if left is not None:
        aliases = {len(operands): 0}
        operands.append(left)
        in_specs.append(pl.BlockSpec(memory_space=pl.ANY))
    return pl.pallas_call(
        functools.partial(chunk_body, pieces),
        grid=(tiles,),
        in_specs=in_specs,
        out_specs=pl.BlockSpec((total, order), lambda i: (index, 0)),
        out_shape=jax.ShapeDtypeStruct((tokens, order), jnp.float32),
        scratch_shapes=[pltpu.VMEM((total, depth), jnp.bfloat16)],
        input_output_aliases=aliases,
        compiler_params=pltpu.CompilerParams(vmem_limit_bytes=18 * MIB),
        cost_estimate=pl.CostEstimate(
            flops=2 * total * depth * tiles * 2 * LANES,
            bytes_accessed=4 * depth * units,
            transcendentals=0,
        ),
        name="chunk",
    )(*operands)


def one_sketch(left_ref, masked, at, half):
    left = jnp.concatenate([left_ref[p * half : (p + 1) * half, :] for p in at], axis=0)
    high = left.astype(jnp.bfloat16)
    low = (left - high.astype(jnp.float32)).astype(jnp.bfloat16)
    return sum(lax.dot_general(part, masked, TN, preferred_element_type=jnp.float32) for part in (low, high))


def sketch_body(places, half, names, left_ref, side_ref, out_ref):
    for r, at in enumerate(places):
        masked = side_ref[names[r], : 2 * half, :]
        out_ref[r] = one_sketch(left_ref, masked, at, half).astype(out_ref.dtype)


def sketches(places, half, names, left, side):
    order = left.shape[1]
    vmem = pl.BlockSpec(memory_space=pltpu.VMEM)
    made = pl.pallas_call(
        functools.partial(sketch_body, places, half),
        in_specs=[pl.BlockSpec(memory_space=pltpu.SMEM), vmem, vmem],
        out_specs=vmem,
        out_shape=jax.ShapeDtypeStruct((len(places), order, order), jnp.bfloat16),
        compiler_params=pltpu.CompilerParams(vmem_limit_bytes=8 * MIB),
        cost_estimate=pl.CostEstimate(flops=400_000_000 * len(places), bytes_accessed=0, transcendentals=0),
        name="sketches",
    )(names, left, side)
    return made.reshape(len(places), order * order)


def finish_body(places, half, names, left_ref, side_ref, early_ref, queries_ref, ids_ref, out_ref, twice, flat):
    order = left_ref.shape[1]
    early = early_ref.shape[0]
    lane = lax.broadcasted_iota(jnp.int32, (order // 2, 2 * order), 1)
    for r, at in enumerate(places):
        masked = side_ref[names[early + r], : 2 * half, :]
        sketch = one_sketch(left_ref, masked, at, half)
        twice[...] = jnp.concatenate([sketch, sketch], axis=1)
        even = twice[pl.ds(0, order // 2, 2), :]
        odd = twice[pl.ds(1, order // 2, 2), :]
        flat[:, r, :] = jnp.where(lane < order, even, odd)
    late = jnp.concatenate([flat[c] for c in range(order // 2)], axis=1).astype(jnp.bfloat16)
    queries = queries_ref[...]
    count = queries.shape[0]
    value = lax.broadcasted_iota(jnp.int32, (NVAL, count), 0)
    members = (value == ids_ref[...]).astype(jnp.bfloat16)

    def influence(sketch):
        rest = lax.dot_general(sketch, queries, NT, preferred_element_type=jnp.float32)
        total = 0.0
        for _ in range(3):
            part = rest.astype(jnp.bfloat16)
            rest = rest - part.astype(jnp.float32)
            total += lax.dot_general(part, members, NT, preferred_element_type=jnp.float32)
        return total

    rows = influence(jnp.concatenate([late, early_ref[...]], axis=0))
    for r in range(early):
        out_ref[pl.ds(names[r], 1), :] = rows[flat.shape[1] + r : flat.shape[1] + r + 1, :]
    for r in range(len(places)):
        out_ref[pl.ds(names[early + r], 1), :] = rows[r : r + 1, :]


def finish(places, half, names, left, side, early, queries, ids):
    order = left.shape[1]
    vmem = pl.BlockSpec(memory_space=pltpu.VMEM)
    slots = -(-len(places) // 8) * 8
    return pl.pallas_call(
        functools.partial(finish_body, places, half),
        in_specs=[pl.BlockSpec(memory_space=pltpu.SMEM)] + [vmem] * 5,
        out_specs=vmem,
        out_shape=jax.ShapeDtypeStruct((names.shape[0], NVAL), jnp.float32),
        scratch_shapes=[
            pltpu.VMEM((order, 2 * order), jnp.float32),
            pltpu.VMEM((order // 2, slots, 2 * order), jnp.float32),
        ],
        compiler_params=pltpu.CompilerParams(vmem_limit_bytes=16 * MIB),
        name="finish",
    )(names, left, side, early, queries, ids)


def local(
    devices,
    groups,
    layer_inputs,
    example_lengths,
    norm_gain,
    gate_weight,
    up_weight,
    in_factor,
    out_factor,
    out_grads,
    queries,
    query_ids,
):
    chips = devices // 2
    far = chips // 2
    ring = chip_ring(chips)
    me = lax.axis_index("examples")
    core = me % 2
    place = jnp.array([ring.index(c) for c in range(chips)], jnp.int32)[me // 2]

    forward = [(ring[r] * 2 + c, ring[(r + 1) % chips] * 2 + c) for r in range(chips) for c in range(2)]
    backward = [(b, a) for a, b in forward]
    other_core = [(d, d ^ 1) for d in range(devices)]

    span, depth = layer_inputs.shape
    half = span // 2
    order = in_factor.shape[1]
    units = gate_weight.shape[1]
    short = -units % LANES
    if short:
        gate_weight = jnp.pad(gate_weight, ((0, 0), (0, short)))
        up_weight = jnp.pad(up_weight, ((0, 0), (0, short)))
        in_factor = jnp.pad(in_factor, ((0, short), (0, 0)))
    gain = norm_gain[None, :]
    tokens = 2 * span * chips + span

    def send(x, way):
        return lax.ppermute(x, "examples", way)

    def project(xs, left, index):
        return chunk(xs, gain, gate_weight, up_weight, in_factor, left, index, tokens)

    x_a, x_b = layer_inputs[:half], layer_inputs[half:]
    coming = {
        1: (send(x_a, forward), send(x_a, backward)),
        2: (send(x_b, forward), send(x_b, backward)),
    }
    swapped = tuple(send(x, other_core) for x in (x_a, x_b))
    left = project((x_a, x_b), None, 1)

    out_grads, queries, query_ids, left = lax.optimization_barrier((out_grads, queries, query_ids, left))
    right = jnp.dot(out_grads, out_factor, preferred_element_type=jnp.float32)
    live = jnp.arange(span, dtype=jnp.int32)[:, None] < example_lengths[0]
    masked = jnp.where(live, right, 0.0).astype(jnp.bfloat16)
    nq = queries.shape[0]
    ids_row = jnp.pad(query_ids.astype(jnp.bfloat16)[None, :], ((0, 15), (0, order - nq)))
    side = lax.all_gather(jnp.concatenate([masked, ids_row], axis=0), "examples", axis=0)
    share = nq // groups
    mine = lax.dynamic_slice_in_dim(queries, lax.axis_index("groups") * share, share, axis=0)
    mine = lax.all_gather(mine, "examples", axis=0, tiled=True)

    def pair(where):
        first = jnp.array(ring, jnp.int32)[where % chips] * 2
        return [first + core, first + 1 - core]

    names, spots = [], []
    for distance in range(far + 1):
        sides = [(1, 0)] if distance in (0, far) else [(-1, 0), (1, 1)]
        for sign, piece in sides:
            names += pair(place + sign * distance)
            if distance == 0:
                halves = [(0, 0), (0, 1)]
            elif distance == far:
                halves = [(chips - 1, 0), (chips - 1, 1)]
            else:
                halves = [(2 * distance - 1, piece), (2 * distance, piece)]
            spots.append([4 * k + 2 + p for k, p in halves])
            spots.append([4 * k + 4 + p for k, p in halves])
    names = jnp.stack(names)

    for k in range(1, chips):
        own_1, own_2, left = lax.optimization_barrier((*coming.pop(k), left))
        own = (own_1, own_2)
        if k + 2 < chips - 1:
            coming[k + 2] = (send(own_1, forward), send(own_2, backward))
        elif k + 2 == chips - 1:
            opposite = send(own_1, forward)
        elif k + 1 == chips - 1:
            coming[chips - 1] = (opposite, send(own_2, backward))
        before, swapped = swapped, tuple(send(x, other_core) for x in own)
        if k < chips - 1:
            left = project(before + own, left, k)
        if k == chips - 3:
            side, mine, left = lax.optimization_barrier((side, mine, left))
            all_queries = lax.all_gather(mine, "groups", axis=0, tiled=True)
            ids = side[:, span, :nq].reshape(devices, groups, share).swapaxes(0, 1).reshape(1, devices * nq)
            ids = ids.astype(jnp.int32)
            ready = devices - 6
            early = [sketches(spots[:ready], half, names[:ready], left, side)]
        if k == chips - 2:
            left = project(swapped, left, 2 * k + 2)
            early.append(sketches(spots[ready:-2], half, names[ready:-2], left, side))
            early = jnp.concatenate(early, axis=0)
            early, left = lax.optimization_barrier((early, left))
    left = project(own, left, 2 * chips - 1)
    left = project(swapped, left, 2 * chips)

    partial = finish(spots[-2:], half, names, left, side, early, all_queries, ids)
    shares = lax.all_to_all(partial, "examples", split_axis=0, concat_axis=0, tiled=True)
    return jnp.sum(shares, axis=0, keepdims=True)


def solution(mesh):
    return jax.shard_map(
        functools.partial(local, mesh.shape["examples"], mesh.shape["groups"]),
        mesh=mesh,
        in_specs=(
            P(("groups", "examples"), None),
            P(("groups", "examples")),
            P(),
            P(None, "examples"),
            P(None, "examples"),
            P("examples", None),
            P(),
            P(("groups", "examples"), None),
            P("examples", None),
            P("examples"),
        ),
        out_specs=P(("groups", "examples"), None),
        check_vma=False,
    )
```

```python
import functools

import jax
import jax.numpy as jnp
from jax import lax
from jax.experimental import pallas as pl
from jax.experimental.pallas import tpu as pltpu
from jax.sharding import PartitionSpec as P

NVAL = 256
LANES = 128
MIB = 1024 * 1024
NT = (((1,), (1,)), ((), ()))
TN = (((0,), (0,)), ((), ()))


def chip_ring(chips):
    if chips == 8:
        return [0, 2, 4, 6, 7, 5, 3, 1]
    return list(range(chips))


def prepare_body(width, x_ref, gain_ref, queries_ref, a_ref, b_ref, mine_ref):
    half = a_ref.shape[0]
    block = 16
    for start in range(0, 2 * half, block):
        x = x_ref[start : start + block, :].astype(jnp.float32)
        scale = lax.rsqrt(jnp.mean(x * x, axis=-1, keepdims=True) + 1e-05)
        rows = (x * scale * gain_ref[...]).astype(jnp.bfloat16)
        if start < half:
            a_ref[start : start + block, :] = rows
        else:
            b_ref[start - half : start - half + block, :] = rows
    offset = pl.multiple_of(lax.axis_index("groups") * width, width)
    mine_ref[...] = queries_ref[:, pl.ds(offset, width)]


def prepare(x, gain, queries, groups):
    span, depth = x.shape
    width = depth // groups
    vmem = pl.BlockSpec(memory_space=pltpu.VMEM)
    rows = jax.ShapeDtypeStruct((span // 2, depth), jnp.bfloat16)
    return pl.pallas_call(
        functools.partial(prepare_body, width),
        in_specs=[vmem] * 3,
        out_specs=[vmem] * 3,
        out_shape=[rows, rows, jax.ShapeDtypeStruct((queries.shape[0], width), queries.dtype)],
        compiler_params=pltpu.CompilerParams(vmem_limit_bytes=16 * MIB),
        name="prepare",
    )(x, gain, queries)


def chunk_body(pieces, tiles, packing, *refs):
    x_refs, refs = refs[:pieces], refs[pieces:]
    if packing:
        gate_ref, up_ref, f_ref, out_ref, w_ref, xn, even, odd = refs
    else:
        w_ref, f_ref, _, out_ref, xn, even, odd = refs
    rows = x_refs[0].shape[0]
    step = pl.program_id(0)

    def first_product(into):
        if packing:
            w_ref[0, :, :LANES] = gate_ref[...]
            w_ref[0, :, LANES:] = up_ref[...]
        into[...] = jnp.dot(xn[...], w_ref[0], preferred_element_type=jnp.float32)

    def second_product(source):
        gate, up = source[:, :LANES], source[:, LANES:]
        hidden = (jax.nn.silu(gate) * up).astype(jnp.bfloat16)
        part = jnp.dot(hidden, f_ref[...], preferred_element_type=jnp.float32)
        out_ref[...] = jnp.where(step == 1, 0.0, out_ref[...]) + part

    @pl.when(step == 0)
    def _():
        for k, ref in enumerate(x_refs):
            xn[k * rows : (k + 1) * rows, :] = ref[...]
        first_product(even)

    @pl.when((step > 0) & (step < tiles) & (step % 2 == 1))
    def _():
        second_product(even)
        first_product(odd)

    @pl.when((step > 0) & (step < tiles) & (step % 2 == 0))
    def _():
        second_product(odd)
        first_product(even)

    @pl.when(step == tiles)
    def _():
        second_product(even if tiles % 2 == 1 else odd)


def chunk(xs, weights, in_factor, left, index, tokens):
    packing = left is None
    pieces = len(xs)
    rows, depth = xs[0].shape
    units, order = in_factor.shape
    tiles = units // LANES
    total = pieces * rows
    tile = pl.BlockSpec((1, depth, 2 * LANES), lambda i: (jnp.minimum(i, tiles - 1), 0, 0))
    in_specs = [pl.BlockSpec((rows, depth), lambda i: (0, 0))] * pieces
    out_specs = [pl.BlockSpec((total, order), lambda i: (index, 0))]
    out_shape = [jax.ShapeDtypeStruct((tokens, order), jnp.float32)]
    if packing:
        operands = [*xs, *weights, in_factor]
        in_specs += [pl.BlockSpec((depth, LANES), lambda i: (0, jnp.minimum(i, tiles - 1)))] * 2
        out_specs.append(tile)
        out_shape.append(jax.ShapeDtypeStruct((tiles, depth, 2 * LANES), jnp.bfloat16))
        aliases = {}
    else:
        operands = [*xs, weights, in_factor, left]
        in_specs.append(tile)
        aliases = {pieces + 2: 0}
    in_specs.append(pl.BlockSpec((LANES, order), lambda i: (jnp.maximum(i - 1, 0), 0)))
    if not packing:
        in_specs.append(pl.BlockSpec(memory_space=pl.ANY))
    made = pl.pallas_call(
        functools.partial(chunk_body, pieces, tiles, packing),
        grid=(tiles + 1,),
        in_specs=in_specs,
        out_specs=out_specs,
        out_shape=out_shape,
        scratch_shapes=[pltpu.VMEM((total, depth), jnp.bfloat16)]
        + [pltpu.VMEM((total, 2 * LANES), jnp.float32)] * 2,
        input_output_aliases=aliases,
        compiler_params=pltpu.CompilerParams(vmem_limit_bytes=50 * MIB),
        cost_estimate=pl.CostEstimate(
            flops=2 * total * depth * tiles * 2 * LANES,
            bytes_accessed=(8 if packing else 4) * depth * units,
            transcendentals=0,
        ),
        name="first_chunk" if packing else "chunk",
    )(*operands)
    return made if packing else made[0]


def one_sketch(left_ref, masked, at, half):
    left = jnp.concatenate([left_ref[p * half : (p + 1) * half, :] for p in at], axis=0)
    high = left.astype(jnp.bfloat16)
    low = (left - high.astype(jnp.float32)).astype(jnp.bfloat16)
    return sum(lax.dot_general(part, masked, TN, preferred_element_type=jnp.float32) for part in (low, high))


def sketch_body(places, half, names, left_ref, side_ref, out_ref):
    for r, at in enumerate(places):
        masked = side_ref[names[r], : 2 * half, :]
        out_ref[r] = one_sketch(left_ref, masked, at, half).astype(out_ref.dtype)


def sketches(places, half, names, left, side):
    order = left.shape[1]
    vmem = pl.BlockSpec(memory_space=pltpu.VMEM)
    made = pl.pallas_call(
        functools.partial(sketch_body, places, half),
        in_specs=[pl.BlockSpec(memory_space=pltpu.SMEM), vmem, vmem],
        out_specs=vmem,
        out_shape=jax.ShapeDtypeStruct((len(places), order, order), jnp.bfloat16),
        compiler_params=pltpu.CompilerParams(vmem_limit_bytes=8 * MIB),
        cost_estimate=pl.CostEstimate(flops=400_000_000 * len(places), bytes_accessed=0, transcendentals=0),
        name="sketches",
    )(names, left, side)
    return made.reshape(len(places), order * order)


def finish_body(places, half, groups, names, left_ref, side_ref, early_ref, *refs):
    query_refs, (ids_ref, out_ref, twice, flat, whole) = refs[:groups], refs[groups:]
    order = left_ref.shape[1]
    early = early_ref.shape[0]
    slots = flat.shape[1]
    lane = lax.broadcasted_iota(jnp.int32, (order // 2, 2 * order), 1)
    for r, at in enumerate(places):
        masked = side_ref[names[early + r], : 2 * half, :]
        sketch = one_sketch(left_ref, masked, at, half)
        twice[...] = jnp.concatenate([sketch, sketch], axis=1)
        even = twice[pl.ds(0, order // 2, 2), :]
        odd = twice[pl.ds(1, order // 2, 2), :]
        flat[:, r, :] = jnp.where(lane < order, even, odd)
    late = jnp.concatenate([flat[c] for c in range(order // 2)], axis=1).astype(jnp.bfloat16)
    whole[...] = jnp.concatenate([late, early_ref[...]], axis=0)

    width = query_refs[0].shape[1]
    group = lax.axis_index("groups")
    scores = 0.0
    for r, ref in enumerate(query_refs):
        offset = pl.multiple_of(lax.rem(group + r, groups) * width, width)
        scores += lax.dot_general(whole[:, pl.ds(offset, width)], ref[...], NT, preferred_element_type=jnp.float32)
    value = lax.broadcasted_iota(jnp.int32, (NVAL, ids_ref.shape[1]), 0)
    members = (value == ids_ref[...]).astype(jnp.bfloat16)
    rows = 0.0
    for _ in range(3):
        part = scores.astype(jnp.bfloat16)
        scores = scores - part.astype(jnp.float32)
        rows += lax.dot_general(part, members, NT, preferred_element_type=jnp.float32)
    for r in range(early):
        out_ref[pl.ds(names[r], 1), :] = rows[slots + r : slots + r + 1, :]
    for r in range(len(places)):
        out_ref[pl.ds(names[early + r], 1), :] = rows[r : r + 1, :]


def finish(places, half, names, left, side, early, queries, ids):
    order = left.shape[1]
    vmem = pl.BlockSpec(memory_space=pltpu.VMEM)
    slots = -(-len(places) // 8) * 8
    return pl.pallas_call(
        functools.partial(finish_body, places, half, len(queries)),
        in_specs=[pl.BlockSpec(memory_space=pltpu.SMEM)] + [vmem] * (4 + len(queries)),
        out_specs=vmem,
        out_shape=jax.ShapeDtypeStruct((names.shape[0], NVAL), jnp.float32),
        scratch_shapes=[
            pltpu.VMEM((order, 2 * order), jnp.float32),
            pltpu.VMEM((order // 2, slots, 2 * order), jnp.float32),
            pltpu.VMEM((slots + early.shape[0], order * order), jnp.bfloat16),
        ],
        compiler_params=pltpu.CompilerParams(vmem_limit_bytes=16 * MIB),
        name="finish",
    )(names, left, side, early, *queries, ids)


def local(
    devices,
    groups,
    layer_inputs,
    example_lengths,
    norm_gain,
    gate_weight,
    up_weight,
    in_factor,
    out_factor,
    out_grads,
    queries,
    query_ids,
):
    chips = devices // 2
    far = chips // 2
    ring = chip_ring(chips)
    me = lax.axis_index("examples")
    core = me % 2
    place = jnp.array([ring.index(c) for c in range(chips)], jnp.int32)[me // 2]

    forward = [(ring[r] * 2 + c, ring[(r + 1) % chips] * 2 + c) for r in range(chips) for c in range(2)]
    backward = [(b, a) for a, b in forward]
    other_core = [(d, d ^ 1) for d in range(devices)]

    span, depth = layer_inputs.shape
    half = span // 2
    order = in_factor.shape[1]
    units = gate_weight.shape[1]
    short = -units % LANES
    if short:
        gate_weight = jnp.pad(gate_weight, ((0, 0), (0, short)))
        up_weight = jnp.pad(up_weight, ((0, 0), (0, short)))
        in_factor = jnp.pad(in_factor, ((0, short), (0, 0)))
    tokens = 2 * span * chips + span

    def send(x, way):
        return lax.ppermute(x, "examples", way)

    def project(xs, left, index):
        return chunk(xs, weights, in_factor, left, index, tokens)

    x_a, x_b, mine = prepare(layer_inputs, norm_gain[None, :], queries, groups)
    coming = {
        1: (send(x_a, forward), send(x_a, backward)),
        2: (send(x_b, forward), send(x_b, backward)),
    }
    swapped = tuple(send(x, other_core) for x in (x_a, x_b))
    weights = (gate_weight, up_weight)
    left, weights = project((x_a, x_b), None, 1)

    out_grads, query_ids, mine, left = lax.optimization_barrier((out_grads, query_ids, mine, left))
    right = jnp.dot(out_grads, out_factor, preferred_element_type=jnp.float32)
    live = jnp.arange(span, dtype=jnp.int32)[:, None] < example_lengths[0]
    masked = jnp.where(live, right, 0.0).astype(jnp.bfloat16)
    nq, width = mine.shape
    masked = masked.reshape(span * order // width, width)
    ids_row = jnp.pad(query_ids.astype(jnp.bfloat16)[None, :], ((0, 0), (0, width - nq)))
    more = jnp.concatenate([mine, masked, ids_row], axis=0)
    more = jnp.pad(more, ((0, -more.shape[0] % 8), (0, 0)))
    more = lax.all_gather(more, "examples", axis=0)

    def pair(where):
        first = jnp.array(ring, jnp.int32)[where % chips] * 2
        return [first + core, first + 1 - core]

    names, spots = [], []
    for distance in range(far + 1):
        sides = [(1, 0)] if distance in (0, far) else [(-1, 0), (1, 1)]
        for sign, piece in sides:
            names += pair(place + sign * distance)
            if distance == 0:
                halves = [(0, 0), (0, 1)]
            elif distance == far:
                halves = [(chips - 1, 0), (chips - 1, 1)]
            else:
                halves = [(2 * distance - 1, piece), (2 * distance, piece)]
            spots.append([4 * k + 2 + p for k, p in halves])
            spots.append([4 * k + 4 + p for k, p in halves])
    names = jnp.stack(names)

    for k in range(1, chips):
        own_1, own_2, left = lax.optimization_barrier((*coming.pop(k), left))
        own = (own_1, own_2)
        if k + 2 < chips - 1:
            coming[k + 2] = (send(own_1, forward), send(own_2, backward))
        elif k + 2 == chips - 1:
            opposite = send(own_1, forward)
        elif k + 1 == chips - 1:
            coming[chips - 1] = (opposite, send(own_2, backward))
        before, swapped = swapped, tuple(send(x, other_core) for x in own)
        if k < chips - 1:
            left = project(before + own, left, k)
        if k == chips - 3:
            more, left = lax.optimization_barrier((more, left))
            mine = more[:, :nq].reshape(devices * nq, width)
            side = more[:, nq : nq + masked.shape[0]].reshape(devices, span, order)
            shares = [mine]
            for r in range(1, groups):
                way = [((g + r) % groups, g) for g in range(groups)]
                shares.append(lax.ppermute(mine, "groups", way))
            ids = more[:, nq + masked.shape[0], :nq].astype(jnp.int32).reshape(1, devices * nq)
            ready = devices - 6
            early = [sketches(spots[:ready], half, names[:ready], left, side)]
        if k == chips - 2:
            left = project(swapped, left, 2 * k + 2)
            early.append(sketches(spots[ready:-2], half, names[ready:-2], left, side))
            early = jnp.concatenate(early, axis=0)
            early, left = lax.optimization_barrier((early, left))
    left = project(own, left, 2 * chips - 1)
    left = project(swapped, left, 2 * chips)

    partial = finish(spots[-2:], half, names, left, side, early, shares, ids)
    shares = lax.all_to_all(partial, "examples", split_axis=0, concat_axis=0, tiled=True)
    return jnp.sum(shares, axis=0, keepdims=True)


def solution(mesh):
    return jax.shard_map(
        functools.partial(local, mesh.shape["examples"], mesh.shape["groups"]),
        mesh=mesh,
        in_specs=(
            P(("groups", "examples"), None),
            P(("groups", "examples")),
            P(),
            P(None, "examples"),
            P(None, "examples"),
            P("examples", None),
            P(),
            P(("groups", "examples"), None),
            P("examples", None),
            P("examples"),
        ),
        out_specs=P(("groups", "examples"), None),
        check_vma=False,
    )
```

```python
import functools

import jax
import jax.numpy as jnp
from jax import lax
from jax.experimental import pallas as pl
from jax.experimental.pallas import tpu as pltpu
from jax.sharding import PartitionSpec as P

NVAL = 256
LANES = 128
MIB = 1024 * 1024
NT = (((1,), (1,)), ((), ()))
TN = (((0,), (0,)), ((), ()))
SMALL = pl.CostEstimate(flops=1_000_000, bytes_accessed=100_000, transcendentals=0)


def chip_ring(chips):
    if chips == 8:
        return [0, 2, 4, 6, 7, 5, 3, 1]
    return list(range(chips))


def prepare_body(width, x_ref, gain_ref, queries_ref, a_ref, b_ref, mine_ref):
    half = a_ref.shape[0]
    block = 16
    for start in range(0, 2 * half, block):
        x = x_ref[start : start + block, :].astype(jnp.float32)
        scale = lax.rsqrt(jnp.mean(x * x, axis=-1, keepdims=True) + 1e-05)
        rows = (x * scale * gain_ref[...]).astype(jnp.bfloat16)
        if start < half:
            a_ref[start : start + block, :] = rows
        else:
            b_ref[start - half : start - half + block, :] = rows
    offset = pl.multiple_of(lax.axis_index("groups") * width, width)
    mine_ref[...] = queries_ref[:, pl.ds(offset, width)]


def prepare(x, gain, queries, groups):
    span, depth = x.shape
    width = depth // groups
    vmem = pl.BlockSpec(memory_space=pltpu.VMEM)
    rows = jax.ShapeDtypeStruct((span // 2, depth), jnp.bfloat16)
    return pl.pallas_call(
        functools.partial(prepare_body, width),
        in_specs=[vmem] * 3,
        out_specs=[vmem] * 3,
        out_shape=[rows, rows, jax.ShapeDtypeStruct((queries.shape[0], width), queries.dtype)],
        compiler_params=pltpu.CompilerParams(vmem_limit_bytes=16 * MIB),
        name="prepare",
    )(x, gain, queries)


def tile_product(x, w):
    return jnp.dot(x, w, preferred_element_type=jnp.float32)


def projected(both, factor):
    gate, up = both[:, :LANES], both[:, LANES:]
    hidden = (jax.nn.silu(gate) * up).astype(jnp.bfloat16)
    return jnp.dot(hidden, factor, preferred_element_type=jnp.float32)


def gather_rows(x_refs, xn):
    rows = x_refs[0].shape[0]
    for k, ref in enumerate(x_refs):
        xn[k * rows : (k + 1) * rows, :] = ref[...]


def first_body(pieces, *refs):
    x_refs, (gate_ref, up_ref, f_ref, out_ref, w_ref, xn) = refs[:pieces], refs[pieces:]
    step = pl.program_id(0)

    @pl.when(step == 0)
    def _():
        gather_rows(x_refs, xn)

    w_ref[step, :, :LANES] = gate_ref[...]
    w_ref[step, :, LANES:] = up_ref[...]
    part = projected(tile_product(xn[...], w_ref[step]), f_ref[...])
    out_ref[...] = jnp.where(step == 0, 0.0, out_ref[...]) + part


def first_chunk(xs, gate_weight, up_weight, in_factor, index, tokens):
    pieces = len(xs)
    rows, depth = xs[0].shape
    units, order = in_factor.shape
    tiles = units // LANES
    total = pieces * rows
    return pl.pallas_call(
        functools.partial(first_body, pieces),
        grid=(tiles,),
        in_specs=[pl.BlockSpec((rows, depth), lambda i: (0, 0))] * pieces
        + [
            pl.BlockSpec((depth, LANES), lambda i: (0, i)),
            pl.BlockSpec((depth, LANES), lambda i: (0, i)),
            pl.BlockSpec((LANES, order), lambda i: (i, 0)),
        ],
        out_specs=[
            pl.BlockSpec((total, order), lambda i: (index, 0)),
            pl.BlockSpec(memory_space=pltpu.VMEM),
        ],
        out_shape=[
            jax.ShapeDtypeStruct((tokens, order), jnp.float32),
            pltpu.VMEM((tiles, depth, 2 * LANES), jnp.bfloat16),
        ],
        scratch_shapes=[pltpu.VMEM((total, depth), jnp.bfloat16)],
        compiler_params=pltpu.CompilerParams(vmem_limit_bytes=14 * MIB),
        cost_estimate=SMALL,
        name="first_chunk",
    )(*xs, gate_weight, up_weight, in_factor)


def chunk_body(pieces, *refs):
    x_refs, (w_ref, f_ref, _, out_ref, xn) = refs[:pieces], refs[pieces:]
    gather_rows(x_refs, xn)
    total = 0.0
    before = None
    for tile in range(w_ref.shape[0]):
        both = tile_product(xn[...], w_ref[tile])
        if before is not None:
            total += projected(before, f_ref[(tile - 1) * LANES : tile * LANES, :])
        before = both
    out_ref[...] = total + projected(before, f_ref[tile * LANES :, :])


def chunk(xs, weights, in_factor, left, index):
    pieces = len(xs)
    rows, depth = xs[0].shape
    order = in_factor.shape[1]
    total = pieces * rows
    vmem = pl.BlockSpec(memory_space=pltpu.VMEM)
    weights = pltpu.with_memory_space_constraint(weights, pltpu.VMEM)
    return pl.pallas_call(
        functools.partial(chunk_body, pieces),
        grid=(1,),
        in_specs=[vmem] * (pieces + 2) + [pl.BlockSpec(memory_space=pl.ANY)],
        out_specs=pl.BlockSpec((total, order), lambda i: (index, 0)),
        out_shape=jax.ShapeDtypeStruct(left.shape, left.dtype),
        scratch_shapes=[pltpu.VMEM((total, depth), jnp.bfloat16)],
        input_output_aliases={pieces + 2: 0},
        compiler_params=pltpu.CompilerParams(vmem_limit_bytes=12 * MIB),
        cost_estimate=SMALL,
        name="chunk",
    )(*xs, weights, in_factor, left)


def one_sketch(left_ref, masked, at, half):
    left = jnp.concatenate([left_ref[p * half : (p + 1) * half, :] for p in at], axis=0)
    high = left.astype(jnp.bfloat16)
    low = (left - high.astype(jnp.float32)).astype(jnp.bfloat16)
    return sum(lax.dot_general(part, masked, TN, preferred_element_type=jnp.float32) for part in (low, high))


def sketch_body(places, half, names, left_ref, side_ref, out_ref):
    for r, at in enumerate(places):
        masked = side_ref[names[r], : 2 * half, :]
        out_ref[r] = one_sketch(left_ref, masked, at, half).astype(out_ref.dtype)


def sketches(places, half, names, left, side):
    order = left.shape[1]
    vmem = pl.BlockSpec(memory_space=pltpu.VMEM)
    made = pl.pallas_call(
        functools.partial(sketch_body, places, half),
        in_specs=[pl.BlockSpec(memory_space=pltpu.SMEM), vmem, vmem],
        out_specs=vmem,
        out_shape=jax.ShapeDtypeStruct((len(places), order, order), jnp.bfloat16),
        compiler_params=pltpu.CompilerParams(vmem_limit_bytes=8 * MIB),
        cost_estimate=SMALL,
        name="sketches",
    )(names, left, side)
    return made.reshape(len(places), order * order)


def finish_body(places, half, groups, names, left_ref, side_ref, early_ref, *refs):
    query_refs, (ids_ref, out_ref, twice, flat, whole) = refs[:groups], refs[groups:]
    order = left_ref.shape[1]
    early = early_ref.shape[0]
    slots = flat.shape[1]
    lane = lax.broadcasted_iota(jnp.int32, (order // 2, 2 * order), 1)
    for r, at in enumerate(places):
        masked = side_ref[names[early + r], : 2 * half, :]
        sketch = one_sketch(left_ref, masked, at, half)
        twice[...] = jnp.concatenate([sketch, sketch], axis=1)
        even = twice[pl.ds(0, order // 2, 2), :]
        odd = twice[pl.ds(1, order // 2, 2), :]
        flat[:, r, :] = jnp.where(lane < order, even, odd)
    late = jnp.concatenate([flat[c] for c in range(order // 2)], axis=1).astype(jnp.bfloat16)
    whole[...] = jnp.concatenate([late, early_ref[...]], axis=0)

    width = query_refs[0].shape[1]
    group = lax.axis_index("groups")
    scores = 0.0
    for r, ref in enumerate(query_refs):
        offset = pl.multiple_of(lax.rem(group + r, groups) * width, width)
        scores += lax.dot_general(whole[:, pl.ds(offset, width)], ref[...], NT, preferred_element_type=jnp.float32)
    value = lax.broadcasted_iota(jnp.int32, (NVAL, ids_ref.shape[1]), 0)
    members = (value == ids_ref[...]).astype(jnp.bfloat16)
    rows = 0.0
    for _ in range(3):
        part = scores.astype(jnp.bfloat16)
        scores = scores - part.astype(jnp.float32)
        rows += lax.dot_general(part, members, NT, preferred_element_type=jnp.float32)
    for r in range(early):
        out_ref[pl.ds(names[r], 1), :] = rows[slots + r : slots + r + 1, :]
    for r in range(len(places)):
        out_ref[pl.ds(names[early + r], 1), :] = rows[r : r + 1, :]


def finish(places, half, names, left, side, early, queries, ids):
    order = left.shape[1]
    vmem = pl.BlockSpec(memory_space=pltpu.VMEM)
    slots = -(-len(places) // 8) * 8
    return pl.pallas_call(
        functools.partial(finish_body, places, half, len(queries)),
        in_specs=[pl.BlockSpec(memory_space=pltpu.SMEM)] + [vmem] * (4 + len(queries)),
        out_specs=vmem,
        out_shape=jax.ShapeDtypeStruct((names.shape[0], NVAL), jnp.float32),
        scratch_shapes=[
            pltpu.VMEM((order, 2 * order), jnp.float32),
            pltpu.VMEM((order // 2, slots, 2 * order), jnp.float32),
            pltpu.VMEM((slots + early.shape[0], order * order), jnp.bfloat16),
        ],
        compiler_params=pltpu.CompilerParams(vmem_limit_bytes=16 * MIB),
        name="finish",
    )(names, left, side, early, *queries, ids)


def arrivals(ring, devices):
    chips = len(ring)
    far = chips // 2
    table, spots = [[] for _ in range(devices)], []
    for distance in range(far + 1):
        for sign, piece in [(1, 0)] if distance in (0, far) else [(-1, 0), (1, 1)]:
            for me in range(devices):
                chip = ring[(ring.index(me // 2) + sign * distance) % chips]
                table[me] += [2 * chip + me % 2, 2 * chip + 1 - me % 2]
            if distance == 0:
                halves = [(0, 0), (0, 1)]
            elif distance == far:
                halves = [(chips - 1, 0), (chips - 1, 1)]
            else:
                halves = [(2 * distance - 1, piece), (2 * distance, piece)]
            spots.append([4 * k + 2 + p for k, p in halves])
            spots.append([4 * k + 4 + p for k, p in halves])
    return table, spots


def local(
    devices,
    groups,
    layer_inputs,
    example_lengths,
    norm_gain,
    gate_weight,
    up_weight,
    in_factor,
    out_factor,
    out_grads,
    queries,
    query_ids,
):
    chips = devices // 2
    ring = chip_ring(chips)
    me = lax.axis_index("examples")

    forward = [(ring[r] * 2 + c, ring[(r + 1) % chips] * 2 + c) for r in range(chips) for c in range(2)]
    backward = [(b, a) for a, b in forward]
    other_core = [(d, d ^ 1) for d in range(devices)]

    span, depth = layer_inputs.shape
    half = span // 2
    order = in_factor.shape[1]
    units = gate_weight.shape[1]
    short = -units % LANES
    if short:
        gate_weight = jnp.pad(gate_weight, ((0, 0), (0, short)))
        up_weight = jnp.pad(up_weight, ((0, 0), (0, short)))
        in_factor = jnp.pad(in_factor, ((0, short), (0, 0)))
    tokens = 2 * span * chips + span

    def send(x, way):
        return lax.ppermute(x, "examples", way)

    def project(xs, left, index):
        return chunk(xs, weights, in_factor, left, index)

    x_a, x_b, mine = prepare(layer_inputs, norm_gain[None, :], queries, groups)
    coming = {
        1: (send(x_a, forward), send(x_a, backward)),
        2: (send(x_b, forward), send(x_b, backward)),
    }
    swapped = tuple(send(x, other_core) for x in (x_a, x_b))
    mine = lax.all_gather(mine, "examples", axis=0, tiled=True)
    left, weights = first_chunk((x_a, x_b), gate_weight, up_weight, in_factor, 1, tokens)

    out_grads, query_ids, left = lax.optimization_barrier((out_grads, query_ids, left))
    right = jnp.dot(out_grads, out_factor, preferred_element_type=jnp.float32)
    live = jnp.arange(span, dtype=jnp.int32)[:, None] < example_lengths[0]
    masked = jnp.where(live, right, 0.0).astype(jnp.bfloat16)
    nq = queries.shape[0]
    ids_row = jnp.pad(query_ids.astype(jnp.bfloat16)[None, :], ((0, 15), (0, order - nq)))
    side = lax.all_gather(jnp.concatenate([masked, ids_row], axis=0), "examples", axis=0)

    names, spots = arrivals(ring, devices)
    names = lax.dynamic_index_in_dim(jnp.array(names, jnp.int32), me, keepdims=False)

    for k in range(1, chips):
        own_1, own_2, left = lax.optimization_barrier((*coming.pop(k), left))
        own = (own_1, own_2)
        if k + 2 < chips - 1:
            coming[k + 2] = (send(own_1, forward), send(own_2, backward))
        elif k + 2 == chips - 1:
            opposite = send(own_1, forward)
        elif k + 1 == chips - 1:
            coming[chips - 1] = (opposite, send(own_2, backward))
        before, swapped = swapped, tuple(send(x, other_core) for x in own)
        if k == chips - 5:
            mine, left = lax.optimization_barrier((mine, left))
            shares = [mine]
            for r in range(1, groups):
                way = [((g + r) % groups, g) for g in range(groups)]
                shares.append(lax.ppermute(mine, "groups", way))
        if k < chips - 1:
            left = project(before + own, left, k)
        if k == chips - 3:
            side, left = lax.optimization_barrier((side, left))
            ids = side[:, span, :nq].astype(jnp.int32).reshape(1, devices * nq)
            ready = devices - 6
            early = [sketches(spots[:ready], half, names[:ready], left, side)]
        if k == chips - 2:
            left = project(swapped, left, 2 * k + 2)
            early.append(sketches(spots[ready:-2], half, names[ready:-2], left, side))
            early = jnp.concatenate(early, axis=0)
            early, left = lax.optimization_barrier((early, left))
    left = project(own, left, 2 * chips - 1)
    left = project(swapped, left, 2 * chips)

    partial = finish(spots[-2:], half, names, left, side, early, shares, ids)
    shares = lax.all_to_all(partial, "examples", split_axis=0, concat_axis=0, tiled=True)
    return jnp.sum(shares, axis=0, keepdims=True)


def solution(mesh):
    return jax.shard_map(
        functools.partial(local, mesh.shape["examples"], mesh.shape["groups"]),
        mesh=mesh,
        in_specs=(
            P(("groups", "examples"), None),
            P(("groups", "examples")),
            P(),
            P(None, "examples"),
            P(None, "examples"),
            P("examples", None),
            P(),
            P(("groups", "examples"), None),
            P("examples", None),
            P("examples"),
        ),
        out_specs=P(("groups", "examples"), None),
        check_vma=False,
    )
```

```python
import functools

import jax
import jax.numpy as jnp
from jax import lax
from jax.experimental import pallas as pl
from jax.experimental.pallas import tpu as pltpu
from jax.sharding import PartitionSpec as P

NVAL = 256
LANES = 128
MIB = 1024 * 1024
NT = (((1,), (1,)), ((), ()))
TN = (((0,), (0,)), ((), ()))
SMALL = pl.CostEstimate(flops=1_000_000, bytes_accessed=100_000, transcendentals=0)


def chip_ring(chips):
    if chips == 8:
        return [0, 2, 4, 6, 7, 5, 3, 1]
    return list(range(chips))


def prepare_body(x_ref, gain_ref, a_ref, b_ref):
    half = a_ref.shape[0]
    block = 16
    for start in range(0, 2 * half, block):
        x = x_ref[start : start + block, :].astype(jnp.float32)
        scale = lax.rsqrt(jnp.mean(x * x, axis=-1, keepdims=True) + 1e-05)
        rows = (x * scale * gain_ref[...]).astype(jnp.bfloat16)
        if start < half:
            a_ref[start : start + block, :] = rows
        else:
            b_ref[start - half : start - half + block, :] = rows


def prepare(x, gain):
    span, depth = x.shape
    vmem = pl.BlockSpec(memory_space=pltpu.VMEM)
    rows = jax.ShapeDtypeStruct((span // 2, depth), jnp.bfloat16)
    return pl.pallas_call(
        prepare_body,
        in_specs=[vmem] * 2,
        out_specs=[vmem] * 2,
        out_shape=[rows, rows],
        compiler_params=pltpu.CompilerParams(vmem_limit_bytes=12 * MIB),
        cost_estimate=SMALL,
        name="prepare",
    )(x, gain)


def share_body(lengths_ref, grads_ref, factor_ref, ids_ref, queries_ref, _, out_ref):
    count, width = queries_ref.shape[0], out_ref.shape[1]
    span, order = grads_ref.shape[0], factor_ref.shape[1]
    rows = span * LANES // width
    offset = pl.multiple_of(lax.axis_index("groups") * width, width)
    out_ref[:count, :] = queries_ref[:, pl.ds(offset, width)]
    right = jnp.dot(grads_ref[...], factor_ref[...], preferred_element_type=jnp.float32)
    live = lax.broadcasted_iota(jnp.int32, (span, order), 0) < lengths_ref[0]
    masked = jnp.where(live, right, 0.0)
    both = jnp.concatenate([masked, jnp.broadcast_to(ids_ref[...], (span, LANES - order))], axis=1)
    wide = jnp.concatenate([both[r : r + rows, :] for r in range(0, span, rows)], axis=1)
    out_ref[count : count + rows, :] = wide.astype(out_ref.dtype)
    if count + rows < out_ref.shape[0]:
        out_ref[count + rows :, :] = jnp.zeros((out_ref.shape[0] - count - rows, width), out_ref.dtype)


def own_share(lengths, grads, factor, ids, queries, after, groups):
    count, depth = queries.shape
    width = depth // groups
    span, order = grads.shape[0], factor.shape[1]
    rows = span * LANES // width
    ids = jnp.pad(ids.astype(jnp.float32)[None, :], ((0, 0), (0, LANES - order - count)))
    vmem = pl.BlockSpec(memory_space=pltpu.VMEM)
    return pl.pallas_call(
        share_body,
        in_specs=[pl.BlockSpec(memory_space=pltpu.SMEM)] + [vmem] * 4 + [pl.BlockSpec(memory_space=pl.ANY)],
        out_specs=vmem,
        out_shape=jax.ShapeDtypeStruct((-(-(count + rows) // 8) * 8, width), queries.dtype),
        compiler_params=pltpu.CompilerParams(vmem_limit_bytes=12 * MIB),
        cost_estimate=SMALL,
        name="own_share",
    )(lengths, grads, factor, ids, queries, after)


def gather_rows(x_refs, xn):
    rows = x_refs[0].shape[0]
    for k, ref in enumerate(x_refs):
        xn[k * rows : (k + 1) * rows, :] = ref[...]


def gated(gate, up):
    return (jax.nn.silu(gate) * up).astype(jnp.bfloat16)


def project(xn, gate_ref, up_ref, mix_ref, f_ref):
    units, order = f_ref.shape
    wide = 2 * LANES

    def product(w):
        return jnp.dot(xn[...], w, preferred_element_type=jnp.float32)

    total = jnp.zeros((xn.shape[0], order), jnp.float32)
    hidden, start = None, 0
    for at in range(0, units, wide):
        if at + wide <= units:
            gate = product(gate_ref[:, at : at + wide])
            if hidden is not None:
                total += jnp.dot(hidden, f_ref[start:at, :], preferred_element_type=jnp.float32)
            hidden = gated(gate, product(up_ref[:, at : at + wide]))
        else:
            both = product(mix_ref[...])
            if hidden is not None:
                total += jnp.dot(hidden, f_ref[start:at, :], preferred_element_type=jnp.float32)
            hidden = gated(both[:, :LANES], both[:, LANES:])
        start = at
    return total + jnp.dot(hidden, f_ref[start:, :], preferred_element_type=jnp.float32)


def first_body(pieces, *refs):
    x_refs, (gate_hbm, up_hbm, f_ref, out_ref, gate_ref, up_ref, mix_ref, xn, sems) = refs[:pieces], refs[pieces:]
    depth, units = gate_ref.shape
    parts = sems.shape[1]
    copies = []
    for p in range(parts):
        rows = pl.ds(p * (depth // parts), depth // parts)
        copies.append(pltpu.make_async_copy(gate_hbm.at[rows], gate_ref.at[rows], sems.at[0, p]))
        copies.append(pltpu.make_async_copy(up_hbm.at[rows], up_ref.at[rows], sems.at[1, p]))
    for copy in copies:
        copy.start()
    gather_rows(x_refs, xn)
    for copy in copies:
        copy.wait()
    if units % (2 * LANES):
        mix_ref[:, :LANES] = gate_ref[:, units - LANES :]
        mix_ref[:, LANES:] = up_ref[:, units - LANES :]
    out_ref[...] = project(xn, gate_ref, up_ref, mix_ref, f_ref)


def first_chunk(xs, gate_weight, up_weight, in_factor, index, tokens):
    pieces = len(xs)
    rows, depth = xs[0].shape
    units, order = in_factor.shape
    total = pieces * rows
    vmem = pl.BlockSpec(memory_space=pltpu.VMEM)
    hbm = pl.BlockSpec(memory_space=pltpu.HBM)
    mix = 2 * LANES if units % (2 * LANES) else LANES
    left, *weights = pl.pallas_call(
        functools.partial(first_body, pieces),
        grid=(1,),
        in_specs=[vmem] * pieces + [hbm, hbm, vmem],
        out_specs=[pl.BlockSpec((total, order), lambda i: (index, 0)), vmem, vmem, vmem],
        out_shape=[
            jax.ShapeDtypeStruct((tokens, order), jnp.float32),
            pltpu.VMEM((depth, units), jnp.bfloat16),
            pltpu.VMEM((depth, units), jnp.bfloat16),
            pltpu.VMEM((depth if mix > LANES else 16, mix), jnp.bfloat16),
        ],
        scratch_shapes=[pltpu.VMEM((total, depth), jnp.bfloat16), pltpu.SemaphoreType.DMA((2, 4))],
        compiler_params=pltpu.CompilerParams(vmem_limit_bytes=12 * MIB),
        cost_estimate=SMALL,
        name="first_chunk",
    )(
        *xs,
        pltpu.with_memory_space_constraint(gate_weight, pltpu.HBM),
        pltpu.with_memory_space_constraint(up_weight, pltpu.HBM),
        in_factor,
    )
    return left, weights


def chunk_body(pieces, *refs):
    x_refs, (gate_ref, up_ref, mix_ref, f_ref, _, out_ref, _, _, _, xn) = refs[:pieces], refs[pieces:]
    gather_rows(x_refs, xn)
    out_ref[...] = project(xn, gate_ref, up_ref, mix_ref, f_ref)


def chunk(xs, weights, in_factor, left, index):
    pieces = len(xs)
    rows, depth = xs[0].shape
    order = in_factor.shape[1]
    total = pieces * rows
    vmem = pl.BlockSpec(memory_space=pltpu.VMEM)
    left, *weights = pl.pallas_call(
        functools.partial(chunk_body, pieces),
        grid=(1,),
        in_specs=[vmem] * (pieces + 4) + [pl.BlockSpec(memory_space=pl.ANY)],
        out_specs=[pl.BlockSpec((total, order), lambda i: (index, 0)), vmem, vmem, vmem],
        out_shape=[jax.ShapeDtypeStruct(left.shape, left.dtype)] + [pltpu.VMEM(w.shape, w.dtype) for w in weights],
        scratch_shapes=[pltpu.VMEM((total, depth), jnp.bfloat16)],
        input_output_aliases={pieces + 4: 0, pieces: 1, pieces + 1: 2, pieces + 2: 3},
        compiler_params=pltpu.CompilerParams(vmem_limit_bytes=12 * MIB),
        cost_estimate=SMALL,
        name="chunk",
    )(*xs, *[pltpu.with_memory_space_constraint(w, pltpu.VMEM) for w in weights], in_factor, left)
    return left, weights


def masked_of(side_ref, name, count, span, order):
    width = side_ref.shape[2]
    rows = span * LANES // width
    wide = side_ref[name, count : count + rows, :].astype(jnp.float32)
    both = jnp.concatenate([wide[:, c : c + LANES] for c in range(0, width, LANES)], axis=0)
    return both[:, :order].astype(jnp.bfloat16)


def one_sketch(left_ref, masked, at, half):
    left = jnp.concatenate([left_ref[p * half : (p + 1) * half, :] for p in at], axis=0)
    high = left.astype(jnp.bfloat16)
    low = (left - high.astype(jnp.float32)).astype(jnp.bfloat16)
    return sum(lax.dot_general(part, masked, TN, preferred_element_type=jnp.float32) for part in (low, high))


def sketch_body(places, half, count, names, left_ref, side_ref, out_ref):
    for r, at in enumerate(places):
        masked = masked_of(side_ref, names[r], count, 2 * half, left_ref.shape[1])
        out_ref[r] = one_sketch(left_ref, masked, at, half).astype(out_ref.dtype)


def sketches(places, half, count, names, left, side):
    order = left.shape[1]
    vmem = pl.BlockSpec(memory_space=pltpu.VMEM)
    made = pl.pallas_call(
        functools.partial(sketch_body, places, half, count),
        in_specs=[pl.BlockSpec(memory_space=pltpu.SMEM), vmem, vmem],
        out_specs=vmem,
        out_shape=jax.ShapeDtypeStruct((len(places), order, order), jnp.bfloat16),
        compiler_params=pltpu.CompilerParams(vmem_limit_bytes=8 * MIB),
        cost_estimate=SMALL,
        name="sketches",
    )(names, left, side)
    return made.reshape(len(places), order * order)


def finish_body(places, half, groups, count, names, left_ref, early_ref, *refs):
    share_refs, (ids_ref, out_ref, twice, flat, whole) = refs[:groups], refs[groups:]
    order = left_ref.shape[1]
    early = early_ref.shape[0]
    slots = flat.shape[1]
    lane = lax.broadcasted_iota(jnp.int32, (order // 2, 2 * order), 1)
    for r, at in enumerate(places):
        masked = masked_of(share_refs[0], names[early + r], count, 2 * half, order)
        sketch = one_sketch(left_ref, masked, at, half)
        twice[...] = jnp.concatenate([sketch, sketch], axis=1)
        even = twice[pl.ds(0, order // 2, 2), :]
        odd = twice[pl.ds(1, order // 2, 2), :]
        flat[:, r, :] = jnp.where(lane < order, even, odd)
    late = jnp.concatenate([flat[c] for c in range(order // 2)], axis=1).astype(jnp.bfloat16)
    whole[...] = jnp.concatenate([late, early_ref[...]], axis=0)

    devices, _, width = share_refs[0].shape
    group = lax.axis_index("groups")
    scores = 0.0
    for r, ref in enumerate(share_refs):
        offset = pl.multiple_of(lax.rem(group + r, groups) * width, width)
        queries = ref[:, :count, :].reshape(devices * count, width)
        scores += lax.dot_general(whole[:, pl.ds(offset, width)], queries, NT, preferred_element_type=jnp.float32)
    value = lax.broadcasted_iota(jnp.int32, (NVAL, ids_ref.shape[1]), 0)
    members = (value == ids_ref[...]).astype(jnp.bfloat16)
    rows = 0.0
    for _ in range(3):
        part = scores.astype(jnp.bfloat16)
        scores = scores - part.astype(jnp.float32)
        rows += lax.dot_general(part, members, NT, preferred_element_type=jnp.float32)
    for r in range(early):
        out_ref[pl.ds(names[r], 1), :] = rows[slots + r : slots + r + 1, :]
    for r in range(len(places)):
        out_ref[pl.ds(names[early + r], 1), :] = rows[r : r + 1, :]


def finish(places, half, count, names, left, early, shares, ids):
    order = left.shape[1]
    vmem = pl.BlockSpec(memory_space=pltpu.VMEM)
    slots = -(-len(places) // 8) * 8
    return pl.pallas_call(
        functools.partial(finish_body, places, half, len(shares), count),
        in_specs=[pl.BlockSpec(memory_space=pltpu.SMEM)] + [vmem] * (3 + len(shares)),
        out_specs=vmem,
        out_shape=jax.ShapeDtypeStruct((names.shape[0], NVAL), jnp.float32),
        scratch_shapes=[
            pltpu.VMEM((order, 2 * order), jnp.float32),
            pltpu.VMEM((order // 2, slots, 2 * order), jnp.float32),
            pltpu.VMEM((slots + early.shape[0], order * order), jnp.bfloat16),
        ],
        compiler_params=pltpu.CompilerParams(vmem_limit_bytes=14 * MIB),
        cost_estimate=SMALL,
        name="finish",
    )(names, left, early, *shares, ids)


def arrivals(ring, devices):
    chips = len(ring)
    far = chips // 2
    table, spots = [[] for _ in range(devices)], []
    for distance in range(far + 1):
        for sign, piece in [(1, 0)] if distance in (0, far) else [(-1, 0), (1, 1)]:
            for me in range(devices):
                chip = ring[(ring.index(me // 2) + sign * distance) % chips]
                table[me] += [2 * chip + me % 2, 2 * chip + 1 - me % 2]
            if distance == 0:
                halves = [(0, 0), (0, 1)]
            elif distance == far:
                halves = [(chips - 1, 0), (chips - 1, 1)]
            else:
                halves = [(2 * distance - 1, piece), (2 * distance, piece)]
            spots.append([4 * k + 2 + p for k, p in halves])
            spots.append([4 * k + 4 + p for k, p in halves])
    return table, spots


def local(
    devices,
    groups,
    layer_inputs,
    example_lengths,
    norm_gain,
    gate_weight,
    up_weight,
    in_factor,
    out_factor,
    out_grads,
    queries,
    query_ids,
):
    chips = devices // 2
    ring = chip_ring(chips)
    me = lax.axis_index("examples")

    forward = [(ring[r] * 2 + c, ring[(r + 1) % chips] * 2 + c) for r in range(chips) for c in range(2)]
    backward = [(b, a) for a, b in forward]
    other_core = [(d, d ^ 1) for d in range(devices)]

    span, depth = layer_inputs.shape
    half = span // 2
    order = in_factor.shape[1]
    units = gate_weight.shape[1]
    short = -units % LANES
    if short:
        gate_weight = jnp.pad(gate_weight, ((0, 0), (0, short)))
        up_weight = jnp.pad(up_weight, ((0, 0), (0, short)))
        in_factor = jnp.pad(in_factor, ((0, short), (0, 0)))
    tokens = 2 * span * chips + span

    def send(x, way):
        return lax.ppermute(x, "examples", way)

    x_a, x_b = prepare(layer_inputs, norm_gain[None, :])
    coming = {
        1: (send(x_a, forward), send(x_a, backward)),
        2: (send(x_b, forward), send(x_b, backward)),
    }
    swapped = tuple(send(x, other_core) for x in (x_a, x_b))
    nq = queries.shape[0]
    side = own_share(example_lengths, out_grads, out_factor, query_ids, queries, x_a, groups)
    side, x_a = lax.optimization_barrier((side, x_a))
    side = lax.all_gather(side, "examples", axis=0)
    left, weights = first_chunk((x_a, x_b), gate_weight, up_weight, in_factor, 1, tokens)

    names, spots = arrivals(ring, devices)
    names = lax.dynamic_index_in_dim(jnp.array(names, jnp.int32), me, keepdims=False)

    for k in range(1, chips):
        own_1, own_2, left = lax.optimization_barrier((*coming.pop(k), left))
        own = (own_1, own_2)
        if k + 2 < chips - 1:
            coming[k + 2] = (send(own_1, forward), send(own_2, backward))
        elif k + 2 == chips - 1:
            opposite = send(own_1, forward)
        elif k + 1 == chips - 1:
            coming[chips - 1] = (opposite, send(own_2, backward))
        before, swapped = swapped, tuple(send(x, other_core) for x in own)
        if k < chips - 1:
            left, weights = chunk(before + own, weights, in_factor, left, k)
        if k == chips - 3:
            side, left = lax.optimization_barrier((side, left))
            ids = side[:, nq, order : order + nq].astype(jnp.int32).reshape(1, devices * nq)
            shares = [side]
            for r in range(1, groups):
                way = [((g + r) % groups, g) for g in range(groups)]
                shares.append(lax.ppermute(side, "groups", way))
            ready = devices - 6
            early = [sketches(spots[:ready], half, nq, names[:ready], left, side)]
        if k == chips - 2:
            left, weights = chunk(swapped, weights, in_factor, left, 2 * k + 2)
            early.append(sketches(spots[ready:-2], half, nq, names[ready:-2], left, side))
            early = jnp.concatenate(early, axis=0)
            early, left = lax.optimization_barrier((early, left))
    left, weights = chunk(own, weights, in_factor, left, 2 * chips - 1)
    left, weights = chunk(swapped, weights, in_factor, left, 2 * chips)

    partial = finish(spots[-2:], half, nq, names, left, early, shares, ids)
    shares = lax.all_to_all(partial, "examples", split_axis=0, concat_axis=0, tiled=True)
    return jnp.sum(shares, axis=0, keepdims=True)


def solution(mesh):
    return jax.shard_map(
        functools.partial(local, mesh.shape["examples"], mesh.shape["groups"]),
        mesh=mesh,
        in_specs=(
            P(("groups", "examples"), None),
            P(("groups", "examples")),
            P(),
            P(None, "examples"),
            P(None, "examples"),
            P("examples", None),
            P(),
            P(("groups", "examples"), None),
            P("examples", None),
            P("examples"),
        ),
        out_specs=P(("groups", "examples"), None),
        check_vma=False,
    )
```

```python
import functools

import jax
import jax.numpy as jnp
from jax import lax
from jax.experimental import pallas as pl
from jax.experimental.pallas import tpu as pltpu
from jax.sharding import PartitionSpec as P

NVAL = 256
LANES = 128
MIB = 1024 * 1024
NT = (((1,), (1,)), ((), ()))
TN = (((0,), (0,)), ((), ()))
SMALL = pl.CostEstimate(flops=1_000_000, bytes_accessed=100_000, transcendentals=0)


def chip_ring(chips):
    if chips == 8:
        return [0, 2, 4, 6, 7, 5, 3, 1]
    return list(range(chips))


def prepare_body(x_ref, gain_ref, a_ref, b_ref):
    half = a_ref.shape[0]
    block = 16
    for start in range(0, 2 * half, block):
        x = x_ref[start : start + block, :].astype(jnp.float32)
        scale = lax.rsqrt(jnp.mean(x * x, axis=-1, keepdims=True) + 1e-05)
        rows = (x * scale * gain_ref[...]).astype(jnp.bfloat16)
        if start < half:
            a_ref[start : start + block, :] = rows
        else:
            b_ref[start - half : start - half + block, :] = rows


def prepare(x, gain):
    span, depth = x.shape
    vmem = pl.BlockSpec(memory_space=pltpu.VMEM)
    rows = jax.ShapeDtypeStruct((span // 2, depth), jnp.bfloat16)
    return pl.pallas_call(
        prepare_body,
        in_specs=[vmem] * 2,
        out_specs=[vmem] * 2,
        out_shape=[rows, rows],
        compiler_params=pltpu.CompilerParams(vmem_limit_bytes=12 * MIB),
        cost_estimate=SMALL,
        name="prepare",
    )(x, gain)


def share_body(lengths_ref, grads_ref, factor_ref, ids_ref, queries_ref, _, out_ref):
    count, width = queries_ref.shape[0], out_ref.shape[1]
    span, order = grads_ref.shape[0], factor_ref.shape[0]
    rows = span * LANES // width
    offset = pl.multiple_of(lax.axis_index("groups") * width, width)
    out_ref[:count, :] = queries_ref[:, pl.ds(offset, width)]
    right = lax.dot_general(grads_ref[...], factor_ref[...], NT, preferred_element_type=jnp.float32)
    live = lax.broadcasted_iota(jnp.int32, (span, order), 0) < lengths_ref[0]
    masked = jnp.where(live, right, 0.0)
    both = jnp.concatenate([masked, jnp.broadcast_to(ids_ref[...], (span, LANES - order))], axis=1)
    wide = jnp.concatenate([both[r : r + rows, :] for r in range(0, span, rows)], axis=1)
    out_ref[count : count + rows, :] = wide.astype(out_ref.dtype)
    if count + rows < out_ref.shape[0]:
        out_ref[count + rows :, :] = jnp.zeros((out_ref.shape[0] - count - rows, width), out_ref.dtype)


def own_share(lengths, grads, factor, ids, queries, after, groups):
    count, depth = queries.shape
    width = depth // groups
    span, order = grads.shape[0], factor.shape[0]
    rows = span * LANES // width
    ids = jnp.pad(ids.astype(jnp.float32)[None, :], ((0, 0), (0, LANES - order - count)))
    vmem = pl.BlockSpec(memory_space=pltpu.VMEM)
    return pl.pallas_call(
        share_body,
        in_specs=[pl.BlockSpec(memory_space=pltpu.SMEM)] + [vmem] * 4 + [pl.BlockSpec(memory_space=pl.ANY)],
        out_specs=vmem,
        out_shape=jax.ShapeDtypeStruct((-(-(count + rows) // 8) * 8, width), queries.dtype),
        compiler_params=pltpu.CompilerParams(vmem_limit_bytes=12 * MIB),
        cost_estimate=SMALL,
        name="own_share",
    )(lengths, grads, factor, ids, queries, after)


def gather_rows(x_refs, xn):
    rows = x_refs[0].shape[0]
    for k, ref in enumerate(x_refs):
        xn[k * rows : (k + 1) * rows, :] = ref[...]


def gated(gate, up):
    return (jax.nn.silu(gate) * up).astype(jnp.bfloat16)


def project(xn, gate_ref, up_ref, mix_ref, f_ref):
    order, units = f_ref.shape
    wide = 2 * LANES

    def product(w):
        return jnp.dot(xn[...], w, preferred_element_type=jnp.float32)

    def left_of(hidden, start, end):
        return lax.dot_general(hidden, f_ref[:, start:end], NT, preferred_element_type=jnp.float32)

    total = jnp.zeros((xn.shape[0], order), jnp.float32)
    hidden, start = None, 0
    for at in range(0, units, wide):
        if at + wide <= units:
            gate = product(gate_ref[:, at : at + wide])
            if hidden is not None:
                total += left_of(hidden, start, at)
            hidden = gated(gate, product(up_ref[:, at : at + wide]))
        else:
            both = product(mix_ref[...])
            if hidden is not None:
                total += left_of(hidden, start, at)
            hidden = gated(both[:, :LANES], both[:, LANES:])
        start = at
    return total + left_of(hidden, start, units)


def first_body(pieces, *refs):
    x_refs, (gate_hbm, up_hbm, f_ref, out_ref, gate_ref, up_ref, mix_ref, xn, sems) = refs[:pieces], refs[pieces:]
    depth, units = gate_ref.shape
    parts = sems.shape[1]
    copies = []
    for p in range(parts):
        rows = pl.ds(p * (depth // parts), depth // parts)
        copies.append(pltpu.make_async_copy(gate_hbm.at[rows], gate_ref.at[rows], sems.at[0, p]))
        copies.append(pltpu.make_async_copy(up_hbm.at[rows], up_ref.at[rows], sems.at[1, p]))
    for copy in copies:
        copy.start()
    gather_rows(x_refs, xn)
    for copy in copies:
        copy.wait()
    if units % (2 * LANES):
        mix_ref[:, :LANES] = gate_ref[:, units - LANES :]
        mix_ref[:, LANES:] = up_ref[:, units - LANES :]
    out_ref[...] = project(xn, gate_ref, up_ref, mix_ref, f_ref)


def first_chunk(xs, gate_weight, up_weight, in_factor, index, tokens):
    pieces = len(xs)
    rows, depth = xs[0].shape
    order, units = in_factor.shape
    total = pieces * rows
    vmem = pl.BlockSpec(memory_space=pltpu.VMEM)
    hbm = pl.BlockSpec(memory_space=pltpu.HBM)
    mix = 2 * LANES if units % (2 * LANES) else LANES
    left, *weights = pl.pallas_call(
        functools.partial(first_body, pieces),
        grid=(1,),
        in_specs=[vmem] * pieces + [hbm, hbm, vmem],
        out_specs=[pl.BlockSpec((total, order), lambda i: (index, 0)), vmem, vmem, vmem],
        out_shape=[
            jax.ShapeDtypeStruct((tokens, order), jnp.float32),
            pltpu.VMEM((depth, units), jnp.bfloat16),
            pltpu.VMEM((depth, units), jnp.bfloat16),
            pltpu.VMEM((depth if mix > LANES else 16, mix), jnp.bfloat16),
        ],
        scratch_shapes=[pltpu.VMEM((total, depth), jnp.bfloat16), pltpu.SemaphoreType.DMA((2, 4))],
        compiler_params=pltpu.CompilerParams(vmem_limit_bytes=12 * MIB),
        cost_estimate=SMALL,
        name="first_chunk",
    )(
        *xs,
        pltpu.with_memory_space_constraint(gate_weight, pltpu.HBM),
        pltpu.with_memory_space_constraint(up_weight, pltpu.HBM),
        in_factor,
    )
    return left, weights


def chunk_body(pieces, *refs):
    x_refs, (gate_ref, up_ref, mix_ref, f_ref, _, out_ref, _, _, _, xn) = refs[:pieces], refs[pieces:]
    gather_rows(x_refs, xn)
    out_ref[...] = project(xn, gate_ref, up_ref, mix_ref, f_ref)


def chunk(xs, weights, in_factor, left, index):
    pieces = len(xs)
    rows, depth = xs[0].shape
    order = in_factor.shape[0]
    total = pieces * rows
    vmem = pl.BlockSpec(memory_space=pltpu.VMEM)
    left, *weights = pl.pallas_call(
        functools.partial(chunk_body, pieces),
        grid=(1,),
        in_specs=[vmem] * (pieces + 4) + [pl.BlockSpec(memory_space=pl.ANY)],
        out_specs=[pl.BlockSpec((total, order), lambda i: (index, 0)), vmem, vmem, vmem],
        out_shape=[jax.ShapeDtypeStruct(left.shape, left.dtype)] + [pltpu.VMEM(w.shape, w.dtype) for w in weights],
        scratch_shapes=[pltpu.VMEM((total, depth), jnp.bfloat16)],
        input_output_aliases={pieces + 4: 0, pieces: 1, pieces + 1: 2, pieces + 2: 3},
        compiler_params=pltpu.CompilerParams(vmem_limit_bytes=12 * MIB),
        cost_estimate=SMALL,
        name="chunk",
    )(*xs, *[pltpu.with_memory_space_constraint(w, pltpu.VMEM) for w in weights], in_factor, left)
    return left, weights


def masked_of(wide, span, order):
    wide = wide.astype(jnp.float32)
    both = jnp.concatenate([wide[:, c : c + LANES] for c in range(0, wide.shape[1], LANES)], axis=0)
    return both[:, :order].astype(jnp.bfloat16)


def one_sketch(left_ref, masked, at, half):
    left = jnp.concatenate([left_ref[p * half : (p + 1) * half, :] for p in at], axis=0)
    high = left.astype(jnp.bfloat16)
    low = (left - high.astype(jnp.float32)).astype(jnp.bfloat16)
    return sum(lax.dot_general(part, masked, TN, preferred_element_type=jnp.float32) for part in (low, high))


def write_flat(flat, slot, sketch, twice):
    order = sketch.shape[0]
    twice[...] = jnp.concatenate([sketch, sketch], axis=1)
    lane = lax.broadcasted_iota(jnp.int32, (order // 2, 2 * order), 1)
    even = twice[pl.ds(0, order // 2, 2), :]
    odd = twice[pl.ds(1, order // 2, 2), :]
    flat[:, slot, :] = jnp.where(lane < order, even, odd)


def sketch_body(places, first, half, count, *refs):
    names, left_ref, side_hbm = refs[:3]
    flat, side_ref, twice, sems = refs[-4:]
    order = left_ref.shape[1]
    rows = 2 * half * LANES // side_ref.shape[2]
    copies = [
        pltpu.make_async_copy(side_hbm.at[names[first + r]], side_ref.at[r], sems.at[r]) for r in range(len(places))
    ]
    for copy in copies:
        copy.start()
    for copy in copies:
        copy.wait()
    for r, at in enumerate(places):
        masked = masked_of(side_ref[r, count : count + rows, :], 2 * half, order)
        write_flat(flat, first + r, one_sketch(left_ref, masked, at, half), twice)


def sketches(places, first, half, count, names, left, side, flat):
    order = left.shape[1]
    vmem = pl.BlockSpec(memory_space=pltpu.VMEM)
    operands = [names, left, pltpu.with_memory_space_constraint(side, pltpu.HBM)]
    in_specs = [pl.BlockSpec(memory_space=pltpu.SMEM), vmem, pl.BlockSpec(memory_space=pltpu.HBM)]
    aliases = {}
    if flat is not None:
        aliases = {3: 0}
        operands.append(flat)
        in_specs.append(vmem)
    return pl.pallas_call(
        functools.partial(sketch_body, places, first, half, count),
        in_specs=in_specs,
        out_specs=vmem,
        out_shape=jax.ShapeDtypeStruct((order // 2, names.shape[0], 2 * order), jnp.float32),
        scratch_shapes=[
            pltpu.VMEM((len(places), *side.shape[1:]), side.dtype),
            pltpu.VMEM((order, 2 * order), jnp.float32),
            pltpu.SemaphoreType.DMA((len(places),)),
        ],
        input_output_aliases=aliases,
        compiler_params=pltpu.CompilerParams(vmem_limit_bytes=12 * MIB),
        cost_estimate=SMALL,
        name="sketches",
    )(*operands)


def finish_body(places, half, groups, count, names, left_ref, flat_ref, ids_ref, *refs):
    shares_hbm, (out_ref, share_ref, twice, flat, sems) = refs[:groups], refs[groups:]
    devices, width = share_ref.shape[1], share_ref.shape[3]
    order = left_ref.shape[1]
    rows = 2 * half * LANES // width
    parts = sems.shape[1]
    copies = []
    for r, ref in enumerate(shares_hbm):
        for p in range(parts):
            some = pl.ds(p * (devices // parts), devices // parts)
            copies.append(pltpu.make_async_copy(ref.at[some], share_ref.at[r, some], sems.at[r, p]))
    for copy in copies:
        copy.start()
    flat[...] = flat_ref[...]
    value = lax.broadcasted_iota(jnp.int32, (NVAL, ids_ref.shape[1]), 0)
    members = (value == ids_ref[...]).astype(jnp.bfloat16)
    for copy in copies:
        copy.wait()
    first = names.shape[0] - len(places)
    for r, at in enumerate(places):
        masked = masked_of(share_ref[0, names[first + r], count : count + rows, :], 2 * half, order)
        write_flat(flat, first + r, one_sketch(left_ref, masked, at, half), twice)
    group = lax.axis_index("groups")
    scores = 0.0
    for r in range(groups):
        block = lax.rem(group + r, groups) * (width // LANES)
        sketch = jnp.concatenate([flat[block + c] for c in range(width // LANES)], axis=1).astype(jnp.bfloat16)
        queries = share_ref[r, :, :count, :].reshape(devices * count, width)
        scores += lax.dot_general(sketch, queries, NT, preferred_element_type=jnp.float32)
    total = 0.0
    for _ in range(3):
        part = scores.astype(jnp.bfloat16)
        scores = scores - part.astype(jnp.float32)
        total += lax.dot_general(part, members, NT, preferred_element_type=jnp.float32)
    for r in range(names.shape[0]):
        out_ref[pl.ds(names[r], 1), :] = total[r : r + 1, :]


def finish(places, half, count, names, left, flat, shares, ids):
    order = left.shape[1]
    vmem = pl.BlockSpec(memory_space=pltpu.VMEM)
    hbm = pl.BlockSpec(memory_space=pltpu.HBM)
    return pl.pallas_call(
        functools.partial(finish_body, places, half, len(shares), count),
        in_specs=[pl.BlockSpec(memory_space=pltpu.SMEM)] + [vmem] * 3 + [hbm] + [pl.BlockSpec(memory_space=pl.ANY)] * (len(shares) - 1),
        out_specs=vmem,
        out_shape=jax.ShapeDtypeStruct((names.shape[0], NVAL), jnp.float32),
        scratch_shapes=[
            pltpu.VMEM((len(shares), *shares[0].shape), shares[0].dtype),
            pltpu.VMEM((order, 2 * order), jnp.float32),
            pltpu.VMEM(flat.shape, jnp.float32),
            pltpu.SemaphoreType.DMA((len(shares), 4)),
        ],
        compiler_params=pltpu.CompilerParams(vmem_limit_bytes=20 * MIB),
        cost_estimate=SMALL,
        name="finish",
    )(names, left, flat, ids, pltpu.with_memory_space_constraint(shares[0], pltpu.HBM), *shares[1:])


def arrivals(ring, devices):
    chips = len(ring)
    far = chips // 2
    table, spots = [[] for _ in range(devices)], []
    for distance in range(far + 1):
        for sign, piece in [(1, 0)] if distance in (0, far) else [(-1, 0), (1, 1)]:
            for me in range(devices):
                chip = ring[(ring.index(me // 2) + sign * distance) % chips]
                table[me] += [2 * chip + me % 2, 2 * chip + 1 - me % 2]
            if distance == 0:
                halves = [(0, 0), (0, 1)]
            elif distance == far:
                halves = [(chips - 1, 0), (chips - 1, 1)]
            else:
                halves = [(2 * distance - 1, piece), (2 * distance, piece)]
            spots.append([4 * k + 2 + p for k, p in halves])
            spots.append([4 * k + 4 + p for k, p in halves])
    return table, spots


def local(
    devices,
    groups,
    layer_inputs,
    example_lengths,
    norm_gain,
    gate_weight,
    up_weight,
    in_factor,
    out_factor,
    out_grads,
    queries,
    query_ids,
):
    chips = devices // 2
    ring = chip_ring(chips)
    me = lax.axis_index("examples")

    forward = [(ring[r] * 2 + c, ring[(r + 1) % chips] * 2 + c) for r in range(chips) for c in range(2)]
    backward = [(b, a) for a, b in forward]
    other_core = [(d, d ^ 1) for d in range(devices)]

    span, depth = layer_inputs.shape
    half = span // 2
    order = in_factor.shape[1]
    units = gate_weight.shape[1]
    short = -units % LANES
    if short:
        gate_weight = jnp.pad(gate_weight, ((0, 0), (0, short)))
        up_weight = jnp.pad(up_weight, ((0, 0), (0, short)))
        in_factor = jnp.pad(in_factor, ((0, short), (0, 0)))
    tokens = 2 * span * chips + span

    def send(x, way):
        return lax.ppermute(x, "examples", way)

    x_a, x_b = prepare(layer_inputs, norm_gain[None, :])
    coming = {
        1: (send(x_a, forward), send(x_a, backward)),
        2: (send(x_b, forward), send(x_b, backward)),
    }
    swapped = tuple(send(x, other_core) for x in (x_a, x_b))
    left, weights = first_chunk((x_a, x_b), gate_weight, up_weight, in_factor.T, 1, tokens)
    nq = queries.shape[0]
    side = own_share(example_lengths, out_grads, out_factor.T, query_ids, queries, left, groups)
    side, left = lax.optimization_barrier((side, left))
    side = lax.all_gather(side, "examples", axis=0)

    names, spots = arrivals(ring, devices)
    names = lax.dynamic_index_in_dim(jnp.array(names, jnp.int32), me, keepdims=False)

    for k in range(1, chips):
        own_1, own_2, left = lax.optimization_barrier((*coming.pop(k), left))
        own = (own_1, own_2)
        if k + 2 < chips - 1:
            coming[k + 2] = (send(own_1, forward), send(own_2, backward))
        elif k + 2 == chips - 1:
            opposite = send(own_1, forward)
        elif k + 1 == chips - 1:
            coming[chips - 1] = (opposite, send(own_2, backward))
        before, swapped = swapped, tuple(send(x, other_core) for x in own)
        if k < chips - 1:
            left, weights = chunk(before + own, weights, in_factor.T, left, k)
        if k == chips - 3:
            side, left = lax.optimization_barrier((side, left))
            ids = side[:, nq, order : order + nq].astype(jnp.int32).reshape(1, devices * nq)
            shares = [side]
            for r in range(1, groups):
                way = [((g + r) % groups, g) for g in range(groups)]
                shares.append(lax.ppermute(side, "groups", way))
            ready = devices - 6
            flat = sketches(spots[:ready], 0, half, nq, names, left, side, None)
            flat, ids, left = lax.optimization_barrier((flat, ids, left))
        if k == chips - 2:
            left, weights = chunk(swapped, weights, in_factor.T, left, 2 * k + 2)
            flat = sketches(spots[ready:-2], ready, half, nq, names, left, side, flat)
            flat, left = lax.optimization_barrier((flat, left))
    left, weights = chunk(own, weights, in_factor.T, left, 2 * chips - 1)
    left, weights = chunk(swapped, weights, in_factor.T, left, 2 * chips)

    partial = finish(spots[-2:], half, nq, names, left, flat, shares, ids)
    shares = lax.all_to_all(partial, "examples", split_axis=0, concat_axis=0, tiled=True)
    return jnp.sum(shares, axis=0, keepdims=True)


def solution(mesh):
    return jax.shard_map(
        functools.partial(local, mesh.shape["examples"], mesh.shape["groups"]),
        mesh=mesh,
        in_specs=(
            P(("groups", "examples"), None),
            P(("groups", "examples")),
            P(),
            P(None, "examples"),
            P(None, "examples"),
            P("examples", None),
            P(),
            P(("groups", "examples"), None),
            P("examples", None),
            P("examples"),
        ),
        out_specs=P(("groups", "examples"), None),
        check_vma=False,
    )
```

```python
import functools

import jax
import jax.numpy as jnp
from jax import lax
from jax.experimental import pallas as pl
from jax.experimental.pallas import tpu as pltpu
from jax.sharding import PartitionSpec as P

NVAL = 256
LANES = 128
MIB = 1024 * 1024
NT = (((1,), (1,)), ((), ()))
TN = (((0,), (0,)), ((), ()))
SMALL = pl.CostEstimate(flops=1_000_000, bytes_accessed=100_000, transcendentals=0)


def chip_ring(chips):
    if chips == 8:
        return [0, 2, 4, 6, 7, 5, 3, 1]
    return list(range(chips))


def prepare_body(lengths_ref, ids_ref, x_hbm, gain_hbm, grads_hbm, factor_hbm, queries_hbm, *refs):
    a_ref, b_ref, out_ref, x_ref, gain_ref, grads_ref, factor_ref, queries_ref, sems = refs
    half, span = a_ref.shape[0], x_ref.shape[0]
    block = 32
    starts = range(0, span, block)
    x_copies = []
    for k, start in enumerate(starts):
        some = pl.ds(start, block)
        x_copies.append(pltpu.make_async_copy(x_hbm.at[some], x_ref.at[some], sems.at[k]))
    copies = []
    pairs = [(gain_hbm, gain_ref), (grads_hbm, grads_ref), (factor_hbm, factor_ref), (queries_hbm, queries_ref)]
    for k, (source, target) in enumerate(pairs):
        copies.append(pltpu.make_async_copy(source, target, sems.at[len(x_copies) + k]))
    copies[0].start()
    for copy in x_copies + copies[1:]:
        copy.start()
    copies[0].wait()
    for start, copy in zip(starts, x_copies):
        copy.wait()
        for at in range(start, start + block, 16):
            x = x_ref[at : at + 16, :].astype(jnp.float32)
            scale = lax.rsqrt(jnp.mean(x * x, axis=-1, keepdims=True) + 1e-05)
            rows = (x * scale * gain_ref[...]).astype(jnp.bfloat16)
            if at < half:
                a_ref[at : at + 16, :] = rows
            else:
                b_ref[at - half : at - half + 16, :] = rows
    for copy in copies[1:]:
        copy.wait()

    count, width = queries_ref.shape[0], out_ref.shape[1]
    order = factor_ref.shape[0]
    rows = span * LANES // width
    offset = pl.multiple_of(lax.axis_index("groups") * width, width)
    out_ref[:count, :] = queries_ref[:, pl.ds(offset, width)]
    right = lax.dot_general(grads_ref[...], factor_ref[...], NT, preferred_element_type=jnp.float32)
    live = lax.broadcasted_iota(jnp.int32, (span, order), 0) < lengths_ref[0]
    masked = jnp.where(live, right, 0.0)
    ids = jnp.concatenate([ids_ref[...], jnp.zeros((1, LANES - order - count), jnp.int32)], axis=1)
    ids = jnp.broadcast_to(ids.astype(jnp.float32), (span, LANES - order))
    both = jnp.concatenate([masked, ids], axis=1)
    wide = jnp.concatenate([both[r : r + rows, :] for r in range(0, span, rows)], axis=1)
    out_ref[count : count + rows, :] = wide.astype(out_ref.dtype)
    if count + rows < out_ref.shape[0]:
        out_ref[count + rows :, :] = jnp.zeros((out_ref.shape[0] - count - rows, width), out_ref.dtype)


def prepare(x, gain, lengths, grads, factor, ids, queries, groups):
    span, depth = x.shape
    count = queries.shape[0]
    width = depth // groups
    vmem = pl.BlockSpec(memory_space=pltpu.VMEM)
    hbm = pl.BlockSpec(memory_space=pltpu.HBM)
    rows = jax.ShapeDtypeStruct((span // 2, depth), jnp.bfloat16)
    share = -(-(count + span * LANES // width) // 8) * 8
    operands = [x, gain, grads, factor, queries]
    return pl.pallas_call(
        prepare_body,
        in_specs=[pl.BlockSpec(memory_space=pltpu.SMEM), vmem] + [hbm] * len(operands),
        out_specs=[vmem] * 3,
        out_shape=[rows, rows, jax.ShapeDtypeStruct((share, width), queries.dtype)],
        scratch_shapes=[pltpu.VMEM(o.shape, o.dtype) for o in operands]
        + [pltpu.SemaphoreType.DMA((span // 32 + len(operands) - 1,))],
        compiler_params=pltpu.CompilerParams(vmem_limit_bytes=12 * MIB),
        cost_estimate=SMALL,
        name="prepare",
    )(lengths, ids, *[pltpu.with_memory_space_constraint(o, pltpu.HBM) for o in operands])


def gather_rows(x_refs, xn):
    rows = x_refs[0].shape[0]
    for k, ref in enumerate(x_refs):
        xn[k * rows : (k + 1) * rows, :] = ref[...]


def gated(gate, up):
    return (jax.nn.silu(gate) * up).astype(jnp.bfloat16)


def project(xn, gate_ref, up_ref, f_ref):
    order, units = f_ref.shape
    wide = 2 * LANES

    def product(w):
        return jnp.dot(xn[...], w, preferred_element_type=jnp.float32)

    def left_of(hidden, start, end):
        return lax.dot_general(hidden, f_ref[:, start:end], NT, preferred_element_type=jnp.float32)

    total = jnp.zeros((xn.shape[0], order), jnp.float32)
    hidden, start = None, 0
    for at in range(0, units, wide):
        both = product(gate_ref[:, at : at + wide])
        if hidden is not None:
            total += left_of(hidden, start, at)
        if at + wide <= units:
            hidden = gated(both, product(up_ref[:, at : at + wide]))
        else:
            hidden = gated(both[:, :LANES], both[:, LANES:])
        start = at
    return total + left_of(hidden, start, units)


def first_body(pieces, *refs):
    x_refs, (gate_hbm, up_hbm, f_ref, out_ref, gate_ref, up_ref, xn, sems) = refs[:pieces], refs[pieces:]
    depth, units = gate_hbm.shape
    even = up_ref.shape[1]
    parts = sems.shape[1]
    copies = []
    for p in range(parts):
        rows = pl.ds(p * (depth // parts), depth // parts)
        moves = [
            (gate_hbm.at[rows], gate_ref.at[rows, pl.ds(0, units)]),
            (up_hbm.at[rows, pl.ds(0, even)], up_ref.at[rows]),
        ]
        if even < units:
            moves.append((up_hbm.at[rows, pl.ds(even, LANES)], gate_ref.at[rows, pl.ds(units, LANES)]))
        for k, (source, target) in enumerate(moves):
            copies.append(pltpu.make_async_copy(source, target, sems.at[k, p]))
    for copy in copies:
        copy.start()
    gather_rows(x_refs, xn)
    for copy in copies:
        copy.wait()
    out_ref[...] = project(xn, gate_ref, up_ref, f_ref)


def first_chunk(xs, gate_weight, up_weight, in_factor, index, tokens):
    pieces = len(xs)
    rows, depth = xs[0].shape
    order, units = in_factor.shape
    total = pieces * rows
    vmem = pl.BlockSpec(memory_space=pltpu.VMEM)
    hbm = pl.BlockSpec(memory_space=pltpu.HBM)
    rest = units % (2 * LANES)
    left, *weights = pl.pallas_call(
        functools.partial(first_body, pieces),
        grid=(1,),
        in_specs=[vmem] * pieces + [hbm, hbm, vmem],
        out_specs=[pl.BlockSpec((total, order), lambda i: (index, 0)), vmem, vmem],
        out_shape=[
            jax.ShapeDtypeStruct((tokens, order), jnp.float32),
            pltpu.VMEM((depth, units + rest), jnp.bfloat16),
            pltpu.VMEM((depth, units - rest), jnp.bfloat16),
        ],
        scratch_shapes=[pltpu.VMEM((total, depth), jnp.bfloat16), pltpu.SemaphoreType.DMA((3, 4))],
        compiler_params=pltpu.CompilerParams(vmem_limit_bytes=12 * MIB),
        cost_estimate=SMALL,
        name="first_chunk",
    )(
        *xs,
        pltpu.with_memory_space_constraint(gate_weight, pltpu.HBM),
        pltpu.with_memory_space_constraint(up_weight, pltpu.HBM),
        in_factor,
    )
    return left, weights


def chunk_body(pieces, *refs):
    x_refs, (gate_ref, up_ref, f_ref, _, out_ref, _, _, xn) = refs[:pieces], refs[pieces:]
    gather_rows(x_refs, xn)
    out_ref[...] = project(xn, gate_ref, up_ref, f_ref)


def chunk(xs, weights, in_factor, left, index):
    pieces = len(xs)
    rows, depth = xs[0].shape
    order = in_factor.shape[0]
    total = pieces * rows
    vmem = pl.BlockSpec(memory_space=pltpu.VMEM)
    left, *weights = pl.pallas_call(
        functools.partial(chunk_body, pieces),
        grid=(1,),
        in_specs=[vmem] * (pieces + 3) + [pl.BlockSpec(memory_space=pl.ANY)],
        out_specs=[pl.BlockSpec((total, order), lambda i: (index, 0)), vmem, vmem],
        out_shape=[jax.ShapeDtypeStruct(left.shape, left.dtype)] + [pltpu.VMEM(w.shape, w.dtype) for w in weights],
        scratch_shapes=[pltpu.VMEM((total, depth), jnp.bfloat16)],
        input_output_aliases={pieces + 3: 0, pieces: 1, pieces + 1: 2},
        compiler_params=pltpu.CompilerParams(vmem_limit_bytes=12 * MIB),
        cost_estimate=SMALL,
        name="chunk",
    )(*xs, *[pltpu.with_memory_space_constraint(w, pltpu.VMEM) for w in weights], in_factor, left)
    return left, weights


def masked_of(wide, span, order):
    wide = wide.astype(jnp.float32)
    both = jnp.concatenate([wide[:, c : c + LANES] for c in range(0, wide.shape[1], LANES)], axis=0)
    return both[:, :order].astype(jnp.bfloat16)


def one_sketch(left_ref, masked, at, half):
    left = jnp.concatenate([left_ref[p * half : (p + 1) * half, :] for p in at], axis=0)
    high = left.astype(jnp.bfloat16)
    low = (left - high.astype(jnp.float32)).astype(jnp.bfloat16)
    return sum(lax.dot_general(part, masked, TN, preferred_element_type=jnp.float32) for part in (low, high))


def write_flat(flat, slot, sketch, twice):
    order = sketch.shape[0]
    twice[...] = jnp.concatenate([sketch, sketch], axis=1)
    lane = lax.broadcasted_iota(jnp.int32, (order // 2, 2 * order), 1)
    even = twice[pl.ds(0, order // 2, 2), :]
    odd = twice[pl.ds(1, order // 2, 2), :]
    flat[:, slot, :] = jnp.where(lane < order, even, odd)


def sketch_body(places, first, half, count, *refs):
    names, left_ref, side_hbm = refs[:3]
    flat, side_ref, twice, sems = refs[-4:]
    order = left_ref.shape[1]
    rows = 2 * half * LANES // side_ref.shape[2]
    copies = [
        pltpu.make_async_copy(side_hbm.at[names[first + r]], side_ref.at[r], sems.at[r]) for r in range(len(places))
    ]
    for copy in copies:
        copy.start()
    for copy in copies:
        copy.wait()
    for r, at in enumerate(places):
        masked = masked_of(side_ref[r, count : count + rows, :], 2 * half, order)
        write_flat(flat, first + r, one_sketch(left_ref, masked, at, half), twice)


def sketches(places, first, half, count, names, left, side, flat):
    order = left.shape[1]
    vmem = pl.BlockSpec(memory_space=pltpu.VMEM)
    operands = [names, left, pltpu.with_memory_space_constraint(side, pltpu.HBM)]
    in_specs = [pl.BlockSpec(memory_space=pltpu.SMEM), vmem, pl.BlockSpec(memory_space=pltpu.HBM)]
    aliases = {}
    if flat is not None:
        aliases = {3: 0}
        operands.append(flat)
        in_specs.append(vmem)
    return pl.pallas_call(
        functools.partial(sketch_body, places, first, half, count),
        in_specs=in_specs,
        out_specs=vmem,
        out_shape=jax.ShapeDtypeStruct((order // 2, names.shape[0], 2 * order), jnp.float32),
        scratch_shapes=[
            pltpu.VMEM((len(places), *side.shape[1:]), side.dtype),
            pltpu.VMEM((order, 2 * order), jnp.float32),
            pltpu.SemaphoreType.DMA((len(places),)),
        ],
        input_output_aliases=aliases,
        compiler_params=pltpu.CompilerParams(vmem_limit_bytes=12 * MIB),
        cost_estimate=SMALL,
        name="sketches",
    )(*operands)


def finish_body(places, half, groups, count, names, left_ref, flat_ref, ids_ref, *refs):
    shares_hbm, (out_ref, share_ref, twice, flat, sems) = refs[:groups], refs[groups:]
    devices, width = share_ref.shape[1], share_ref.shape[3]
    order = left_ref.shape[1]
    rows = 2 * half * LANES // width
    parts = sems.shape[1]
    copies = []
    for r, ref in enumerate(shares_hbm):
        for p in range(parts):
            some = pl.ds(p * (devices // parts), devices // parts)
            copies.append(pltpu.make_async_copy(ref.at[some], share_ref.at[r, some], sems.at[r, p]))
    for copy in copies:
        copy.start()
    flat[...] = flat_ref[...]
    value = lax.broadcasted_iota(jnp.int32, (NVAL, ids_ref.shape[1]), 0)
    members = (value == ids_ref[...]).astype(jnp.bfloat16)
    for copy in copies:
        copy.wait()
    first = names.shape[0] - len(places)
    for r, at in enumerate(places):
        masked = masked_of(share_ref[0, names[first + r], count : count + rows, :], 2 * half, order)
        write_flat(flat, first + r, one_sketch(left_ref, masked, at, half), twice)
    group = lax.axis_index("groups")
    scores = 0.0
    for r in range(groups):
        block = lax.rem(group + r, groups) * (width // LANES)
        sketch = jnp.concatenate([flat[block + c] for c in range(width // LANES)], axis=1).astype(jnp.bfloat16)
        queries = share_ref[r, :, :count, :].reshape(devices * count, width)
        scores += lax.dot_general(sketch, queries, NT, preferred_element_type=jnp.float32)
    total = 0.0
    for _ in range(3):
        part = scores.astype(jnp.bfloat16)
        scores = scores - part.astype(jnp.float32)
        total += lax.dot_general(part, members, NT, preferred_element_type=jnp.float32)
    for r in range(names.shape[0]):
        out_ref[pl.ds(names[r], 1), :] = total[r : r + 1, :]


def finish(places, half, count, names, left, flat, shares, ids):
    order = left.shape[1]
    vmem = pl.BlockSpec(memory_space=pltpu.VMEM)
    hbm = pl.BlockSpec(memory_space=pltpu.HBM)
    return pl.pallas_call(
        functools.partial(finish_body, places, half, len(shares), count),
        in_specs=[pl.BlockSpec(memory_space=pltpu.SMEM)] + [vmem] * 3 + [hbm] + [pl.BlockSpec(memory_space=pl.ANY)] * (len(shares) - 1),
        out_specs=vmem,
        out_shape=jax.ShapeDtypeStruct((names.shape[0], NVAL), jnp.float32),
        scratch_shapes=[
            pltpu.VMEM((len(shares), *shares[0].shape), shares[0].dtype),
            pltpu.VMEM((order, 2 * order), jnp.float32),
            pltpu.VMEM(flat.shape, jnp.float32),
            pltpu.SemaphoreType.DMA((len(shares), 4)),
        ],
        compiler_params=pltpu.CompilerParams(vmem_limit_bytes=20 * MIB),
        cost_estimate=SMALL,
        name="finish",
    )(names, left, flat, ids, pltpu.with_memory_space_constraint(shares[0], pltpu.HBM), *shares[1:])


def arrivals(ring, devices):
    chips = len(ring)
    far = chips // 2
    table, spots = [[] for _ in range(devices)], []
    for distance in range(far + 1):
        for sign, piece in [(1, 0)] if distance in (0, far) else [(-1, 0), (1, 1)]:
            for me in range(devices):
                chip = ring[(ring.index(me // 2) + sign * distance) % chips]
                table[me] += [2 * chip + me % 2, 2 * chip + 1 - me % 2]
            if distance == 0:
                halves = [(0, 0), (0, 1)]
            elif distance == far:
                halves = [(chips - 1, 0), (chips - 1, 1)]
            else:
                halves = [(2 * distance - 1, piece), (2 * distance, piece)]
            spots.append([4 * k + 2 + p for k, p in halves])
            spots.append([4 * k + 4 + p for k, p in halves])
    return table, spots


def local(
    devices,
    groups,
    layer_inputs,
    example_lengths,
    norm_gain,
    gate_weight,
    up_weight,
    in_factor,
    out_factor,
    out_grads,
    queries,
    query_ids,
):
    chips = devices // 2
    ring = chip_ring(chips)
    me = lax.axis_index("examples")

    forward = [(ring[r] * 2 + c, ring[(r + 1) % chips] * 2 + c) for r in range(chips) for c in range(2)]
    backward = [(b, a) for a, b in forward]
    other_core = [(d, d ^ 1) for d in range(devices)]

    span, depth = layer_inputs.shape
    half = span // 2
    order = in_factor.shape[1]
    units = gate_weight.shape[1]
    short = -units % LANES
    if short:
        gate_weight = jnp.pad(gate_weight, ((0, 0), (0, short)))
        up_weight = jnp.pad(up_weight, ((0, 0), (0, short)))
        in_factor = jnp.pad(in_factor, ((0, short), (0, 0)))
    tokens = 2 * span * chips + span

    def send(x, way):
        return lax.ppermute(x, "examples", way)

    nq = queries.shape[0]
    x_a, x_b, side = prepare(
        layer_inputs,
        norm_gain[None, :],
        example_lengths,
        out_grads,
        out_factor.T,
        query_ids[None, :],
        queries,
        groups,
    )
    side = lax.all_gather(side, "examples", axis=0)
    coming = {
        1: (send(x_a, forward), send(x_a, backward)),
        2: (send(x_b, forward), send(x_b, backward)),
    }
    swapped = tuple(send(x, other_core) for x in (x_a, x_b))
    left, weights = first_chunk((x_a, x_b), gate_weight, up_weight, in_factor.T, 1, tokens)

    names, spots = arrivals(ring, devices)
    names = lax.dynamic_index_in_dim(jnp.array(names, jnp.int32), me, keepdims=False)

    for k in range(1, chips):
        own_1, own_2, left = lax.optimization_barrier((*coming.pop(k), left))
        own = (own_1, own_2)
        if k + 2 < chips - 1:
            coming[k + 2] = (send(own_1, forward), send(own_2, backward))
        elif k + 2 == chips - 1:
            opposite = send(own_1, forward)
        elif k + 1 == chips - 1:
            coming[chips - 1] = (opposite, send(own_2, backward))
        before, swapped = swapped, tuple(send(x, other_core) for x in own)
        if k < chips - 1:
            left, weights = chunk(before + own, weights, in_factor.T, left, k)
        if k == chips - 4:
            side, left = lax.optimization_barrier((side, left))
            ids = side[:, nq, order : order + nq].astype(jnp.int32).reshape(1, devices * nq)
            ids, left = lax.optimization_barrier((ids, left))
            shares = [side]
            for r in range(1, groups):
                way = [((g + r) % groups, g) for g in range(groups)]
                shares.append(lax.ppermute(side, "groups", way))
        if k == chips - 3:
            ready = devices - 6
            flat = sketches(spots[:ready], 0, half, nq, names, left, side, None)
            flat, left = lax.optimization_barrier((flat, left))
        if k == chips - 2:
            left, weights = chunk(swapped, weights, in_factor.T, left, 2 * k + 2)
            flat = sketches(spots[ready:-2], ready, half, nq, names, left, side, flat)
            flat, left = lax.optimization_barrier((flat, left))
    left, weights = chunk(own, weights, in_factor.T, left, 2 * chips - 1)
    left, weights = chunk(swapped, weights, in_factor.T, left, 2 * chips)

    partial = finish(spots[-2:], half, nq, names, left, flat, shares, ids)
    shares = lax.all_to_all(partial, "examples", split_axis=0, concat_axis=0, tiled=True)
    return jnp.sum(shares, axis=0, keepdims=True)


def solution(mesh):
    return jax.shard_map(
        functools.partial(local, mesh.shape["examples"], mesh.shape["groups"]),
        mesh=mesh,
        in_specs=(
            P(("groups", "examples"), None),
            P(("groups", "examples")),
            P(),
            P(None, "examples"),
            P(None, "examples"),
            P("examples", None),
            P(),
            P(("groups", "examples"), None),
            P("examples", None),
            P("examples"),
        ),
        out_specs=P(("groups", "examples"), None),
        check_vma=False,
    )
```

```python
import functools

import jax
import jax.numpy as jnp
from jax import lax
from jax.experimental import pallas as pl
from jax.experimental.pallas import tpu as pltpu
from jax.sharding import PartitionSpec as P

NVAL = 256
LANES = 128
MIB = 1024 * 1024
NT = (((1,), (1,)), ((), ()))
TN = (((0,), (0,)), ((), ()))
SMALL = pl.CostEstimate(flops=1_000_000, bytes_accessed=100_000, transcendentals=0)


def chip_ring(chips):
    if chips == 8:
        return [0, 2, 4, 6, 7, 5, 3, 1]
    return list(range(chips))


def prepare_body(lengths_ref, ids_ref, x_hbm, gain_hbm, grads_hbm, factor_hbm, queries_hbm, *refs):
    a_ref, b_ref, out_ref, x_ref, gain_ref, grads_ref, factor_ref, queries_ref, sems = refs
    half, span = a_ref.shape[0], x_ref.shape[0]
    block = 32
    starts = range(0, span, block)
    x_copies = []
    for k, start in enumerate(starts):
        some = pl.ds(start, block)
        x_copies.append(pltpu.make_async_copy(x_hbm.at[some], x_ref.at[some], sems.at[k]))
    copies = []
    pairs = [(gain_hbm, gain_ref), (grads_hbm, grads_ref), (factor_hbm, factor_ref), (queries_hbm, queries_ref)]
    for k, (source, target) in enumerate(pairs):
        copies.append(pltpu.make_async_copy(source, target, sems.at[len(x_copies) + k]))
    copies[0].start()
    for copy in x_copies + copies[1:]:
        copy.start()
    copies[0].wait()
    for start, copy in zip(starts, x_copies):
        copy.wait()
        for at in range(start, start + block, 16):
            x = x_ref[at : at + 16, :].astype(jnp.float32)
            scale = lax.rsqrt(jnp.mean(x * x, axis=-1, keepdims=True) + 1e-05)
            rows = (x * scale * gain_ref[...]).astype(jnp.bfloat16)
            if at < half:
                a_ref[at : at + 16, :] = rows
            else:
                b_ref[at - half : at - half + 16, :] = rows
    for copy in copies[1:]:
        copy.wait()

    count, width = queries_ref.shape[0], out_ref.shape[1]
    order = factor_ref.shape[0]
    rows = span * LANES // width
    offset = pl.multiple_of(lax.axis_index("groups") * width, width)
    out_ref[:count, :] = queries_ref[:, pl.ds(offset, width)]
    right = lax.dot_general(grads_ref[...], factor_ref[...], NT, preferred_element_type=jnp.float32)
    live = lax.broadcasted_iota(jnp.int32, (span, order), 0) < lengths_ref[0]
    masked = jnp.where(live, right, 0.0)
    ids = jnp.concatenate([ids_ref[...], jnp.zeros((1, LANES - order - count), jnp.int32)], axis=1)
    ids = jnp.broadcast_to(ids.astype(jnp.float32), (span, LANES - order))
    both = jnp.concatenate([masked, ids], axis=1)
    wide = jnp.concatenate([both[r : r + rows, :] for r in range(0, span, rows)], axis=1)
    out_ref[count : count + rows, :] = wide.astype(out_ref.dtype)
    if count + rows < out_ref.shape[0]:
        out_ref[count + rows :, :] = jnp.zeros((out_ref.shape[0] - count - rows, width), out_ref.dtype)


def prepare(x, gain, lengths, grads, factor, ids, queries, groups):
    span, depth = x.shape
    count = queries.shape[0]
    width = depth // groups
    vmem = pl.BlockSpec(memory_space=pltpu.VMEM)
    hbm = pl.BlockSpec(memory_space=pltpu.HBM)
    rows = jax.ShapeDtypeStruct((span // 2, depth), jnp.bfloat16)
    share = -(-(count + span * LANES // width) // 8) * 8
    operands = [x, gain, grads, factor, queries]
    return pl.pallas_call(
        prepare_body,
        in_specs=[pl.BlockSpec(memory_space=pltpu.SMEM), vmem] + [hbm] * len(operands),
        out_specs=[vmem] * 3,
        out_shape=[rows, rows, jax.ShapeDtypeStruct((share, width), queries.dtype)],
        scratch_shapes=[pltpu.VMEM(o.shape, o.dtype) for o in operands]
        + [pltpu.SemaphoreType.DMA((span // 32 + len(operands) - 1,))],
        compiler_params=pltpu.CompilerParams(vmem_limit_bytes=12 * MIB),
        cost_estimate=SMALL,
        name="prepare",
    )(lengths, ids, *[pltpu.with_memory_space_constraint(o, pltpu.HBM) for o in operands])


def gather_rows(x_refs, xn):
    rows = x_refs[0].shape[0]
    for k, ref in enumerate(x_refs):
        xn[k * rows : (k + 1) * rows, :] = ref[...]


def gated(gate, up):
    return (jax.nn.silu(gate) * up).astype(jnp.bfloat16)


def project(xn, gate_ref, up_ref, f_ref):
    order, units = f_ref.shape
    wide = 2 * LANES

    def product(w):
        return jnp.dot(xn[...], w, preferred_element_type=jnp.float32)

    def left_of(hidden, start, end):
        return lax.dot_general(hidden, f_ref[:, start:end], NT, preferred_element_type=jnp.float32)

    total = jnp.zeros((xn.shape[0], order), jnp.float32)
    hidden, start = None, 0
    for at in range(0, units, wide):
        both = product(gate_ref[:, at : at + wide])
        if hidden is not None:
            total += left_of(hidden, start, at)
        if at + wide <= units:
            hidden = gated(both, product(up_ref[:, at : at + wide]))
        else:
            hidden = gated(both[:, :LANES], both[:, LANES:])
        start = at
    return total + left_of(hidden, start, units)


def first_body(pieces, *refs):
    x_refs, (gate_hbm, up_hbm, f_ref, out_ref, gate_ref, up_ref, xn, sems) = refs[:pieces], refs[pieces:]
    depth, units = gate_hbm.shape
    even = up_ref.shape[1]
    parts = sems.shape[1]
    copies = []
    for p in range(parts):
        rows = pl.ds(p * (depth // parts), depth // parts)
        moves = [
            (gate_hbm.at[rows], gate_ref.at[rows, pl.ds(0, units)]),
            (up_hbm.at[rows, pl.ds(0, even)], up_ref.at[rows]),
        ]
        if even < units:
            moves.append((up_hbm.at[rows, pl.ds(even, LANES)], gate_ref.at[rows, pl.ds(units, LANES)]))
        for k, (source, target) in enumerate(moves):
            copies.append(pltpu.make_async_copy(source, target, sems.at[k, p]))
    for copy in copies:
        copy.start()
    gather_rows(x_refs, xn)
    for copy in copies:
        copy.wait()
    out_ref[...] = project(xn, gate_ref, up_ref, f_ref)


def first_chunk(xs, gate_weight, up_weight, in_factor, index, tokens):
    pieces = len(xs)
    rows, depth = xs[0].shape
    order, units = in_factor.shape
    total = pieces * rows
    vmem = pl.BlockSpec(memory_space=pltpu.VMEM)
    hbm = pl.BlockSpec(memory_space=pltpu.HBM)
    rest = units % (2 * LANES)
    left, *weights = pl.pallas_call(
        functools.partial(first_body, pieces),
        grid=(1,),
        in_specs=[vmem] * pieces + [hbm, hbm, vmem],
        out_specs=[pl.BlockSpec((total, order), lambda i: (index, 0)), vmem, vmem],
        out_shape=[
            jax.ShapeDtypeStruct((tokens, order), jnp.float32),
            pltpu.VMEM((depth, units + rest), jnp.bfloat16),
            pltpu.VMEM((depth, units - rest), jnp.bfloat16),
        ],
        scratch_shapes=[pltpu.VMEM((total, depth), jnp.bfloat16), pltpu.SemaphoreType.DMA((3, 4))],
        compiler_params=pltpu.CompilerParams(vmem_limit_bytes=12 * MIB),
        cost_estimate=SMALL,
        name="first_chunk",
    )(
        *xs,
        pltpu.with_memory_space_constraint(gate_weight, pltpu.HBM),
        pltpu.with_memory_space_constraint(up_weight, pltpu.HBM),
        in_factor,
    )
    return left, weights


def chunk_body(pieces, *refs):
    x_refs, (gate_ref, up_ref, f_ref, _, out_ref, _, _, xn) = refs[:pieces], refs[pieces:]
    gather_rows(x_refs, xn)
    out_ref[...] = project(xn, gate_ref, up_ref, f_ref)


def chunk(xs, weights, in_factor, left, index):
    pieces = len(xs)
    rows, depth = xs[0].shape
    order = in_factor.shape[0]
    total = pieces * rows
    vmem = pl.BlockSpec(memory_space=pltpu.VMEM)
    left, *weights = pl.pallas_call(
        functools.partial(chunk_body, pieces),
        grid=(1,),
        in_specs=[vmem] * (pieces + 3) + [pl.BlockSpec(memory_space=pl.ANY)],
        out_specs=[pl.BlockSpec((total, order), lambda i: (index, 0)), vmem, vmem],
        out_shape=[jax.ShapeDtypeStruct(left.shape, left.dtype)] + [pltpu.VMEM(w.shape, w.dtype) for w in weights],
        scratch_shapes=[pltpu.VMEM((total, depth), jnp.bfloat16)],
        input_output_aliases={pieces + 3: 0, pieces: 1, pieces + 1: 2},
        compiler_params=pltpu.CompilerParams(vmem_limit_bytes=12 * MIB),
        cost_estimate=SMALL,
        name="chunk",
    )(*xs, *[pltpu.with_memory_space_constraint(w, pltpu.VMEM) for w in weights], in_factor, left)
    return left, weights


def masked_of(wide, span, order):
    wide = wide.astype(jnp.float32)
    both = jnp.concatenate([wide[:, c : c + LANES] for c in range(0, wide.shape[1], LANES)], axis=0)
    return both[:, :order].astype(jnp.bfloat16)


def one_sketch(left_ref, masked, at, half):
    left = jnp.concatenate([left_ref[p * half : (p + 1) * half, :] for p in at], axis=0)
    high = left.astype(jnp.bfloat16)
    low = (left - high.astype(jnp.float32)).astype(jnp.bfloat16)
    return sum(lax.dot_general(part, masked, TN, preferred_element_type=jnp.float32) for part in (low, high))


def write_flat(flat, slot, sketch, twice):
    order = sketch.shape[0]
    twice[...] = jnp.concatenate([sketch, sketch], axis=1)
    lane = lax.broadcasted_iota(jnp.int32, (order // 2, 2 * order), 1)
    even = twice[pl.ds(0, order // 2, 2), :]
    odd = twice[pl.ds(1, order // 2, 2), :]
    flat[:, slot, :] = jnp.where(lane < order, even, odd)


def sketch_body(places, first, half, count, table, left_ref, mine_ref, other_ref, *refs):
    flat, twice = refs[-2:]
    me = lax.axis_index("examples")
    order = left_ref.shape[1]
    rows = 2 * half * LANES // mine_ref.shape[2]
    total = table.shape[1] // 2
    for r, at in enumerate(places, first):
        ref = mine_ref if r % 2 == 0 else other_ref
        masked = masked_of(ref[table[me, total + r], count : count + rows, :], 2 * half, order)
        write_flat(flat, r, one_sketch(left_ref, masked, at, half), twice)


def sketches(places, first, half, count, table, left, mine, other, flat):
    order = left.shape[1]
    vmem = pl.BlockSpec(memory_space=pltpu.VMEM)
    operands = [table, left, mine, other]
    aliases = {}
    if flat is not None:
        aliases = {4: 0}
        operands.append(flat)
    return pl.pallas_call(
        functools.partial(sketch_body, places, first, half, count),
        in_specs=[pl.BlockSpec(memory_space=pltpu.SMEM)] + [vmem] * (len(operands) - 1),
        out_specs=vmem,
        out_shape=jax.ShapeDtypeStruct((order // 2, table.shape[0], 2 * order), jnp.float32),
        scratch_shapes=[pltpu.VMEM((order, 2 * order), jnp.float32)],
        input_output_aliases=aliases,
        compiler_params=pltpu.CompilerParams(vmem_limit_bytes=12 * MIB),
        cost_estimate=SMALL,
        name="sketches",
    )(*operands)


def members_of(share_ref, count, order):
    devices = share_ref.shape[0]
    first = share_ref[:, count : count + 8, :LANES].astype(jnp.float32)[:, 0, :].astype(jnp.bfloat16)
    shape = (LANES, devices * count)
    place = lax.broadcasted_iota(jnp.int32, shape, 0) - order
    query = lax.broadcasted_iota(jnp.int32, shape, 1)
    spread = (place >= 0) & (place < count) & (((query - place) & (count - 1)) == 0)
    ids = jnp.dot(first, spread.astype(jnp.bfloat16), preferred_element_type=jnp.float32)
    place = lax.broadcasted_iota(jnp.int32, ids.shape, 1) - count * lax.broadcasted_iota(jnp.int32, ids.shape, 0)
    ids = jnp.sum(jnp.where((place >= 0) & (place < count), ids, 0.0), axis=0, keepdims=True)
    value = lax.broadcasted_iota(jnp.int32, (NVAL, devices * count), 0).astype(jnp.float32)
    return (value == ids).astype(jnp.bfloat16)


def finish_body(places, half, groups, count, table, left_ref, flat_ref, *refs):
    share_refs, (out_ref, twice, flat) = (refs[:groups], refs[groups : 2 * groups]), refs[2 * groups :]
    chips, _, width = share_refs[0][0].shape
    order = left_ref.shape[1]
    rows = 2 * half * LANES // width
    me, group = lax.axis_index("examples"), lax.axis_index("groups")
    examples = table.shape[0]
    flat[...] = flat_ref[...]
    members = [members_of(refs[0], count, order) for refs in share_refs]
    first = examples - len(places)
    for r, at in enumerate(places, first):
        masked = masked_of(share_refs[r % 2][0][table[me, examples + r], count : count + rows, :], 2 * half, order)
        write_flat(flat, r, one_sketch(left_ref, masked, at, half), twice)
    scores = [0.0, 0.0]
    for r in range(groups):
        block = lax.rem(group + r, groups) * (width // LANES)
        sketch = jnp.concatenate([flat[block + c] for c in range(width // LANES)], axis=1).astype(jnp.bfloat16)
        for kind in range(2):
            queries = share_refs[kind][r][:, :count, :].reshape(chips * count, width)
            scores[kind] += lax.dot_general(sketch, queries, NT, preferred_element_type=jnp.float32)
    total = 0.0
    for kind in range(2):
        rest = scores[kind]
        for _ in range(3):
            part = rest.astype(jnp.bfloat16)
            rest = rest - part.astype(jnp.float32)
            total += lax.dot_general(part, members[kind], NT, preferred_element_type=jnp.float32)
    for r in range(examples):
        out_ref[pl.ds(table[me, r], 1), :] = total[r : r + 1, :]


def finish(places, half, count, table, left, flat, mine, other):
    order = left.shape[1]
    groups = len(mine)
    vmem = pl.BlockSpec(memory_space=pltpu.VMEM)
    return pl.pallas_call(
        functools.partial(finish_body, places, half, groups, count),
        in_specs=[pl.BlockSpec(memory_space=pltpu.SMEM)] + [vmem] * (2 + 2 * groups),
        out_specs=vmem,
        out_shape=jax.ShapeDtypeStruct((table.shape[0], NVAL), jnp.float32),
        scratch_shapes=[pltpu.VMEM((order, 2 * order), jnp.float32), pltpu.VMEM(flat.shape, jnp.float32)],
        compiler_params=pltpu.CompilerParams(vmem_limit_bytes=12 * MIB),
        cost_estimate=SMALL,
        name="finish",
    )(table, left, flat, *mine, *other)


def arrivals(ring, devices):
    chips = len(ring)
    far = chips // 2
    table, spots = [[] for _ in range(devices)], []
    for distance in range(far + 1):
        for sign, piece in [(1, 0)] if distance in (0, far) else [(-1, 0), (1, 1)]:
            for me in range(devices):
                chip = ring[(ring.index(me // 2) + sign * distance) % chips]
                table[me] += [2 * chip + me % 2, 2 * chip + 1 - me % 2]
            if distance == 0:
                halves = [(0, 0), (0, 1)]
            elif distance == far:
                halves = [(chips - 1, 0), (chips - 1, 1)]
            else:
                halves = [(2 * distance - 1, piece), (2 * distance, piece)]
            spots.append([4 * k + 2 + p for k, p in halves])
            spots.append([4 * k + 4 + p for k, p in halves])
    bits = chips.bit_length() - 1
    for me, row in enumerate(table):
        apart = [(example // 2) ^ (me // 2) for example in row]
        row += [sum(((x >> b) & 1) << (bits - 1 - b) for b in range(bits)) for x in apart]
    return table, spots


def local(
    devices,
    groups,
    layer_inputs,
    example_lengths,
    norm_gain,
    gate_weight,
    up_weight,
    in_factor,
    out_factor,
    out_grads,
    queries,
    query_ids,
):
    chips = devices // 2
    ring = chip_ring(chips)
    forward = [(ring[r] * 2 + c, ring[(r + 1) % chips] * 2 + c) for r in range(chips) for c in range(2)]
    backward = [(b, a) for a, b in forward]
    other_core = [(d, d ^ 1) for d in range(devices)]

    span, depth = layer_inputs.shape
    half = span // 2
    order = in_factor.shape[1]
    units = gate_weight.shape[1]
    short = -units % LANES
    if short:
        gate_weight = jnp.pad(gate_weight, ((0, 0), (0, short)))
        up_weight = jnp.pad(up_weight, ((0, 0), (0, short)))
        in_factor = jnp.pad(in_factor, ((0, short), (0, 0)))
    tokens = 2 * span * chips + span

    def send(x, way):
        return lax.ppermute(x, "examples", way)

    nq = queries.shape[0]
    x_a, x_b, side = prepare(
        layer_inputs,
        norm_gain[None, :],
        example_lengths,
        out_grads,
        out_factor.T,
        query_ids[None, :],
        queries,
        groups,
    )
    distances = [chips >> b for b in range(1, chips.bit_length())]
    apart = [[(d, 2 * ((d // 2) ^ distance) + d % 2) for d in range(devices)] for distance in distances]
    side = side[None]
    pending = [send(side, apart[0])]
    coming = {
        1: (send(x_a, forward), send(x_a, backward)),
        2: (send(x_b, forward), send(x_b, backward)),
    }
    swapped = tuple(send(x, other_core) for x in (x_a, x_b))
    left, weights = first_chunk((x_a, x_b), gate_weight, up_weight, in_factor.T, 1, tokens)

    table, spots = arrivals(ring, devices)
    table = jnp.array(table, jnp.int32)

    for k in range(1, chips):
        own_1, own_2, left, *pending = lax.optimization_barrier((*coming.pop(k), left, *pending))
        own = (own_1, own_2)
        if k + 2 < chips - 1:
            coming[k + 2] = (send(own_1, forward), send(own_2, backward))
        elif k + 2 == chips - 1:
            opposite = send(own_1, forward)
        elif k + 1 == chips - 1:
            coming[chips - 1] = (opposite, send(own_2, backward))
        before, swapped = swapped, tuple(send(x, other_core) for x in own)
        if k < chips - 1:
            left, weights = chunk(before + own, weights, in_factor.T, left, k)
        if k <= len(distances):
            side = jnp.concatenate([side, *pending], axis=0)
            pending = []
        if k < len(distances):
            pending = [send(side, apart[k])]
        if k == len(distances):
            other = [send(side, other_core)]
            mine = [side]
            for r in range(1, groups):
                way = [((g + r) % groups, g) for g in range(groups)]
                pending.append(lax.ppermute(side, "groups", way))
        if k == chips - 3:
            mine += pending
            other += [send(x, other_core) for x in pending]
            pending = []
            ready = devices - 6
            flat = sketches(spots[:ready], 0, half, nq, table, left, mine[0], other[0], None)
            flat, left = lax.optimization_barrier((flat, left))
        if k == chips - 2:
            left, weights = chunk(swapped, weights, in_factor.T, left, 2 * k + 2)
            flat = sketches(spots[ready:-2], ready, half, nq, table, left, mine[0], other[0], flat)
            flat, left = lax.optimization_barrier((flat, left))
    left, weights = chunk(own, weights, in_factor.T, left, 2 * chips - 1)
    left, weights = chunk(swapped, weights, in_factor.T, left, 2 * chips)

    partial = finish(spots[-2:], half, nq, table, left, flat, mine, other)
    shares = lax.all_to_all(partial, "examples", split_axis=0, concat_axis=0, tiled=True)
    return jnp.sum(shares, axis=0, keepdims=True)


def solution(mesh):
    return jax.shard_map(
        functools.partial(local, mesh.shape["examples"], mesh.shape["groups"]),
        mesh=mesh,
        in_specs=(
            P(("groups", "examples"), None),
            P(("groups", "examples")),
            P(),
            P(None, "examples"),
            P(None, "examples"),
            P("examples", None),
            P(),
            P(("groups", "examples"), None),
            P("examples", None),
            P("examples"),
        ),
        out_specs=P(("groups", "examples"), None),
        check_vma=False,
    )
```

```python
import functools

import jax
import jax.numpy as jnp
from jax import lax
from jax.experimental import pallas as pl
from jax.experimental.pallas import tpu as pltpu
from jax.sharding import PartitionSpec as P

NVAL = 256
LANES = 128
MIB = 1024 * 1024
NT = (((1,), (1,)), ((), ()))
TN = (((0,), (0,)), ((), ()))
SMALL = pl.CostEstimate(flops=1_000_000, bytes_accessed=100_000, transcendentals=0)


def chip_ring(chips):
    if chips == 8:
        return [0, 2, 4, 6, 7, 5, 3, 1]
    return list(range(chips))


def prepare_body(lengths_ref, ids_ref, x_hbm, gain_hbm, grads_hbm, factor_hbm, queries_hbm, *refs):
    rows_ref, out_ref, x_ref, gain_ref, grads_ref, factor_ref, queries_ref, sems = refs
    span = x_ref.shape[0]
    block = 32
    starts = range(0, span, block)
    x_copies = []
    for k, start in enumerate(starts):
        some = pl.ds(start, block)
        x_copies.append(pltpu.make_async_copy(x_hbm.at[some], x_ref.at[some], sems.at[k]))
    copies = []
    pairs = [(gain_hbm, gain_ref), (grads_hbm, grads_ref), (factor_hbm, factor_ref), (queries_hbm, queries_ref)]
    for k, (source, target) in enumerate(pairs):
        copies.append(pltpu.make_async_copy(source, target, sems.at[len(x_copies) + k]))
    copies[0].start()
    for copy in x_copies + copies[1:]:
        copy.start()
    copies[0].wait()
    for start, copy in zip(starts, x_copies):
        copy.wait()
        for at in range(start, start + block, 16):
            x = x_ref[at : at + 16, :].astype(jnp.float32)
            scale = lax.rsqrt(jnp.mean(x * x, axis=-1, keepdims=True) + 1e-05)
            rows_ref[at : at + 16, :] = (x * scale * gain_ref[...]).astype(jnp.bfloat16)
    for copy in copies[1:]:
        copy.wait()

    count, width = queries_ref.shape[0], out_ref.shape[1]
    order = factor_ref.shape[0]
    rows = span * LANES // width
    offset = pl.multiple_of(lax.axis_index("groups") * width, width)
    out_ref[:count, :] = queries_ref[:, pl.ds(offset, width)]
    right = lax.dot_general(grads_ref[...], factor_ref[...], NT, preferred_element_type=jnp.float32)
    live = lax.broadcasted_iota(jnp.int32, (span, order), 0) < lengths_ref[0]
    masked = jnp.where(live, right, 0.0)
    ids = jnp.concatenate([ids_ref[...], jnp.zeros((1, LANES - order - count), jnp.int32)], axis=1)
    ids = jnp.broadcast_to(ids.astype(jnp.float32), (span, LANES - order))
    both = jnp.concatenate([masked, ids], axis=1)
    wide = jnp.concatenate([both[r : r + rows, :] for r in range(0, span, rows)], axis=1)
    out_ref[count : count + rows, :] = wide.astype(out_ref.dtype)
    if count + rows < out_ref.shape[0]:
        out_ref[count + rows :, :] = jnp.zeros((out_ref.shape[0] - count - rows, width), out_ref.dtype)


def prepare(x, gain, lengths, grads, factor, ids, queries, groups):
    span, depth = x.shape
    count = queries.shape[0]
    width = depth // groups
    vmem = pl.BlockSpec(memory_space=pltpu.VMEM)
    hbm = pl.BlockSpec(memory_space=pltpu.HBM)
    share = -(-(count + span * LANES // width) // 8) * 8
    operands = [x, gain, grads, factor, queries]
    return pl.pallas_call(
        prepare_body,
        in_specs=[pl.BlockSpec(memory_space=pltpu.SMEM), vmem] + [hbm] * len(operands),
        out_specs=[vmem] * 2,
        out_shape=[
            jax.ShapeDtypeStruct((span, depth), jnp.bfloat16),
            jax.ShapeDtypeStruct((share, width), queries.dtype),
        ],
        scratch_shapes=[pltpu.VMEM(o.shape, o.dtype) for o in operands]
        + [pltpu.SemaphoreType.DMA((span // 32 + len(operands) - 1,))],
        compiler_params=pltpu.CompilerParams(vmem_limit_bytes=12 * MIB),
        cost_estimate=SMALL,
        name="prepare",
    )(lengths, ids, *[pltpu.with_memory_space_constraint(o, pltpu.HBM) for o in operands])


def gather_rows(x_refs, xn):
    if len(x_refs) == 1:
        return x_refs[0]
    rows = x_refs[0].shape[0]
    for k, ref in enumerate(x_refs):
        xn[k * rows : (k + 1) * rows, :] = ref[...]
    return xn


def gated(gate, up):
    return (jax.nn.silu(gate) * up).astype(jnp.bfloat16)


def project(xn, gate_ref, up_ref, f_ref):
    order, units = f_ref.shape
    wide = 2 * LANES

    def product(w):
        return jnp.dot(xn[...], w, preferred_element_type=jnp.float32)

    def left_of(hidden, start, end):
        return lax.dot_general(hidden, f_ref[:, start:end], NT, preferred_element_type=jnp.float32)

    total = jnp.zeros((xn.shape[0], order), jnp.float32)
    hidden, start = None, 0
    for at in range(0, units, wide):
        both = product(gate_ref[:, at : at + wide])
        if hidden is not None:
            total += left_of(hidden, start, at)
        if at + wide <= units:
            hidden = gated(both, product(up_ref[:, at : at + wide]))
        else:
            hidden = gated(both[:, :LANES], both[:, LANES:])
        start = at
    return total + left_of(hidden, start, units)


def first_body(pieces, *refs):
    x_refs, (gate_hbm, up_hbm, f_ref, out_ref, gate_ref, up_ref, xn, sems) = refs[:pieces], refs[pieces:]
    depth, units = gate_hbm.shape
    even = up_ref.shape[1]
    parts = sems.shape[1]
    copies = []
    for p in range(parts):
        rows = pl.ds(p * (depth // parts), depth // parts)
        moves = [
            (gate_hbm.at[rows], gate_ref.at[rows, pl.ds(0, units)]),
            (up_hbm.at[rows, pl.ds(0, even)], up_ref.at[rows]),
        ]
        if even < units:
            moves.append((up_hbm.at[rows, pl.ds(even, LANES)], gate_ref.at[rows, pl.ds(units, LANES)]))
        for k, (source, target) in enumerate(moves):
            copies.append(pltpu.make_async_copy(source, target, sems.at[k, p]))
    for copy in copies:
        copy.start()
    for copy in copies:
        copy.wait()
    out_ref[...] = project(gather_rows(x_refs, xn), gate_ref, up_ref, f_ref)


def first_chunk(xs, gate_weight, up_weight, in_factor, index, tokens):
    pieces = len(xs)
    rows, depth = xs[0].shape
    order, units = in_factor.shape
    total = pieces * rows
    vmem = pl.BlockSpec(memory_space=pltpu.VMEM)
    hbm = pl.BlockSpec(memory_space=pltpu.HBM)
    rest = units % (2 * LANES)
    left, *weights = pl.pallas_call(
        functools.partial(first_body, pieces),
        grid=(1,),
        in_specs=[vmem] * pieces + [hbm, hbm, vmem],
        out_specs=[pl.BlockSpec((total, order), lambda i: (index, 0)), vmem, vmem],
        out_shape=[
            jax.ShapeDtypeStruct((tokens, order), jnp.float32),
            pltpu.VMEM((depth, units + rest), jnp.bfloat16),
            pltpu.VMEM((depth, units - rest), jnp.bfloat16),
        ],
        scratch_shapes=[pltpu.VMEM((total, depth), jnp.bfloat16), pltpu.SemaphoreType.DMA((3, 4))],
        compiler_params=pltpu.CompilerParams(vmem_limit_bytes=12 * MIB),
        cost_estimate=SMALL,
        name="first_chunk",
    )(
        *xs,
        pltpu.with_memory_space_constraint(gate_weight, pltpu.HBM),
        pltpu.with_memory_space_constraint(up_weight, pltpu.HBM),
        in_factor,
    )
    return left, weights


def chunk_body(pieces, *refs):
    x_refs, (gate_ref, up_ref, f_ref, _, out_ref, _, _, xn) = refs[:pieces], refs[pieces:]
    out_ref[...] = project(gather_rows(x_refs, xn), gate_ref, up_ref, f_ref)


def chunk(xs, weights, in_factor, left, index):
    pieces = len(xs)
    rows, depth = xs[0].shape
    order = in_factor.shape[0]
    total = pieces * rows
    vmem = pl.BlockSpec(memory_space=pltpu.VMEM)
    left, *weights = pl.pallas_call(
        functools.partial(chunk_body, pieces),
        grid=(1,),
        in_specs=[vmem] * (pieces + 3) + [pl.BlockSpec(memory_space=pl.ANY)],
        out_specs=[pl.BlockSpec((total, order), lambda i: (index, 0)), vmem, vmem],
        out_shape=[jax.ShapeDtypeStruct(left.shape, left.dtype)] + [pltpu.VMEM(w.shape, w.dtype) for w in weights],
        scratch_shapes=[pltpu.VMEM((total, depth), jnp.bfloat16)],
        input_output_aliases={pieces + 3: 0, pieces: 1, pieces + 1: 2},
        compiler_params=pltpu.CompilerParams(vmem_limit_bytes=12 * MIB),
        cost_estimate=SMALL,
        name="chunk",
    )(*xs, *[pltpu.with_memory_space_constraint(w, pltpu.VMEM) for w in weights], in_factor, left)
    return left, weights


def masked_of(wide, span, order):
    wide = wide.astype(jnp.float32)
    both = jnp.concatenate([wide[:, c : c + LANES] for c in range(0, wide.shape[1], LANES)], axis=0)
    return both[:, :order].astype(jnp.bfloat16)


def one_sketch(left_ref, masked, at, half):
    left = jnp.concatenate([left_ref[p * half : (p + 1) * half, :] for p in at], axis=0)
    high = left.astype(jnp.bfloat16)
    low = (left - high.astype(jnp.float32)).astype(jnp.bfloat16)
    return sum(lax.dot_general(part, masked, TN, preferred_element_type=jnp.float32) for part in (low, high))


def write_flat(flat, slot, sketch, twice):
    order = sketch.shape[0]
    twice[...] = jnp.concatenate([sketch, sketch], axis=1)
    lane = lax.broadcasted_iota(jnp.int32, (order // 2, 2 * order), 1)
    even = twice[pl.ds(0, order // 2, 2), :]
    odd = twice[pl.ds(1, order // 2, 2), :]
    flat[:, slot, :] = jnp.where(lane < order, even, odd)


def share_of(refs, at):
    first, second = refs
    count = first.shape[0]
    inside = lax.rem(at, count)
    return jnp.where(at < count, first[inside].astype(jnp.float32), second[inside].astype(jnp.float32))


def sketch_body(places, half, count, table, left_ref, *refs):
    share_refs, (flat, twice) = (refs[:2], refs[2:4]), refs[4:]
    me = lax.axis_index("examples")
    order = left_ref.shape[1]
    rows = 2 * half * LANES // refs[0].shape[2]
    total = table.shape[1] // 2
    for r, at in enumerate(places):
        masked = masked_of(share_of(share_refs[r % 2], table[me, total + r])[count : count + rows], 2 * half, order)
        write_flat(flat, r, one_sketch(left_ref, masked, at, half), twice)


def sketches(places, half, count, table, left, mine, other):
    order = left.shape[1]
    vmem = pl.BlockSpec(memory_space=pltpu.VMEM)
    return pl.pallas_call(
        functools.partial(sketch_body, places, half, count),
        in_specs=[pl.BlockSpec(memory_space=pltpu.SMEM)] + [vmem] * 5,
        out_specs=vmem,
        out_shape=jax.ShapeDtypeStruct((order // 2, table.shape[0], 2 * order), jnp.float32),
        scratch_shapes=[pltpu.VMEM((order, 2 * order), jnp.float32)],
        compiler_params=pltpu.CompilerParams(vmem_limit_bytes=12 * MIB),
        cost_estimate=SMALL,
        name="sketches",
    )(table, left, *mine, *other)


def members_of(share_ref, count, order):
    devices = share_ref.shape[0]
    first = share_ref[:, count : count + 8, :LANES].astype(jnp.float32)[:, 0, :].astype(jnp.bfloat16)
    shape = (LANES, devices * count)
    place = lax.broadcasted_iota(jnp.int32, shape, 0) - order
    query = lax.broadcasted_iota(jnp.int32, shape, 1)
    spread = (place >= 0) & (place < count) & (((query - place) & (count - 1)) == 0)
    ids = jnp.dot(first, spread.astype(jnp.bfloat16), preferred_element_type=jnp.float32)
    place = lax.broadcasted_iota(jnp.int32, ids.shape, 1) - count * lax.broadcasted_iota(jnp.int32, ids.shape, 0)
    ids = jnp.sum(jnp.where((place >= 0) & (place < count), ids, 0.0), axis=0, keepdims=True)
    value = lax.broadcasted_iota(jnp.int32, (NVAL, devices * count), 0).astype(jnp.float32)
    return (value == ids).astype(jnp.bfloat16)


def finish_body(places, half, groups, count, table, left_ref, flat_ref, *refs):
    share_refs, (out_ref, twice, flat) = refs[:-3], refs[-3:]
    kinds = 4
    chips, _, width = share_refs[0].shape
    order = left_ref.shape[1]
    rows = 2 * half * LANES // width
    me, group = lax.axis_index("examples"), lax.axis_index("groups")
    examples = table.shape[0]
    flat[...] = flat_ref[...]
    first = examples - len(places)
    for r, at in enumerate(places, first):
        side = share_of(share_refs[2 * (r % 2) : 2 * (r % 2) + 2], table[me, examples + r])
        masked = masked_of(side[count : count + rows], 2 * half, order)
        write_flat(flat, r, one_sketch(left_ref, masked, at, half), twice)
    scores = [0.0] * kinds
    for r in range(groups):
        block = lax.rem(group + r, groups) * (width // LANES)
        sketch = jnp.concatenate([flat[block + c] for c in range(width // LANES)], axis=1).astype(jnp.bfloat16)
        for kind in range(kinds):
            queries = share_refs[kinds * r + kind][:, :count, :].reshape(chips * count, width)
            scores[kind] += lax.dot_general(sketch, queries, NT, preferred_element_type=jnp.float32)
    total = 0.0
    for kind in range(kinds):
        members = members_of(share_refs[kind], count, order)
        rest = scores[kind]
        for _ in range(3):
            part = rest.astype(jnp.bfloat16)
            rest = rest - part.astype(jnp.float32)
            total += lax.dot_general(part, members, NT, preferred_element_type=jnp.float32)
    for r in range(examples):
        out_ref[pl.ds(table[me, r], 1), :] = total[r : r + 1, :]


def finish(places, half, groups, count, table, left, flat, shares):
    order = left.shape[1]
    vmem = pl.BlockSpec(memory_space=pltpu.VMEM)
    return pl.pallas_call(
        functools.partial(finish_body, places, half, groups, count),
        in_specs=[pl.BlockSpec(memory_space=pltpu.SMEM)] + [vmem] * (2 + len(shares)),
        out_specs=vmem,
        out_shape=jax.ShapeDtypeStruct((table.shape[0], NVAL), jnp.float32),
        scratch_shapes=[pltpu.VMEM((order, 2 * order), jnp.float32), pltpu.VMEM(flat.shape, jnp.float32)],
        compiler_params=pltpu.CompilerParams(vmem_limit_bytes=12 * MIB),
        cost_estimate=SMALL,
        name="finish",
    )(table, left, flat, *shares)


def arrivals(ring, devices):
    chips = len(ring)
    far = chips // 2
    table, spots = [[] for _ in range(devices)], []
    for distance in range(far + 1):
        for sign, piece in [(1, 0)] if distance in (0, far) else [(-1, 0), (1, 1)]:
            for me in range(devices):
                chip = ring[(ring.index(me // 2) + sign * distance) % chips]
                table[me] += [2 * chip + me % 2, 2 * chip + 1 - me % 2]
            if distance == 0:
                spots += [[0, 1], [2, 3]]
            elif distance == far:
                at = 4 * (2 * far - 1)
                spots += [[at, at + 1], [at + 2, at + 3]]
            else:
                at = 4 * (2 * distance - 1) + 2 * piece
                spots += [[at, at + 1], [at + 4, at + 5]]
    bits = chips.bit_length() - 1
    for me, row in enumerate(table):
        apart = [(example // 2) ^ (me // 2) for example in row]
        row += [sum(((x >> b) & 1) << (bits - 1 - b) for b in range(bits)) for x in apart]
    return table, spots


def local(
    devices,
    groups,
    layer_inputs,
    example_lengths,
    norm_gain,
    gate_weight,
    up_weight,
    in_factor,
    out_factor,
    out_grads,
    queries,
    query_ids,
):
    chips = devices // 2
    ring = chip_ring(chips)
    forward = [(ring[r] * 2 + c, ring[(r + 1) % chips] * 2 + c) for r in range(chips) for c in range(2)]
    backward = [(b, a) for a, b in forward]
    other_core = [(d, d ^ 1) for d in range(devices)]

    span, depth = layer_inputs.shape
    half = span // 2
    order = in_factor.shape[1]
    units = gate_weight.shape[1]
    short = -units % LANES
    if short:
        gate_weight = jnp.pad(gate_weight, ((0, 0), (0, short)))
        up_weight = jnp.pad(up_weight, ((0, 0), (0, short)))
        in_factor = jnp.pad(in_factor, ((0, short), (0, 0)))
    far = chips // 2
    tokens = devices * span
    table, spots = arrivals(ring, devices)
    table = jnp.array(table, jnp.int32)
    nq = queries.shape[0]

    def send(x, way):
        return lax.ppermute(x, "examples", way)

    def across(x):
        ways = [[((g + r) % groups, g) for g in range(groups)] for r in range(1, groups)]
        return [lax.ppermute(x, "groups", way) for way in ways]

    rows, side = prepare(
        layer_inputs,
        norm_gain[None, :],
        example_lengths,
        out_grads,
        out_factor.T,
        query_ids[None, :],
        queries,
        groups,
    )

    distances = [chips >> b for b in range(1, chips.bit_length())]
    stages = len(distances)
    apart = [[(d, 2 * ((d // 2) ^ distance) + d % 2) for d in range(devices)] for distance in distances]

    coming = (send(rows, forward), send(rows, backward))
    swapped = send(rows, other_core)
    side = side[None]
    pending = [send(side, apart[0])]
    left, weights = first_chunk((rows,), gate_weight, up_weight, in_factor.T, 0, tokens)
    left, weights = chunk((swapped,), weights, in_factor.T, left, 1)
    first, second = [], []
    for r in range(1, far + 1):
        own_f, own_b, left, *pending = lax.optimization_barrier((*coming, left, *pending))
        if r < far - 1:
            coming = (send(own_f, forward), send(own_b, backward))
        elif r == far - 1:
            coming = (send(own_f[:half], forward), send(own_b[half:], backward))
        swapped = (send(own_f, other_core), send(own_b, other_core))
        if r < stages:
            side = jnp.concatenate([side, *pending], axis=0)
            pending = [send(side, apart[r])]
            if r == stages - 1:
                first = [side, send(side, other_core)]
                pending += across(side)
        elif r == stages:
            side, *others = pending
            second = [side, send(side, other_core)]
            for x in others:
                first += [x, send(x, other_core)]
            pending = across(side)
        elif r == stages + 1:
            for x in pending:
                second += [x, send(x, other_core)]
            pending = []
        if r < far:
            left, weights = chunk((own_f, own_b), weights, in_factor.T, left, 2 * r - 1)
            left, weights = chunk(swapped, weights, in_factor.T, left, 2 * r)
        else:
            left, weights = chunk((own_f, own_b), weights, in_factor.T, left, 2 * (2 * far - 1))
            left, weights = chunk(swapped, weights, in_factor.T, left, 2 * (2 * far - 1) + 1)
        if r == far - 1:
            flat = sketches(spots[:-2], half, nq, table, left, (first[0], second[0]), (first[1], second[1]))
            flat, left = lax.optimization_barrier((flat, left))

    shares = [x for pair in zip(first, second) for x in pair]
    partial = finish(spots[-2:], half, groups, nq, table, left, flat, shares)
    parts = lax.all_to_all(partial, "examples", split_axis=0, concat_axis=0, tiled=True)
    return jnp.sum(parts, axis=0, keepdims=True)


def solution(mesh):
    return jax.shard_map(
        functools.partial(local, mesh.shape["examples"], mesh.shape["groups"]),
        mesh=mesh,
        in_specs=(
            P(("groups", "examples"), None),
            P(("groups", "examples")),
            P(),
            P(None, "examples"),
            P(None, "examples"),
            P("examples", None),
            P(),
            P(("groups", "examples"), None),
            P("examples", None),
            P("examples"),
        ),
        out_specs=P(("groups", "examples"), None),
        check_vma=False,
    )
```

```python
import functools

import jax
import jax.numpy as jnp
from jax import lax
from jax.experimental import pallas as pl
from jax.experimental.pallas import tpu as pltpu
from jax.sharding import PartitionSpec as P

NVAL = 256
LANES = 128
MIB = 1024 * 1024
NT = (((1,), (1,)), ((), ()))
TN = (((0,), (0,)), ((), ()))
SMALL = pl.CostEstimate(flops=1_000_000, bytes_accessed=100_000, transcendentals=0)


def chip_ring(chips):
    if chips == 8:
        return [0, 2, 4, 6, 7, 5, 3, 1]
    return list(range(chips))


def prepare_body(lengths_ref, ids_ref, x_hbm, gain_hbm, grads_hbm, factor_hbm, queries_hbm, *refs):
    rows_ref, share_ref, x_ref, gain_ref, grads_ref, factor_ref, queries_ref, sems = refs
    span = x_ref.shape[0]
    block = 32
    starts = range(0, span, block)
    x_copies = []
    for k, start in enumerate(starts):
        some = pl.ds(start, block)
        x_copies.append(pltpu.make_async_copy(x_hbm.at[some], x_ref.at[some], sems.at[k]))
    copies = []
    pairs = [(gain_hbm, gain_ref), (grads_hbm, grads_ref), (factor_hbm, factor_ref), (queries_hbm, queries_ref)]
    for k, (source, target) in enumerate(pairs):
        copies.append(pltpu.make_async_copy(source, target, sems.at[len(x_copies) + k]))
    copies[0].start()
    for copy in x_copies + copies[1:]:
        copy.start()
    copies[0].wait()
    for start, copy in zip(starts, x_copies):
        copy.wait()
        for at in range(start, start + block, 16):
            x = x_ref[at : at + 16, :].astype(jnp.float32)
            scale = lax.rsqrt(jnp.mean(x * x, axis=-1, keepdims=True) + 1e-05)
            rows_ref[at : at + 16, :] = (x * scale * gain_ref[...]).astype(jnp.bfloat16)
    for copy in copies[1:]:
        copy.wait()

    count, width = share_ref.shape[1:]
    depth, order = factor_ref.shape[1], factor_ref.shape[0]
    rows = span * LANES // width
    extra = rows_ref.shape[0] - span
    offset = pl.multiple_of(lax.axis_index("groups") * width, width)
    share_ref[0] = queries_ref[:, pl.ds(offset, width)]
    right = lax.dot_general(grads_ref[...], factor_ref[...], NT, preferred_element_type=jnp.float32)
    live = lax.broadcasted_iota(jnp.int32, (span, order), 0) < lengths_ref[0]
    masked = jnp.where(live, right, 0.0)
    ids = jnp.concatenate([ids_ref[...], jnp.zeros((1, LANES - order - count), jnp.int32)], axis=1)
    ids = jnp.broadcast_to(ids.astype(jnp.float32), (span, LANES - order))
    both = jnp.concatenate([masked, ids], axis=1)
    wide = jnp.concatenate([both[r : r + rows, :] for r in range(0, span, rows)], axis=1)
    if rows < extra:
        wide = jnp.concatenate([wide, jnp.zeros((extra - rows, width), jnp.float32)], axis=0)
    rows_ref[span:, :width] = queries_ref[:, pl.ds(offset, width)]
    rows_ref[span:, width : 2 * width] = wide.astype(rows_ref.dtype)
    if 2 * width < depth:
        rows_ref[span:, 2 * width :] = jnp.zeros((extra, depth - 2 * width), rows_ref.dtype)


def prepare(x, gain, lengths, grads, factor, ids, queries, groups):
    span, depth = x.shape
    count = queries.shape[0]
    width = depth // groups
    vmem = pl.BlockSpec(memory_space=pltpu.VMEM)
    hbm = pl.BlockSpec(memory_space=pltpu.HBM)
    operands = [x, gain, grads, factor, queries]
    return pl.pallas_call(
        prepare_body,
        in_specs=[pl.BlockSpec(memory_space=pltpu.SMEM), vmem] + [hbm] * len(operands),
        out_specs=[vmem] * 2,
        out_shape=[
            jax.ShapeDtypeStruct((span + count, depth), jnp.bfloat16),
            jax.ShapeDtypeStruct((1, count, width), queries.dtype),
        ],
        scratch_shapes=[pltpu.VMEM(o.shape, o.dtype) for o in operands]
        + [pltpu.SemaphoreType.DMA((span // 32 + len(operands) - 1,))],
        compiler_params=pltpu.CompilerParams(vmem_limit_bytes=12 * MIB),
        cost_estimate=SMALL,
        name="prepare",
    )(lengths, ids, *[pltpu.with_memory_space_constraint(o, pltpu.HBM) for o in operands])


def gather_rows(x_refs, xn, shares_ref, slots, extra):
    at = 0
    for ref, slot in zip(x_refs, slots):
        rows = ref.shape[0] - (0 if slot is None else extra)
        xn[at : at + rows, :] = ref[:rows, :]
        if slot is not None:
            shares_ref[slot] = ref[rows:, :]
        at += rows
    return xn


def gated(gate, up):
    return (jax.nn.silu(gate) * up).astype(jnp.bfloat16)


def project(xn, gate_ref, up_ref, f_ref):
    order, units = f_ref.shape
    wide = 2 * LANES

    def product(w):
        return jnp.dot(xn[...], w, preferred_element_type=jnp.float32)

    def left_of(hidden, start, end):
        return lax.dot_general(hidden, f_ref[:, start:end], NT, preferred_element_type=jnp.float32)

    total = jnp.zeros((xn.shape[0], order), jnp.float32)
    hidden, start = None, 0
    for at in range(0, units, wide):
        both = product(gate_ref[:, at : at + wide])
        if hidden is not None:
            total += left_of(hidden, start, at)
        if at + wide <= units:
            hidden = gated(both, product(up_ref[:, at : at + wide]))
        else:
            hidden = gated(both[:, :LANES], both[:, LANES:])
        start = at
    return total + left_of(hidden, start, units)


def first_body(x_ref, gate_hbm, up_hbm, f_ref, out_ref, gate_ref, up_ref, shares_ref, xn, sems):
    depth, units = gate_hbm.shape
    even = up_ref.shape[1]
    parts = sems.shape[1]
    copies = []
    for p in range(parts):
        rows = pl.ds(p * (depth // parts), depth // parts)
        moves = [
            (gate_hbm.at[rows], gate_ref.at[rows, pl.ds(0, units)]),
            (up_hbm.at[rows, pl.ds(0, even)], up_ref.at[rows]),
        ]
        if even < units:
            moves.append((up_hbm.at[rows, pl.ds(even, LANES)], gate_ref.at[rows, pl.ds(units, LANES)]))
        for k, (source, target) in enumerate(moves):
            copies.append(pltpu.make_async_copy(source, target, sems.at[k, p]))
    for copy in copies:
        copy.start()
    gather_rows([x_ref], xn, shares_ref, [0], shares_ref.shape[1])
    for copy in copies:
        copy.wait()
    out_ref[...] = project(xn, gate_ref, up_ref, f_ref)


def first_chunk(rows, gate_weight, up_weight, in_factor, devices, extra):
    total, depth = rows.shape[0] - extra, rows.shape[1]
    order, units = in_factor.shape
    vmem = pl.BlockSpec(memory_space=pltpu.VMEM)
    hbm = pl.BlockSpec(memory_space=pltpu.HBM)
    rest = units % (2 * LANES)
    left, *kept = pl.pallas_call(
        first_body,
        grid=(1,),
        in_specs=[vmem, hbm, hbm, vmem],
        out_specs=[pl.BlockSpec((total, order), lambda i: (0, 0)), vmem, vmem, vmem],
        out_shape=[
            jax.ShapeDtypeStruct((devices * total, order), jnp.float32),
            pltpu.VMEM((depth, units + rest), jnp.bfloat16),
            pltpu.VMEM((depth, units - rest), jnp.bfloat16),
            pltpu.VMEM((devices, extra, depth), jnp.bfloat16),
        ],
        scratch_shapes=[pltpu.VMEM((total, depth), jnp.bfloat16), pltpu.SemaphoreType.DMA((3, 4))],
        compiler_params=pltpu.CompilerParams(vmem_limit_bytes=12 * MIB),
        cost_estimate=SMALL,
        name="first_chunk",
    )(
        rows,
        pltpu.with_memory_space_constraint(gate_weight, pltpu.HBM),
        pltpu.with_memory_space_constraint(up_weight, pltpu.HBM),
        in_factor,
    )
    return left, kept


def chunk_body(slots, *refs):
    pieces = len(slots)
    x_refs, (gate_ref, up_ref, _, f_ref, _, out_ref, _, _, shares_ref, xn) = refs[:pieces], refs[pieces:]
    gather_rows(x_refs, xn, shares_ref, slots, shares_ref.shape[1])
    out_ref[...] = project(xn, gate_ref, up_ref, f_ref)


def chunk(xs, slots, kept, in_factor, left, index):
    pieces = len(xs)
    depth = xs[0].shape[1]
    order = in_factor.shape[0]
    extra = kept[2].shape[1]
    total = sum(x.shape[0] - (0 if slot is None else extra) for x, slot in zip(xs, slots))
    vmem = pl.BlockSpec(memory_space=pltpu.VMEM)
    left, *kept = pl.pallas_call(
        functools.partial(chunk_body, slots),
        grid=(1,),
        in_specs=[vmem] * (pieces + 4) + [pl.BlockSpec(memory_space=pl.ANY)],
        out_specs=[pl.BlockSpec((total, order), lambda i: (index, 0)), vmem, vmem, vmem],
        out_shape=[jax.ShapeDtypeStruct(left.shape, left.dtype)] + [pltpu.VMEM(w.shape, w.dtype) for w in kept],
        scratch_shapes=[pltpu.VMEM((total, depth), jnp.bfloat16)],
        input_output_aliases={pieces + 4: 0, pieces: 1, pieces + 1: 2, pieces + 2: 3},
        compiler_params=pltpu.CompilerParams(vmem_limit_bytes=12 * MIB),
        cost_estimate=SMALL,
        name="chunk",
    )(*xs, *[pltpu.with_memory_space_constraint(w, pltpu.VMEM) for w in kept], in_factor, left)
    return left, kept


def masked_of(wide, span, order):
    wide = wide.astype(jnp.float32)
    both = jnp.concatenate([wide[:, c : c + LANES] for c in range(0, wide.shape[1], LANES)], axis=0)
    return both[:, :order].astype(jnp.bfloat16)


def one_sketch(left_ref, masked, at, half):
    left = jnp.concatenate([left_ref[p * half : (p + 1) * half, :] for p in at], axis=0)
    high = left.astype(jnp.bfloat16)
    low = (left - high.astype(jnp.float32)).astype(jnp.bfloat16)
    return sum(lax.dot_general(part, masked, TN, preferred_element_type=jnp.float32) for part in (low, high))


def write_flat(flat, slot, sketch, twice):
    order = sketch.shape[0]
    twice[...] = jnp.concatenate([sketch, sketch], axis=1)
    lane = lax.broadcasted_iota(jnp.int32, (order // 2, 2 * order), 1)
    even = twice[pl.ds(0, order // 2, 2), :]
    odd = twice[pl.ds(1, order // 2, 2), :]
    flat[:, slot, :] = jnp.where(lane < order, even, odd)


def masked_in(shares_ref, slot, width, span, order):
    return masked_of(shares_ref[slot, : span * LANES // width, width : 2 * width], span, order)


def sketch_body(places, half, width, left_ref, shares_ref, flat, twice):
    for r, at in enumerate(places):
        masked = masked_in(shares_ref, r, width, 2 * half, left_ref.shape[1])
        write_flat(flat, r, one_sketch(left_ref, masked, at, half), twice)


def sketches(places, half, width, left, shares):
    order = left.shape[1]
    vmem = pl.BlockSpec(memory_space=pltpu.VMEM)
    return pl.pallas_call(
        functools.partial(sketch_body, places, half, width),
        in_specs=[vmem] * 2,
        out_specs=vmem,
        out_shape=jax.ShapeDtypeStruct((order // 2, shares.shape[0], 2 * order), jnp.float32),
        scratch_shapes=[pltpu.VMEM((order, 2 * order), jnp.float32)],
        compiler_params=pltpu.CompilerParams(vmem_limit_bytes=12 * MIB),
        cost_estimate=SMALL,
        name="sketches",
    )(left, pltpu.with_memory_space_constraint(shares, pltpu.VMEM))


def members_of(shares_ref, count, width, order):
    devices = shares_ref.shape[0]
    first = shares_ref[:, :8, width : width + LANES].astype(jnp.float32)[:, 0, :].astype(jnp.bfloat16)
    shape = (LANES, devices * count)
    place = lax.broadcasted_iota(jnp.int32, shape, 0) - order
    query = lax.broadcasted_iota(jnp.int32, shape, 1)
    spread = (place >= 0) & (place < count) & (((query - place) & (count - 1)) == 0)
    ids = jnp.dot(first, spread.astype(jnp.bfloat16), preferred_element_type=jnp.float32)
    place = lax.broadcasted_iota(jnp.int32, ids.shape, 1) - count * lax.broadcasted_iota(jnp.int32, ids.shape, 0)
    ids = jnp.sum(jnp.where((place >= 0) & (place < count), ids, 0.0), axis=0, keepdims=True)
    value = lax.broadcasted_iota(jnp.int32, (NVAL, devices * count), 0).astype(jnp.float32)
    return (value == ids).astype(jnp.bfloat16)


def finish_body(places, half, groups, width, table, left_ref, flat_ref, shares_ref, *refs):
    query_refs, (out_ref, twice, flat) = refs[:-3], refs[-3:]
    examples, count, _ = shares_ref.shape
    order = left_ref.shape[1]
    me, group = lax.axis_index("examples"), lax.axis_index("groups")
    flat[...] = flat_ref[...]
    for r, at in enumerate(places, examples - len(places)):
        masked = masked_in(shares_ref, r, width, 2 * half, order)
        write_flat(flat, r, one_sketch(left_ref, masked, at, half), twice)
    scores = 0.0
    for r in range(groups):
        block = lax.rem(group + r, groups) * (width // LANES)
        sketch = jnp.concatenate([flat[block + c] for c in range(width // LANES)], axis=1).astype(jnp.bfloat16)
        if r == 0:
            queries = shares_ref[:, :, :width].reshape(examples * count, width)
        else:
            parts = []
            for mine, other in zip(query_refs[2 * r - 2 :: 2 * groups - 2], query_refs[2 * r - 1 :: 2 * groups - 2]):
                for k in range(mine.shape[0]):
                    parts += [mine[k], other[k]]
            queries = jnp.concatenate(parts, axis=0)
        scores += lax.dot_general(sketch, queries, NT, preferred_element_type=jnp.float32)
    members = members_of(shares_ref, count, width, order)
    total = 0.0
    for _ in range(3):
        part = scores.astype(jnp.bfloat16)
        scores = scores - part.astype(jnp.float32)
        total += lax.dot_general(part, members, NT, preferred_element_type=jnp.float32)
    for r in range(examples):
        out_ref[pl.ds(table[me, r], 1), :] = total[r : r + 1, :]


def finish(places, half, groups, width, table, left, flat, shares, queries):
    order = left.shape[1]
    vmem = pl.BlockSpec(memory_space=pltpu.VMEM)
    return pl.pallas_call(
        functools.partial(finish_body, places, half, groups, width),
        in_specs=[pl.BlockSpec(memory_space=pltpu.SMEM)] + [vmem] * (3 + len(queries)),
        out_specs=vmem,
        out_shape=jax.ShapeDtypeStruct((table.shape[0], NVAL), jnp.float32),
        scratch_shapes=[pltpu.VMEM((order, 2 * order), jnp.float32), pltpu.VMEM(flat.shape, jnp.float32)],
        compiler_params=pltpu.CompilerParams(vmem_limit_bytes=14 * MIB),
        cost_estimate=SMALL,
        name="finish",
    )(table, left, flat, pltpu.with_memory_space_constraint(shares, pltpu.VMEM), *queries)


def arrivals(ring, devices):
    chips = len(ring)
    far = chips // 2
    table, spots = [[] for _ in range(devices)], []
    for distance in range(far + 1):
        for sign, piece in [(1, 0)] if distance in (0, far) else [(-1, 0), (1, 1)]:
            for me in range(devices):
                chip = ring[(ring.index(me // 2) + sign * distance) % chips]
                table[me] += [2 * chip + me % 2, 2 * chip + 1 - me % 2]
            if distance == 0:
                spots += [[0, 1], [2, 3]]
            elif distance == far:
                at = 4 * (2 * far - 1)
                spots += [[at, at + 1], [at + 2, at + 3]]
            else:
                at = 4 * (2 * distance - 1) + 2 * piece
                spots += [[at, at + 1], [at + 4, at + 5]]
    return table, spots


def local(
    devices,
    groups,
    layer_inputs,
    example_lengths,
    norm_gain,
    gate_weight,
    up_weight,
    in_factor,
    out_factor,
    out_grads,
    queries,
    query_ids,
):
    chips = devices // 2
    ring = chip_ring(chips)
    forward = [(ring[r] * 2 + c, ring[(r + 1) % chips] * 2 + c) for r in range(chips) for c in range(2)]
    backward = [(b, a) for a, b in forward]
    other_core = [(d, d ^ 1) for d in range(devices)]

    span, depth = layer_inputs.shape
    half = span // 2
    order = in_factor.shape[1]
    units = gate_weight.shape[1]
    short = -units % LANES
    if short:
        gate_weight = jnp.pad(gate_weight, ((0, 0), (0, short)))
        up_weight = jnp.pad(up_weight, ((0, 0), (0, short)))
        in_factor = jnp.pad(in_factor, ((0, short), (0, 0)))
    far = chips // 2
    table, spots = arrivals(ring, devices)
    table = jnp.array(table, jnp.int32)

    def send(x, way):
        return lax.ppermute(x, "examples", way)

    def across(x):
        ways = [[((g + r) % groups, g) for g in range(groups)] for r in range(1, groups)]
        return [lax.ppermute(x, "groups", way) for way in ways]

    rows, share = prepare(
        layer_inputs,
        norm_gain[None, :],
        example_lengths,
        out_grads,
        out_factor.T,
        query_ids[None, :],
        queries,
        groups,
    )
    width = share.shape[2]
    extra = rows.shape[0] - span

    coming = (send(rows, forward), send(rows, backward))
    swapped = send(rows, other_core)
    pending, crossed = across(share), []
    left, kept = first_chunk(rows, gate_weight, up_weight, in_factor.T, devices, extra)
    left, kept = chunk((swapped,), (1,), kept, in_factor.T, left, 1)
    for r in range(1, far + 1):
        due = len(pending)
        own_f, own_b, left, *rest = lax.optimization_barrier((*coming, left, *pending, *crossed))
        pending, crossed = rest[:due], rest[due:]
        if r < far - 1:
            coming = (send(own_f, forward), send(own_b, backward))
        elif r == far - 1:
            coming = (send(own_f[:half], forward), send(own_b[half:], backward))
        swapped = (send(own_f, other_core), send(own_b, other_core))
        crossed += [y for x in pending for y in (x, send(x, other_core))]
        if r < far:
            pending = across(jnp.stack([own_f[span:, :width], own_b[span:, :width]]))
            slot = 4 * r - 2
            left, kept = chunk((own_f, own_b), (slot, slot + 2), kept, in_factor.T, left, 2 * r - 1)
            left, kept = chunk(swapped, (slot + 1, slot + 3), kept, in_factor.T, left, 2 * r)
        else:
            pending = across(own_b[half:, :width][None])
            crossed += [y for x in pending for y in (x, send(x, other_core))]
            slot, at = devices - 2, 2 * (2 * far - 1)
            left, kept = chunk((own_f, own_b), (None, slot), kept, in_factor.T, left, at)
            left, kept = chunk(swapped, (None, slot + 1), kept, in_factor.T, left, at + 1)
        if r == far - 1:
            flat = sketches(spots[:-2], half, width, left, kept[2])
            flat, left = lax.optimization_barrier((flat, left))

    partial = finish(spots[-2:], half, groups, width, table, left, flat, kept[2], crossed)
    parts = lax.all_to_all(partial, "examples", split_axis=0, concat_axis=0, tiled=True)
    return jnp.sum(parts, axis=0, keepdims=True)


def solution(mesh):
    return jax.shard_map(
        functools.partial(local, mesh.shape["examples"], mesh.shape["groups"]),
        mesh=mesh,
        in_specs=(
            P(("groups", "examples"), None),
            P(("groups", "examples")),
            P(),
            P(None, "examples"),
            P(None, "examples"),
            P("examples", None),
            P(),
            P(("groups", "examples"), None),
            P("examples", None),
            P("examples"),
        ),
        out_specs=P(("groups", "examples"), None),
        check_vma=False,
    )
```

```python
import functools

import jax
import jax.numpy as jnp
from jax import lax
from jax.experimental import pallas as pl
from jax.experimental.pallas import tpu as pltpu
from jax.sharding import PartitionSpec as P

NVAL = 256
LANES = 128
MIB = 1024 * 1024
NT = (((1,), (1,)), ((), ()))
TN = (((0,), (0,)), ((), ()))
SMALL = pl.CostEstimate(flops=1_000_000, bytes_accessed=100_000, transcendentals=0)


def chip_ring(chips):
    if chips == 8:
        return [0, 2, 4, 6, 7, 5, 3, 1]
    return list(range(chips))


def prepare_body(lengths_ref, ids_ref, x_hbm, gain_hbm, grads_hbm, factor_hbm, queries_hbm, *refs):
    rows_ref, share_ref, x_ref, gain_ref, grads_ref, factor_ref, queries_ref, sems = refs
    span = x_ref.shape[0]
    block = 32
    starts = range(0, span, block)
    x_copies = []
    for k, start in enumerate(starts):
        some = pl.ds(start, block)
        x_copies.append(pltpu.make_async_copy(x_hbm.at[some], x_ref.at[some], sems.at[k]))
    copies = []
    pairs = [(gain_hbm, gain_ref), (grads_hbm, grads_ref), (factor_hbm, factor_ref), (queries_hbm, queries_ref)]
    for k, (source, target) in enumerate(pairs):
        copies.append(pltpu.make_async_copy(source, target, sems.at[len(x_copies) + k]))
    copies[0].start()
    for copy in x_copies + copies[1:]:
        copy.start()
    copies[0].wait()
    for start, copy in zip(starts, x_copies):
        copy.wait()
        for at in range(start, start + block, 16):
            x = x_ref[at : at + 16, :].astype(jnp.float32)
            scale = lax.rsqrt(jnp.mean(x * x, axis=-1, keepdims=True) + 1e-05)
            rows_ref[at : at + 16, :] = (x * scale * gain_ref[...]).astype(jnp.bfloat16)
    for copy in copies[1:]:
        copy.wait()

    count, width = share_ref.shape[1:]
    depth, order = factor_ref.shape[1], factor_ref.shape[0]
    rows = span * LANES // width
    extra = rows_ref.shape[0] - span
    offset = pl.multiple_of(lax.axis_index("groups") * width, width)
    share_ref[0] = queries_ref[:, pl.ds(offset, width)]
    right = lax.dot_general(grads_ref[...], factor_ref[...], NT, preferred_element_type=jnp.float32)
    live = lax.broadcasted_iota(jnp.int32, (span, order), 0) < lengths_ref[0]
    masked = jnp.where(live, right, 0.0)
    ids = jnp.concatenate([ids_ref[...], jnp.zeros((1, LANES - order - count), jnp.int32)], axis=1)
    ids = jnp.broadcast_to(ids.astype(jnp.float32), (span, LANES - order))
    both = jnp.concatenate([masked, ids], axis=1)
    wide = jnp.concatenate([both[r : r + rows, :] for r in range(0, span, rows)], axis=1)
    if rows < extra:
        wide = jnp.concatenate([wide, jnp.zeros((extra - rows, width), jnp.float32)], axis=0)
    rows_ref[span:, :width] = queries_ref[:, pl.ds(offset, width)]
    rows_ref[span:, width : 2 * width] = wide.astype(rows_ref.dtype)
    if 2 * width < depth:
        rows_ref[span:, 2 * width :] = jnp.zeros((extra, depth - 2 * width), rows_ref.dtype)


def prepare(x, gain, lengths, grads, factor, ids, queries, groups):
    span, depth = x.shape
    count = queries.shape[0]
    width = depth // groups
    vmem = pl.BlockSpec(memory_space=pltpu.VMEM)
    hbm = pl.BlockSpec(memory_space=pltpu.HBM)
    operands = [x, gain, grads, factor, queries]
    return pl.pallas_call(
        prepare_body,
        in_specs=[pl.BlockSpec(memory_space=pltpu.SMEM), vmem] + [hbm] * len(operands),
        out_specs=[vmem] * 2,
        out_shape=[
            jax.ShapeDtypeStruct((span + count, depth), jnp.bfloat16),
            jax.ShapeDtypeStruct((1, count, width), queries.dtype),
        ],
        scratch_shapes=[pltpu.VMEM(o.shape, o.dtype) for o in operands]
        + [pltpu.SemaphoreType.DMA((span // 32 + len(operands) - 1,))],
        compiler_params=pltpu.CompilerParams(vmem_limit_bytes=12 * MIB),
        cost_estimate=SMALL,
        name="prepare",
    )(lengths, ids, *[pltpu.with_memory_space_constraint(o, pltpu.HBM) for o in operands])


def gather_rows(x_refs, xn, shares_ref, slots, extra):
    at = 0
    for ref, slot in zip(x_refs, slots):
        rows = ref.shape[0] - (0 if slot is None else extra)
        xn[at : at + rows, :] = ref[:rows, :]
        if slot is not None:
            shares_ref[slot] = ref[rows:, :]
        at += rows
    return xn


def gated(gate, up):
    return (jax.nn.silu(gate) * up).astype(jnp.bfloat16)


def project(xn, gate_ref, up_ref, f_ref):
    order, units = f_ref.shape
    wide = 2 * LANES

    def product(w):
        return jnp.dot(xn[...], w, preferred_element_type=jnp.float32)

    def left_of(hidden, start, end):
        return lax.dot_general(hidden, f_ref[:, start:end], NT, preferred_element_type=jnp.float32)

    total = jnp.zeros((xn.shape[0], order), jnp.float32)
    hidden, start = None, 0
    for at in range(0, units, wide):
        both = product(gate_ref[:, at : at + wide])
        if hidden is not None:
            total += left_of(hidden, start, at)
        if at + wide <= units:
            hidden = gated(both, product(up_ref[:, at : at + wide]))
        else:
            hidden = gated(both[:, :LANES], both[:, LANES:])
        start = at
    return total + left_of(hidden, start, units)


def first_body(x_ref, gate_hbm, up_hbm, f_ref, out_ref, gate_ref, up_ref, shares_ref, xn, sems):
    depth, units = gate_hbm.shape
    even = up_ref.shape[1]
    parts = sems.shape[1]
    copies = []
    for p in range(parts):
        rows = pl.ds(p * (depth // parts), depth // parts)
        moves = [
            (gate_hbm.at[rows], gate_ref.at[rows, pl.ds(0, units)]),
            (up_hbm.at[rows, pl.ds(0, even)], up_ref.at[rows]),
        ]
        if even < units:
            moves.append((up_hbm.at[rows, pl.ds(even, LANES)], gate_ref.at[rows, pl.ds(units, LANES)]))
        for k, (source, target) in enumerate(moves):
            copies.append(pltpu.make_async_copy(source, target, sems.at[k, p]))
    for copy in copies:
        copy.start()
    gather_rows([x_ref], xn, shares_ref, [0], shares_ref.shape[1])
    for copy in copies:
        copy.wait()
    out_ref[...] = project(xn, gate_ref, up_ref, f_ref)


def first_chunk(rows, gate_weight, up_weight, in_factor, devices, extra):
    total, depth = rows.shape[0] - extra, rows.shape[1]
    order, units = in_factor.shape
    vmem = pl.BlockSpec(memory_space=pltpu.VMEM)
    hbm = pl.BlockSpec(memory_space=pltpu.HBM)
    rest = units % (2 * LANES)
    left, *kept = pl.pallas_call(
        first_body,
        grid=(1,),
        in_specs=[vmem, hbm, hbm, vmem],
        out_specs=[pl.BlockSpec((total, order), lambda i: (0, 0)), vmem, vmem, vmem],
        out_shape=[
            jax.ShapeDtypeStruct((devices * total, order), jnp.float32),
            pltpu.VMEM((depth, units + rest), jnp.bfloat16),
            pltpu.VMEM((depth, units - rest), jnp.bfloat16),
            pltpu.VMEM((devices, extra, depth), jnp.bfloat16),
        ],
        scratch_shapes=[pltpu.VMEM((total, depth), jnp.bfloat16), pltpu.SemaphoreType.DMA((3, 4))],
        compiler_params=pltpu.CompilerParams(vmem_limit_bytes=12 * MIB),
        cost_estimate=SMALL,
        name="first_chunk",
    )(
        rows,
        pltpu.with_memory_space_constraint(gate_weight, pltpu.HBM),
        pltpu.with_memory_space_constraint(up_weight, pltpu.HBM),
        in_factor,
    )
    return left, kept


def chunk_body(slots, *refs):
    pieces = len(slots)
    x_refs, (gate_ref, up_ref, _, f_ref, _, out_ref, _, _, shares_ref, xn) = refs[:pieces], refs[pieces:]
    gather_rows(x_refs, xn, shares_ref, slots, shares_ref.shape[1])
    out_ref[...] = project(xn, gate_ref, up_ref, f_ref)


def chunk(xs, slots, kept, in_factor, left, index):
    pieces = len(xs)
    depth = xs[0].shape[1]
    order = in_factor.shape[0]
    extra = kept[2].shape[1]
    total = sum(x.shape[0] - (0 if slot is None else extra) for x, slot in zip(xs, slots))
    vmem = pl.BlockSpec(memory_space=pltpu.VMEM)
    left, *kept = pl.pallas_call(
        functools.partial(chunk_body, slots),
        grid=(1,),
        in_specs=[vmem] * (pieces + 4) + [pl.BlockSpec(memory_space=pl.ANY)],
        out_specs=[pl.BlockSpec((total, order), lambda i: (index, 0)), vmem, vmem, vmem],
        out_shape=[jax.ShapeDtypeStruct(left.shape, left.dtype)] + [pltpu.VMEM(w.shape, w.dtype) for w in kept],
        scratch_shapes=[pltpu.VMEM((total, depth), jnp.bfloat16)],
        input_output_aliases={pieces + 4: 0, pieces: 1, pieces + 1: 2, pieces + 2: 3},
        compiler_params=pltpu.CompilerParams(vmem_limit_bytes=12 * MIB),
        cost_estimate=SMALL,
        name="chunk",
    )(*xs, *[pltpu.with_memory_space_constraint(w, pltpu.VMEM) for w in kept], in_factor, left)
    return left, kept


def masked_of(wide, span, order):
    wide = wide.astype(jnp.float32)
    both = jnp.concatenate([wide[:, c : c + LANES] for c in range(0, wide.shape[1], LANES)], axis=0)
    return both[:, :order].astype(jnp.bfloat16)


def one_sketch(left_ref, masked, at, half):
    left = jnp.concatenate([left_ref[p * half : (p + 1) * half, :] for p in at], axis=0)
    high = left.astype(jnp.bfloat16)
    low = (left - high.astype(jnp.float32)).astype(jnp.bfloat16)
    return sum(lax.dot_general(part, masked, TN, preferred_element_type=jnp.float32) for part in (low, high))


def write_flat(flat, slot, sketch, twice):
    order = sketch.shape[0]
    twice[...] = jnp.concatenate([sketch, sketch], axis=1)
    lane = lax.broadcasted_iota(jnp.int32, (order // 2, 2 * order), 1)
    even = twice[pl.ds(0, order // 2, 2), :]
    odd = twice[pl.ds(1, order // 2, 2), :]
    flat[:, slot, :] = jnp.where(lane < order, even, odd)


def masked_in(shares_ref, slot, width, span, order):
    return masked_of(shares_ref[slot, : span * LANES // width, width : 2 * width], span, order)


def sketch_body(places, half, width, left_ref, shares_ref, flat, twice):
    for r, at in enumerate(places):
        masked = masked_in(shares_ref, r, width, 2 * half, left_ref.shape[1])
        write_flat(flat, r, one_sketch(left_ref, masked, at, half), twice)


def sketches(places, half, width, left, shares):
    order = left.shape[1]
    vmem = pl.BlockSpec(memory_space=pltpu.VMEM)
    return pl.pallas_call(
        functools.partial(sketch_body, places, half, width),
        in_specs=[vmem] * 2,
        out_specs=vmem,
        out_shape=jax.ShapeDtypeStruct((order // 2, shares.shape[0], 2 * order), jnp.float32),
        scratch_shapes=[pltpu.VMEM((order, 2 * order), jnp.float32)],
        compiler_params=pltpu.CompilerParams(vmem_limit_bytes=12 * MIB),
        cost_estimate=SMALL,
        name="sketches",
    )(left, pltpu.with_memory_space_constraint(shares, pltpu.VMEM))


def members_of(shares_ref, count, width, order):
    devices = shares_ref.shape[0]
    first = shares_ref[:, :8, width : width + LANES].astype(jnp.float32)[:, 0, :].astype(jnp.bfloat16)
    shape = (LANES, devices * count)
    place = lax.broadcasted_iota(jnp.int32, shape, 0) - order
    query = lax.broadcasted_iota(jnp.int32, shape, 1)
    spread = (place >= 0) & (place < count) & (((query - place) & (count - 1)) == 0)
    ids = jnp.dot(first, spread.astype(jnp.bfloat16), preferred_element_type=jnp.float32)
    place = lax.broadcasted_iota(jnp.int32, ids.shape, 1) - count * lax.broadcasted_iota(jnp.int32, ids.shape, 0)
    ids = jnp.sum(jnp.where((place >= 0) & (place < count), ids, 0.0), axis=0, keepdims=True)
    value = lax.broadcasted_iota(jnp.int32, (NVAL, devices * count), 0).astype(jnp.float32)
    return (value == ids).astype(jnp.bfloat16)


def finish_body(places, half, groups, width, table, left_ref, flat_ref, shares_ref, *refs):
    query_refs, (out_ref, twice, flat) = refs[:-3], refs[-3:]
    examples, count, _ = shares_ref.shape
    order = left_ref.shape[1]
    me, group = lax.axis_index("examples"), lax.axis_index("groups")
    flat[...] = flat_ref[...]
    for r, at in enumerate(places, examples - len(places)):
        masked = masked_in(shares_ref, r, width, 2 * half, order)
        write_flat(flat, r, one_sketch(left_ref, masked, at, half), twice)
    scores = 0.0
    for r in range(groups):
        block = lax.rem(group + r, groups) * (width // LANES)
        sketch = jnp.concatenate([flat[block + c] for c in range(width // LANES)], axis=1).astype(jnp.bfloat16)
        if r == 0:
            queries = shares_ref[:, :, :width].reshape(examples * count, width)
        else:
            parts = []
            for mine, other in zip(query_refs[2 * r - 2 :: 2 * groups - 2], query_refs[2 * r - 1 :: 2 * groups - 2]):
                for k in range(mine.shape[0]):
                    parts += [mine[k], other[k]]
            queries = jnp.concatenate(parts, axis=0)
        scores += lax.dot_general(sketch, queries, NT, preferred_element_type=jnp.float32)
    members = members_of(shares_ref, count, width, order)
    total = 0.0
    for _ in range(3):
        part = scores.astype(jnp.bfloat16)
        scores = scores - part.astype(jnp.float32)
        total += lax.dot_general(part, members, NT, preferred_element_type=jnp.float32)
    for r in range(examples):
        out_ref[pl.ds(table[me, r], 1), :] = total[r : r + 1, :]


def finish(places, half, groups, width, table, left, flat, shares, queries):
    order = left.shape[1]
    vmem = pl.BlockSpec(memory_space=pltpu.VMEM)
    return pl.pallas_call(
        functools.partial(finish_body, places, half, groups, width),
        in_specs=[pl.BlockSpec(memory_space=pltpu.SMEM)] + [vmem] * (3 + len(queries)),
        out_specs=vmem,
        out_shape=jax.ShapeDtypeStruct((table.shape[0], NVAL), jnp.float32),
        scratch_shapes=[pltpu.VMEM((order, 2 * order), jnp.float32), pltpu.VMEM(flat.shape, jnp.float32)],
        compiler_params=pltpu.CompilerParams(vmem_limit_bytes=14 * MIB),
        cost_estimate=SMALL,
        name="finish",
    )(table, left, flat, pltpu.with_memory_space_constraint(shares, pltpu.VMEM), *queries)


def arrivals(ring, devices):
    chips = len(ring)
    far = chips // 2
    table, spots = [[] for _ in range(devices)], []
    for distance in range(far + 1):
        for sign, piece in [(1, 0)] if distance in (0, far) else [(-1, 0), (1, 1)]:
            for me in range(devices):
                chip = ring[(ring.index(me // 2) + sign * distance) % chips]
                table[me] += [2 * chip + me % 2, 2 * chip + 1 - me % 2]
            if distance == 0:
                spots += [[0, 1], [2, 3]]
            elif distance == far:
                at = 4 * (2 * far - 1)
                spots += [[at, at + 1], [at + 2, at + 3]]
            else:
                at = 4 * (2 * distance - 1) + 2 * piece
                spots += [[at, at + 1], [at + 4, at + 5]]
    return table, spots


def local(
    devices,
    groups,
    layer_inputs,
    example_lengths,
    norm_gain,
    gate_weight,
    up_weight,
    in_factor,
    out_factor,
    out_grads,
    queries,
    query_ids,
):
    chips = devices // 2
    ring = chip_ring(chips)
    forward = [(ring[r] * 2 + c, ring[(r + 1) % chips] * 2 + c) for r in range(chips) for c in range(2)]
    backward = [(b, a) for a, b in forward]
    other_core = [(d, d ^ 1) for d in range(devices)]

    span, depth = layer_inputs.shape
    half = span // 2
    order = in_factor.shape[1]
    units = gate_weight.shape[1]
    short = -units % LANES
    if short:
        gate_weight = jnp.pad(gate_weight, ((0, 0), (0, short)))
        up_weight = jnp.pad(up_weight, ((0, 0), (0, short)))
        in_factor = jnp.pad(in_factor, ((0, short), (0, 0)))
    far = chips // 2
    table, spots = arrivals(ring, devices)
    table = jnp.array(table, jnp.int32)

    def send(x, way):
        return lax.ppermute(x, "examples", way)

    def across(x):
        ways = [[((g + r) % groups, g) for g in range(groups)] for r in range(1, groups)]
        return [lax.ppermute(x, "groups", way) for way in ways]

    rows, share = prepare(
        layer_inputs,
        norm_gain[None, :],
        example_lengths,
        out_grads,
        out_factor.T,
        query_ids[None, :],
        queries,
        groups,
    )
    width = share.shape[2]
    extra = rows.shape[0] - span

    coming = (send(rows, forward), send(rows, backward))
    swapped = send(rows, other_core)
    pending, crossed = across(share), []
    left, kept = first_chunk(rows, gate_weight, up_weight, in_factor.T, devices, extra)
    left, kept = chunk((swapped,), (1,), kept, in_factor.T, left, 1)
    for r in range(1, far + 1):
        due = len(pending)
        own_f, own_b, left, *rest = lax.optimization_barrier((*coming, left, *pending, *crossed))
        pending, crossed = rest[:due], rest[due:]
        if r < far - 1:
            coming = (send(own_f, forward), send(own_b, backward))
        elif r == far - 1:
            coming = (send(own_f[:half], forward), send(own_b[half:], backward))
        swapped = (send(own_f, other_core), send(own_b, other_core))
        crossed += [y for x in pending for y in (x, send(x, other_core))]
        if r < far:
            pending = across(jnp.stack([own_f[span:, :width], own_b[span:, :width]]))
            slot = 4 * r - 2
            left, kept = chunk((own_f, own_b), (slot, slot + 2), kept, in_factor.T, left, 2 * r - 1)
            left, kept = chunk(swapped, (slot + 1, slot + 3), kept, in_factor.T, left, 2 * r)
        else:
            lasts = [across(x[half:, :width][None]) for x in (own_b, swapped[1])]
            crossed += [y for pair in zip(*lasts) for y in pair]
            slot, at = devices - 2, 2 * (2 * far - 1)
            left, kept = chunk((own_f, own_b), (None, slot), kept, in_factor.T, left, at)
            left, kept = chunk(swapped, (None, slot + 1), kept, in_factor.T, left, at + 1)
        if r == far - 1:
            flat = sketches(spots[:-2], half, width, left, kept[2])
            flat, left = lax.optimization_barrier((flat, left))

    partial = finish(spots[-2:], half, groups, width, table, left, flat, kept[2], crossed)
    parts = lax.all_to_all(partial, "examples", split_axis=0, concat_axis=0, tiled=True)
    return jnp.sum(parts, axis=0, keepdims=True)


def solution(mesh):
    return jax.shard_map(
        functools.partial(local, mesh.shape["examples"], mesh.shape["groups"]),
        mesh=mesh,
        in_specs=(
            P(("groups", "examples"), None),
            P(("groups", "examples")),
            P(),
            P(None, "examples"),
            P(None, "examples"),
            P("examples", None),
            P(),
            P(("groups", "examples"), None),
            P("examples", None),
            P("examples"),
        ),
        out_specs=P(("groups", "examples"), None),
        check_vma=False,
    )
```
